32 devices in a mesh: sta: 8 (over z, x), evt: 4 (over y, core).
Axes of the slice: x: 2, y: 2, z: 4, core: 2. Of those that a mesh axis runs over, the one named last changes fastest.
Arguments:
- waveforms: bfloat16 [128, 64, 1024], P(('evt', 'sta')), may hold values from -18 to 18
- pair_events: int32 [4096, 2], P('evt'), may hold values from 0 to 127, as said below
- pair_valid: int32 [4096], P('evt'), may hold values from 0 to 1, as said below
- presence: int32 [128, 64], P(None, 'sta'), may hold values 0 or 1
Outputs:
- correlation: bfloat16 [4096, 64, 256], P('evt', 'sta')
- pair_peak: float32 [4096], P('evt')
The draws below stay inside these ranges and needn't reach their ends.
Inputs may be any that keep to these rules, and one draw needn't show every extreme that they name: `pair_events`: slot rows p * 1024 to (p + 1) * 1024 - 1 belong to block p; each row names first an event of block p (events p * 32 to (p + 1) * 32 - 1), then a different event at most 16 positions away from it; in every block the first row names the block's first event and the second row the block's last event, each with an event exactly 16 away. `pair_valid`: in each block of 1024 slots the valid slots come first; in every draw some block is full.
All inputs are finite; a program needn't handle non-finite values. No bound on the sum of `presence` on one device may be relied on, other than what follows from the above.
Results may differ from the reference program's by a relative error of at most 0.0064.
Values may be sent and summed in bfloat16 or wider, within the bound.
No kernel may reach another device: no remote copies, remote signals or barrier semaphores. Data moves between devices by JAX's collectives and lax.ppermute only.
A program may use at most 64 MiB of HBM per device.

```python
import math
import jax
import jax.numpy as jnp
from jax import lax

WIN = 1024
LAGS = 256
EVT_DEV = 4
PAIR_CAP = 1024
STATIONS = 64
BLOCK = 32
BAND = 16
EVENTS = 128
PAIRS = 4096


def draw_waveforms(key, part):
    subkeys = jax.random.split(jax.random.fold_in(key, 11), 5)
    station_base = jax.random.truncated_normal(subkeys[0], -4.0, 4.0, (STATIONS, WIN), jnp.float32)
    event_delay = jax.random.randint(subkeys[1], (EVENTS, 1, 1), 0, LAGS // 4)
    sample_index = jnp.arange(WIN, dtype=jnp.int32)[None, None, :]
    source_index = (sample_index - event_delay) % WIN
    station_rows = jnp.arange(STATIONS, dtype=jnp.int32)[None, :, None]
    shifted = station_base[station_rows, source_index]
    coherence_ramp = 0.3 + 0.65 * jnp.arange(STATIONS, dtype=jnp.float32) / STATIONS
    coherence = jnp.minimum(coherence_ramp[None, :, None] * jax.random.uniform(subkeys[2], (1, STATIONS, 1), jnp.float32, 0.9, 1.1), 0.95)
    noise_part = jax.random.truncated_normal(subkeys[3], -4.0, 4.0, (EVENTS, STATIONS, WIN), jnp.float32)
    amplitude = jnp.exp(jax.random.uniform(subkeys[4], (EVENTS, STATIONS, 1), jnp.float32, math.log(0.3), math.log(3.0)))
    return (amplitude * (coherence * shifted + jnp.sqrt(1.0 - coherence * coherence) * noise_part)).astype(jnp.bfloat16)


def draw_pair_events(key, part):
    subkeys = jax.random.split(jax.random.fold_in(key, 17), 3)
    slot_index = jnp.arange(PAIRS, dtype=jnp.int32)
    owner_block = slot_index // PAIR_CAP
    slot_in_block = slot_index % PAIR_CAP
    first_event = owner_block * BLOCK + jax.random.randint(subkeys[0], (PAIRS,), 0, BLOCK)
    first_event = jnp.where(slot_in_block == 0, owner_block * BLOCK, first_event)
    first_event = jnp.where(slot_in_block == 1, owner_block * BLOCK + BLOCK - 1, first_event)
    distance = jax.random.randint(subkeys[1], (PAIRS,), 1, BAND + 1)
    distance = jnp.where(slot_in_block < 2, BAND, distance)
    direction = jnp.where(jax.random.randint(subkeys[2], (PAIRS,), 0, 2) == 0, -1, 1)
    direction = jnp.where(slot_in_block == 0, -1, direction)
    direction = jnp.where(slot_in_block == 1, 1, direction)
    second_event = first_event + direction * distance
    outside = (second_event < 0) | (second_event >= EVENTS)
    second_event = jnp.where(outside, first_event - direction * distance, second_event)
    return jnp.stack([first_event, second_event], axis=1).astype(jnp.int32)


def draw_pair_valid(key, part):
    subkeys = jax.random.split(jax.random.fold_in(key, 23), 2)
    owners = PAIRS // PAIR_CAP
    filled = jax.random.randint(subkeys[0], (owners,), PAIR_CAP // 4, PAIR_CAP + 1)
    full_owner = jax.random.randint(subkeys[1], (), 0, owners)
    filled = jnp.where(jnp.arange(owners, dtype=jnp.int32) == full_owner, PAIR_CAP, filled)
    slot_index = jnp.arange(PAIRS, dtype=jnp.int32)
    return (slot_index % PAIR_CAP < filled[slot_index // PAIR_CAP]).astype(jnp.int32)


def place_ends(drawn, own_key, least, largest):
    spot = [jax.random.randint(jax.random.fold_in(own_key, axis), (), 0, length) for axis, length in enumerate(drawn.shape)]
    widest = drawn.shape.index(max(drawn.shape))
    neighbour = spot[:widest] + [(spot[widest] + 1) % drawn.shape[widest]] + spot[widest + 1:]
    return drawn.at[tuple(spot)].set(least).at[tuple(neighbour)].set(largest)


def setup_inputs(seed: int = 0) -> dict:
    key_of = jax.random.split(jax.random.key(seed), 5)
    waveforms = draw_waveforms(jax.random.fold_in(key_of[4], 71), 0)
    pair_events = draw_pair_events(jax.random.fold_in(key_of[4], 71), 0)
    pair_valid = draw_pair_valid(jax.random.fold_in(key_of[4], 71), 0)
    presence = place_ends((jax.random.randint(key_of[3], (EVENTS, STATIONS), 0, 4) < 3).astype(jnp.int32), jax.random.fold_in(key_of[3], 1), 0, 1)
    return {"waveforms": waveforms, "pair_events": pair_events, "pair_valid": pair_valid, "presence": presence}


def spectral_tables(window, lag_count):
    half_width = window // 2
    sample_index = jnp.arange(window, dtype=jnp.int32)
    bin_index = jnp.arange(half_width, dtype=jnp.int32)
    phase_angle = (sample_index[:, None] * bin_index[None, :] % window).astype(jnp.float32) * (2.0 * math.pi / window)
    forward = (jnp.concatenate([jnp.cos(phase_angle), -jnp.sin(phase_angle)], axis=1) / math.sqrt(window)).astype(jnp.bfloat16)
    shifts = jnp.arange(lag_count, dtype=jnp.int32) - lag_count // 2
    lag_angle = (bin_index[:, None] * shifts[None, :] % window).astype(jnp.float32) * (2.0 * math.pi / window)
    factor = jnp.where(bin_index == 0, 1.0, 2.0).astype(jnp.float32)
    inverse = jnp.concatenate([factor[:, None] * jnp.cos(lag_angle), -factor[:, None] * jnp.sin(lag_angle)], axis=0).astype(jnp.bfloat16)
    energy_weights = jnp.concatenate([factor, factor])
    return (forward, inverse, energy_weights)

def to_spectra(traces, forward):
    flattened = traces.reshape(-1, traces.shape[-1])
    result = jnp.dot(flattened, forward, preferred_element_type=jnp.float32).astype(jnp.bfloat16)
    return result.reshape(traces.shape[:-1] + (forward.shape[1],))

def pair_group(spectra, energy, presence, inverse, first_event, second_event, valid_rows):
    window = spectra.shape[-1]
    half_width = window // 2
    first_spec = jnp.take(spectra, first_event, axis=0).astype(jnp.float32)
    second_spec = jnp.take(spectra, second_event, axis=0).astype(jnp.float32)
    first_real, first_imag = (first_spec[..., :half_width], first_spec[..., half_width:])
    second_real, second_imag = (second_spec[..., :half_width], second_spec[..., half_width:])
    cross_spec = jnp.concatenate([first_real * second_real + first_imag * second_imag, first_real * second_imag - first_imag * second_real], axis=-1).astype(jnp.bfloat16)
    group_rows, station_share = (cross_spec.shape[0], cross_spec.shape[1])
    lagged = jnp.dot(cross_spec.reshape(-1, window), inverse, preferred_element_type=jnp.float32)
    lagged = lagged.reshape(group_rows, station_share, inverse.shape[1])
    norm_factor = lax.rsqrt(jnp.take(energy, first_event, axis=0) * jnp.take(energy, second_event, axis=0))
    weight_mask = valid_rows[:, None].astype(jnp.float32) * jnp.take(presence, first_event, axis=0).astype(jnp.float32) * jnp.take(presence, second_event, axis=0).astype(jnp.float32)
    normalized = lagged * (norm_factor * weight_mask)[:, :, None]
    peak_terms = lax.optimization_barrier(jnp.sum(lax.optimization_barrier(jnp.max(normalized, axis=-1)) * weight_mask, axis=-1))
    present = lax.optimization_barrier(jnp.sum(weight_mask, axis=-1))
    return (normalized.astype(jnp.bfloat16), peak_terms, present)

def reference(waveforms, pair_events, pair_valid, presence):
    forward, inverse, energy_weights = spectral_tables(WIN, LAGS)
    grouped = waveforms.reshape(EVENTS // EVT_DEV, EVT_DEV, STATIONS, WIN)
    spectra = lax.map(lambda traces: to_spectra(traces, forward), grouped).reshape(EVENTS, STATIONS, WIN)
    energy = lax.map(lambda piece: lax.optimization_barrier(jnp.sum(energy_weights * jnp.square(piece.astype(jnp.float32)), axis=-1)) + 1e-06, spectra.reshape(EVENTS // EVT_DEV, EVT_DEV, STATIONS, WIN)).reshape(EVENTS, STATIONS)
    group_rows = min(128, PAIR_CAP)
    event_groups = pair_events.reshape(PAIRS // group_rows, group_rows, 2)
    valid_groups = pair_valid.reshape(PAIRS // group_rows, group_rows)

    def one_group(group_item):
        events_here, valid_rows = group_item
        return pair_group(spectra, energy, presence, inverse, events_here[:, 0], events_here[:, 1], valid_rows)
    correlation, peak_terms, present = lax.map(one_group, (event_groups, valid_groups))
    pair_peak = peak_terms.reshape(PAIRS) / jnp.maximum(present.reshape(PAIRS), 1.0)
    return (correlation.reshape(PAIRS, STATIONS, LAGS), pair_peak)
```

```python
import functools
import math

import jax
import jax.numpy as jnp
import numpy as np
from jax import lax
from jax.experimental import pallas as pl
from jax.experimental.pallas import tpu as pltpu
from jax.sharding import PartitionSpec as P

LAGS = 256
LANES = 128


def spectral_tables(window, lag_count):
    half = window // 2
    sample = np.arange(window, dtype=np.int64)
    bins = np.arange(half, dtype=np.int64)
    angle = (sample[:, None] * bins[None, :] % window) * (2.0 * math.pi / window)
    forward = np.concatenate([np.cos(angle), -np.sin(angle)], axis=1) / math.sqrt(window)
    shifts = np.arange(lag_count, dtype=np.int64) - lag_count // 2
    lag_angle = (bins[:, None] * shifts[None, :] % window) * (2.0 * math.pi / window)
    factor = np.where(bins == 0, 1.0, 2.0)[:, None]
    inverse = np.concatenate([factor * np.cos(lag_angle), -factor * np.sin(lag_angle)], axis=0)
    weights = np.concatenate([factor[:, 0], factor[:, 0]])[None, :]
    return (
        jnp.asarray(forward.astype(jnp.bfloat16)),
        jnp.asarray(inverse.astype(jnp.bfloat16)),
        jnp.asarray(weights.astype(np.float32)),
    )


def pair_kernel(
    group, chunk, parts, slots_ref, *refs
):
    traces = refs[:parts]
    (
        presence_ref, forward_ref, inverse_ref, weights_ref,
        out_ref, peak_ref,
        spec_ref, gain_ref, lhs_ref,
    ) = refs[parts:]
    stations, window = spec_ref.shape[1:]
    half = window // 2
    events = spec_ref.shape[0]

    @pl.when(pl.program_id(0) == 0)
    def _():
        start = 0
        for ref in traces:
            rows = ref.shape[0]
            count = rows // stations
            result = jnp.dot(ref[...], forward_ref[...], preferred_element_type=jnp.float32)
            rounded = result.astype(jnp.bfloat16).astype(jnp.float32)
            spec_ref[pl.ds(start, count)] = rounded.reshape(count, stations, window)
            power = jnp.square(rounded) * weights_ref[...]
            energy = jnp.sum(power, axis=1, keepdims=True) + 1e-06
            gain = jnp.broadcast_to(lax.rsqrt(energy), (rows, LANES))
            gain = gain.reshape(count, stations, LANES) * presence_ref[pl.ds(start, count)]
            gain_ref[pl.ds(start, count)] = gain
            start += count
        gain_ref[events] = jnp.zeros((stations, LANES), jnp.float32)

    base = pl.program_id(0) * group
    lane = lax.broadcasted_iota(jnp.int32, (stations, LANES), 1)

    def cross(pair):
        first = spec_ref[slots_ref[0, pair]]
        second = spec_ref[slots_ref[1, pair]]
        ra, ia = first[:, :half], first[:, half:]
        rb, ib = second[:, :half], second[:, half:]
        return jnp.concatenate([ra * rb + ia * ib, ra * ib - ia * rb], axis=1)

    def one_chunk(index, peaks):
        first_pair = base + index * chunk
        for j in range(0, chunk, 2):
            both = jnp.concatenate([cross(first_pair + j), cross(first_pair + j + 1)], axis=0)
            lhs_ref[pl.ds(j * stations, 2 * stations), :] = both.astype(jnp.bfloat16)
        lagged = jnp.dot(lhs_ref[...], inverse_ref[...], preferred_element_type=jnp.float32)
        for j in range(0, chunk, 2):
            rows = []
            for i in (j, j + 1):
                pair = first_pair + i
                gain = gain_ref[slots_ref[2, pair]] * gain_ref[slots_ref[1, pair]]
                scaled = lagged[i * stations:(i + 1) * stations] * jnp.concatenate([gain, gain], axis=1)
                rows.append(scaled)
                top = jnp.max(scaled, axis=1, keepdims=True)
                peaks = jnp.where(lane == index * chunk + i, top, peaks)
            block = jnp.concatenate(rows, axis=0).astype(jnp.bfloat16)
            start = pl.multiple_of(index * chunk * stations, chunk * stations) + j * stations
            out_ref[pl.ds(start, 2 * stations), :] = block
        return peaks

    peaks = lax.fori_loop(0, group // chunk, one_chunk, jnp.zeros((stations, LANES), jnp.float32))
    peak_ref[0] = jnp.sum(peaks, axis=0, keepdims=True)


def pair_call(slots, traces, presence, tables):
    forward, inverse, weights = tables
    window = forward.shape[0]
    lags = inverse.shape[1]
    pairs = slots.shape[1]
    events, stations = presence.shape[:2]
    group = LANES
    chunk = 32
    vmem = pl.BlockSpec(memory_space=pltpu.VMEM)
    return pl.pallas_call(
        functools.partial(pair_kernel, group, chunk, len(traces)),
        grid=(pairs // group,),
        out_shape=(
            jax.ShapeDtypeStruct((pairs * stations, lags), jnp.bfloat16),
            jax.ShapeDtypeStruct((pairs // group, 1, group), jnp.float32),
        ),
        in_specs=[pl.BlockSpec(memory_space=pltpu.SMEM)] + [vmem] * (len(traces) + 4),
        out_specs=(
            pl.BlockSpec((group * stations, lags), lambda i: (i, 0)),
            pl.BlockSpec((1, 1, group), lambda i: (i, 0, 0)),
        ),
        scratch_shapes=[
            pltpu.VMEM((events, stations, window), jnp.float32),
            pltpu.VMEM((events + 1, stations, LANES), jnp.float32),
            pltpu.VMEM((chunk * stations, window), jnp.bfloat16),
        ],
        compiler_params=pltpu.CompilerParams(vmem_limit_bytes=56 * 1024 * 1024),
        cost_estimate=pl.CostEstimate(flops=4_500_000_000, bytes_accessed=8_000_000, transcendentals=0),
    )(slots, *traces, presence, forward, inverse, weights)


def exchange(waveforms, sta_count):
    events, stations, window = waveforms.shape
    share = stations // sta_count
    blocks = waveforms.reshape(events, sta_count, share, window)
    me = lax.axis_index("sta")
    half = sta_count // 2
    evt_count = lax.axis_size("evt")
    toward, away = [], []
    for e in range(evt_count):
        for s in range(sta_count):
            step = -1 if s < half else 1
            for pairs, target in ((toward, e + step), (away, e - step)):
                if 0 <= target < evt_count:
                    pairs.append((s * evt_count + e, s * evt_count + target))
    pieces = [lax.dynamic_index_in_dim(blocks, me, axis=1, keepdims=False)]
    for j in range(1, sta_count):
        piece = lax.dynamic_index_in_dim(blocks, me ^ j, axis=1, keepdims=False)
        pieces.append(lax.ppermute(piece, "sta", [(i, i ^ j) for i in range(sta_count)]))
    rows = half * events * share
    near = jnp.concatenate(pieces[:half], axis=0).reshape(rows, window)
    far = jnp.concatenate(pieces[half:], axis=0).reshape(rows, window)
    near_halo = lax.ppermute(near, ("sta", "evt"), toward)
    far_halo = lax.ppermute(far, ("sta", "evt"), away)
    return (near, far, near_halo, far_halo), me


def exchange_whole(waveforms, sta_count):
    events, stations, window = waveforms.shape
    share = stations // sta_count
    arrived = lax.all_to_all(waveforms, "sta", split_axis=1, concat_axis=0, tiled=True)
    arrived = arrived.reshape(-1, window)
    half = arrived.shape[0] // 2
    count = lax.axis_size("evt")
    down = [(i, i - 1) for i in range(1, count)]
    up = [(i, i + 1) for i in range(count - 1)]
    next_low = lax.ppermute(arrived[:half], "evt", down)
    last_high = lax.ppermute(arrived[half:], "evt", up)
    return (arrived, next_low, last_high), jnp.int32(0)


def body(waveforms, pair_events, pair_valid, presence):
    sta_count = lax.axis_size("sta")
    local_events, stations, window = waveforms.shape
    share = stations // sta_count
    block = sta_count * local_events
    tables = spectral_tables(window, LAGS)
    direct = sta_count <= 8 and sta_count & (sta_count - 1) == 0
    traces, me = (exchange if direct else exchange_whole)(waveforms, sta_count)

    start = lax.axis_index("evt") * block
    offset = pair_events - start
    inside = (offset >= 0) & (offset < block)
    flip = me * local_events
    slot = jnp.where(inside, 0, block) + ((offset % block) ^ flip)
    first, second = slot[:, 0], slot[:, 1]
    gained = jnp.where(pair_valid > 0, first, 2 * block)
    slots = jnp.stack([first, second, gained]).astype(jnp.int32)

    place = jnp.arange(2 * block, dtype=jnp.int32)
    relative = (place % block) ^ flip
    relative = jnp.where(
        place < block, relative, jnp.where(relative < block // 2, relative + block, relative - block)
    )
    held = jnp.clip(start + relative, 0, presence.shape[0] - 1)
    present = presence.astype(jnp.float32)
    slot_presence = jnp.broadcast_to(
        jnp.take(present, held, axis=0)[:, :, None], (2 * block, share, LANES)
    )
    both = jnp.take(present, pair_events[:, 0], axis=0) * jnp.take(present, pair_events[:, 1], axis=0)
    counts = jnp.sum(both, axis=1) * pair_valid.astype(jnp.float32)

    correlation, peaks = pair_call(slots, traces, slot_presence, tables)
    sums = jnp.stack([peaks.reshape(-1), counts])
    if direct:
        step = sta_count // 2
        while step:
            sums = sums + lax.ppermute(sums, "sta", [(i, i ^ step) for i in range(sta_count)])
            step //= 2
    else:
        sums = lax.psum(sums, "sta")
    pair_peak = sums[0] / jnp.maximum(sums[1], 1.0)
    return correlation.reshape(-1, share, LAGS), pair_peak


def solution(mesh):
    return jax.shard_map(
        body,
        mesh=mesh,
        in_specs=(P(("evt", "sta"), None, None), P("evt", None), P("evt"), P(None, "sta")),
        out_specs=(P("evt", "sta", None), P("evt")),
        check_vma=False,
    )
```

```python
import functools
import math

import jax
import jax.numpy as jnp
import numpy as np
from jax import lax
from jax.experimental import pallas as pl
from jax.experimental.pallas import tpu as pltpu
from jax.sharding import PartitionSpec as P

LAGS = 256
LANES = 128


def spectral_tables(window, lag_count):
    half = window // 2
    sample = np.arange(window, dtype=np.int64)
    bins = np.arange(half, dtype=np.int64)
    angle = (sample[:, None] * bins[None, :] % window) * (2.0 * math.pi / window)
    forward = np.concatenate([np.cos(angle), -np.sin(angle)], axis=1) / math.sqrt(window)
    shifts = np.arange(lag_count, dtype=np.int64) - lag_count // 2
    lag_angle = (bins[:, None] * shifts[None, :] % window) * (2.0 * math.pi / window)
    factor = np.where(bins == 0, 1.0, 2.0)[:, None]
    inverse = np.concatenate([factor * np.cos(lag_angle), -factor * np.sin(lag_angle)], axis=0)
    weights = np.concatenate([factor[:, 0], factor[:, 0]])[None, :]
    return (
        jnp.asarray(forward.astype(jnp.bfloat16)),
        jnp.asarray(inverse.astype(jnp.bfloat16)),
        jnp.asarray(weights.astype(np.float32)),
    )


def pair_kernel(
    group, chunk, parts, slots_ref, *refs
):
    traces = refs[:parts]
    (
        presence_ref, forward_ref, inverse_ref, weights_ref,
        out_ref, peak_ref,
        spec_ref, gain_ref, lhs_ref,
    ) = refs[parts:]
    stations, window = spec_ref.shape[1:]
    half = window // 2
    events = spec_ref.shape[0]

    @pl.when(pl.program_id(0) == 0)
    def _():
        start = 0
        for ref in traces:
            rows = ref.shape[0]
            count = rows // stations
            result = jnp.dot(ref[...], forward_ref[...], preferred_element_type=jnp.float32)
            rounded = result.astype(jnp.bfloat16).astype(jnp.float32)
            spec_ref[pl.ds(start, count)] = rounded.reshape(count, stations, window)
            power = jnp.square(rounded) * weights_ref[...]
            energy = jnp.sum(power, axis=1, keepdims=True) + 1e-06
            gain = jnp.broadcast_to(lax.rsqrt(energy), (rows, LANES))
            gain = gain.reshape(count, stations, LANES) * presence_ref[pl.ds(start, count)]
            gain_ref[pl.ds(start, count)] = gain
            start += count
        gain_ref[events] = jnp.zeros((stations, LANES), jnp.float32)

    base = pl.program_id(0) * group
    lane = lax.broadcasted_iota(jnp.int32, (stations, LANES), 1)

    def cross(pair):
        first = spec_ref[slots_ref[0, pair]]
        second = spec_ref[slots_ref[1, pair]]
        ra, ia = first[:, :half], first[:, half:]
        rb, ib = second[:, :half], second[:, half:]
        return jnp.concatenate([ra * rb + ia * ib, ra * ib - ia * rb], axis=1)

    def one_chunk(index, peaks):
        first_pair = base + index * chunk
        for j in range(0, chunk, 2):
            both = jnp.concatenate([cross(first_pair + j), cross(first_pair + j + 1)], axis=0)
            lhs_ref[pl.ds(j * stations, 2 * stations), :] = both.astype(jnp.bfloat16)
        lagged = jnp.dot(lhs_ref[...], inverse_ref[...], preferred_element_type=jnp.float32)
        for j in range(0, chunk, 2):
            rows = []
            for i in (j, j + 1):
                pair = first_pair + i
                gain = gain_ref[slots_ref[2, pair]] * gain_ref[slots_ref[1, pair]]
                scaled = lagged[i * stations:(i + 1) * stations] * jnp.concatenate([gain, gain], axis=1)
                rows.append(scaled)
                top = jnp.max(scaled, axis=1, keepdims=True)
                peaks = jnp.where(lane == index * chunk + i, top, peaks)
            block = jnp.concatenate(rows, axis=0).astype(jnp.bfloat16)
            start = pl.multiple_of(index * chunk * stations, chunk * stations) + j * stations
            out_ref[pl.ds(start, 2 * stations), :] = block
        return peaks

    peaks = lax.fori_loop(0, group // chunk, one_chunk, jnp.zeros((stations, LANES), jnp.float32))
    peak_ref[0] = jnp.sum(peaks, axis=0, keepdims=True)


def pair_call(slots, traces, presence, tables):
    forward, inverse, weights = tables
    window = forward.shape[0]
    lags = inverse.shape[1]
    pairs = slots.shape[1]
    events, stations = presence.shape[:2]
    group = LANES
    chunk = 32
    vmem = pl.BlockSpec(memory_space=pltpu.VMEM)
    return pl.pallas_call(
        functools.partial(pair_kernel, group, chunk, len(traces)),
        grid=(pairs // group,),
        out_shape=(
            jax.ShapeDtypeStruct((pairs * stations, lags), jnp.bfloat16),
            jax.ShapeDtypeStruct((pairs // group, 1, group), jnp.float32),
        ),
        in_specs=[pl.BlockSpec(memory_space=pltpu.SMEM)] + [vmem] * (len(traces) + 4),
        out_specs=(
            pl.BlockSpec((group * stations, lags), lambda i: (i, 0)),
            pl.BlockSpec((1, 1, group), lambda i: (i, 0, 0)),
        ),
        scratch_shapes=[
            pltpu.VMEM((events, stations, window), jnp.float32),
            pltpu.VMEM((events + 1, stations, LANES), jnp.float32),
            pltpu.VMEM((chunk * stations, window), jnp.bfloat16),
        ],
        compiler_params=pltpu.CompilerParams(vmem_limit_bytes=56 * 1024 * 1024),
        cost_estimate=pl.CostEstimate(flops=4_500_000_000, bytes_accessed=8_000_000, transcendentals=0),
    )(slots, *traces, presence, forward, inverse, weights)


def exchange(waveforms, sta_count):
    events, stations, window = waveforms.shape
    share = stations // sta_count
    blocks = waveforms.reshape(events, sta_count, share, window)
    me = lax.axis_index("sta")
    half = sta_count // 2
    evt_count = lax.axis_size("evt")
    toward, away = [], []
    for e in range(evt_count):
        for s in range(sta_count):
            step = -1 if s < half else 1
            for pairs, target in ((toward, e + step), (away, e - step)):
                if 0 <= target < evt_count:
                    pairs.append((s * evt_count + e, s * evt_count + target))
    pieces = [lax.dynamic_index_in_dim(blocks, me, axis=1, keepdims=False)]
    for j in range(1, sta_count):
        piece = lax.dynamic_index_in_dim(blocks, me ^ j, axis=1, keepdims=False)
        pieces.append(lax.ppermute(piece, "sta", [(i, i ^ j) for i in range(sta_count)]))
    rows = half * events * share
    near = jnp.concatenate(pieces[:half], axis=0).reshape(rows, window)
    far = jnp.concatenate(pieces[half:], axis=0).reshape(rows, window)
    near_halo = lax.ppermute(near, ("sta", "evt"), toward)
    far_halo = lax.ppermute(far, ("sta", "evt"), away)
    return (near, far, near_halo, far_halo), me


def exchange_whole(waveforms):
    window = waveforms.shape[2]
    arrived = lax.all_to_all(waveforms, "sta", split_axis=1, concat_axis=0, tiled=True)
    arrived = arrived.reshape(-1, window)
    half = arrived.shape[0] // 2
    count = lax.axis_size("evt")
    down = [(i, i - 1) for i in range(1, count)]
    up = [(i, i + 1) for i in range(count - 1)]
    next_low = lax.ppermute(arrived[:half], "evt", down)
    last_high = lax.ppermute(arrived[half:], "evt", up)
    return arrived, next_low, last_high


def triangle(count):
    return count * (count + 1) // 2


def own_list(block):
    band = block // 2
    return [(x, y) for x in range(block) for y in range(x + 1, min(x + band, block - 1) + 1)]


def lane_rows(count):
    return -(-count // LANES) * LANES


def own_rows(block):
    return lane_rows(2 * len(own_list(block)) + 1)


def halo_rows(block):
    return lane_rows(triangle(block // 2))


def cross_spectra(first, second):
    half = first.shape[1] // 2
    ra, ia = first[:, :half], first[:, half:]
    rb, ib = second[:, :half], second[:, half:]
    return jnp.concatenate([ra * rb + ia * ib, ra * ib - ia * rb], axis=1)


def scaled_spectra(traces_ref, me, each, place, presence_ref, present, forward_ref, weights_ref, spec_ref):
    stations, window = spec_ref.shape[1:]
    events = traces_ref.shape[0] // stations
    pieces = events // each
    result = jnp.dot(traces_ref[...], forward_ref[...], preferred_element_type=jnp.float32)
    rounded = result.astype(jnp.bfloat16).astype(jnp.float32)
    energy = jnp.sum(jnp.square(rounded) * weights_ref[...], axis=1, keepdims=True) + 1e-06
    gain = jnp.broadcast_to(lax.rsqrt(energy), (events * stations, LANES)).reshape(events, stations, LANES)
    rounded = rounded.reshape(events, stations, window)
    for j in range(pieces):
        shift = ((me ^ j) & (pieces - 1)) * each
        piece = slice(j * each, (j + 1) * each)
        scale = gain[piece] * presence_ref[pl.ds(present + shift, each)]
        scale = jnp.concatenate([scale] * (window // LANES), axis=2)
        spec_ref[pl.ds(place + shift, each)] = rounded[piece] * scale


def build(lhs_ref, low, pairs, first_of, second_of):
    for i in range(0, len(pairs), 2):
        both = [cross_spectra(first_of(x), second_of(y)) for x, y in pairs[i:i + 2]]
        rows = 2 * both[0].shape[0]
        lhs_ref[pl.ds((low + i) * rows // 2, rows), :] = jnp.concatenate(both, axis=0).astype(jnp.bfloat16)


def keep(table_ref, peaks, values, row):
    stations = peaks[0].shape[0]
    lane = lax.broadcasted_iota(jnp.int32, peaks[0].shape, 1)
    for i in range(values.shape[0] // stations):
        top = jnp.max(values[i * stations:(i + 1) * stations], axis=1, keepdims=True)
        at, within = divmod(row + i, LANES)
        peaks[at] = jnp.where(lane == within, top, peaks[at])
    table_ref[pl.ds(row * stations, values.shape[0]), :] = values.astype(jnp.bfloat16)


def no_peaks(peak_ref):
    stations, count = peak_ref.shape
    return [jnp.zeros((stations, LANES), jnp.float32) for _ in range(count // LANES)]


def own_kernel(
    each, me_ref, near_ref, far_ref, presence_ref, forward_ref, inverse_ref, weights_ref,
    spec_ref, table_ref, peak_ref, lhs_ref,
):
    block, stations, window = spec_ref.shape
    band = block // 2
    half = window // 2
    me = me_ref[0]
    mine = jnp.where(me * each < band, 0, band)
    for ref, place in ((near_ref, mine), (far_ref, band - mine)):
        scaled_spectra(
            ref, me, each, place, presence_ref, band + place, forward_ref, weights_ref, spec_ref
        )
    pairs = own_list(block)
    peaks = no_peaks(peak_ref)
    chunk = 64
    for low in range(0, len(pairs), chunk):
        some = pairs[low:low + chunk]
        held = {x: spec_ref[x] for x, _ in some}
        build(lhs_ref, low, some, lambda x: held[x], lambda y: spec_ref[y])
        rows = pl.ds(low * stations, len(some) * stations)
        even = jnp.dot(lhs_ref[rows, :half], inverse_ref[:half], preferred_element_type=jnp.float32)
        odd = jnp.dot(lhs_ref[rows, half:], inverse_ref[half:], preferred_element_type=jnp.float32)
        keep(table_ref, peaks, even + odd, low)
        keep(table_ref, peaks, even - odd, len(pairs) + low)
    peak_ref[...] = jnp.concatenate(peaks, axis=1)


def halo_kernel(
    each, is_far, me_ref, traces_ref, own_ref, presence_ref, forward_ref, inverse_ref, weights_ref,
    table_ref, peak_ref, spec_ref, lhs_ref,
):
    band, stations, window = spec_ref.shape
    me = me_ref[0]
    high = (me * each < band) != is_far
    scaled_spectra(
        traces_ref, me, each, 0, presence_ref, jnp.where(high, 3 * band, 0), forward_ref, weights_ref, spec_ref
    )

    def own(u):
        return own_ref[jnp.where(high, band + u, band - 1 - u)]

    def other(h):
        return spec_ref[jnp.where(high, h, band - 1 - h)]

    pairs = [(u, h) for u in range(band) for h in range(u + 1)]
    peaks = no_peaks(peak_ref)
    chunk = 68
    for low in range(0, len(pairs), chunk):
        some = pairs[low:low + chunk]
        held = {u: own(u) for u, _ in some}
        build(lhs_ref, low, some, lambda u: held[u], other)
        rows = pl.ds(low * stations, len(some) * stations)
        lagged = jnp.dot(lhs_ref[rows, :], inverse_ref[...], preferred_element_type=jnp.float32)
        keep(table_ref, peaks, lagged, low)
    peak_ref[...] = jnp.concatenate(peaks, axis=1)


def sum_kernel(own_ref, near_ref, far_ref, row_ref, out_ref):
    rows = row_ref[...]
    lanes = rows & (LANES - 1)
    total = jnp.zeros(rows.shape, jnp.float32)
    at = 0
    for ref in (own_ref, near_ref, far_ref):
        sums = jnp.sum(ref[...], axis=0, keepdims=True)
        for low in range(0, ref.shape[1], LANES):
            line = jnp.broadcast_to(sums[:, low:low + LANES], rows.shape)
            picked = jnp.take_along_axis(line, lanes, axis=1)
            total = jnp.where(rows // LANES == at, picked, total)
            at += 1
    out_ref[...] = total


def pick_kernel(group, starts, row_ref, *refs):
    tables, (out_ref, table_ref) = refs[:len(starts)], refs[len(starts):]
    stations, lags = table_ref.shape[1:]

    @pl.when(pl.program_id(0) == 0)
    def _():
        for ref, start in zip(tables, starts, strict=True):
            count = ref.shape[0] // stations
            wide = ref[...].astype(jnp.float32)
            table_ref[pl.ds(start, count)] = wide.reshape(count, stations, lags)
        zero = tables[0].shape[0] // stations
        table_ref[zero] = jnp.zeros((stations, lags), jnp.float32)

    base = pl.program_id(0) * group
    for j in range(0, group, 2):
        both = [table_ref[row_ref[base + i]] for i in (j, j + 1)]
        out_ref[pl.ds(j * stations, 2 * stations), :] = jnp.concatenate(both, axis=0).astype(jnp.bfloat16)


VMEM = pl.BlockSpec(memory_space=pltpu.VMEM)
SMEM = pl.BlockSpec(memory_space=pltpu.SMEM)
PARAMS = pltpu.CompilerParams(vmem_limit_bytes=40 * 1024 * 1024)


def cost(rows, lags, window, traces, moved):
    return pl.CostEstimate(
        flops=2 * window * (rows * lags + traces * window), bytes_accessed=moved, transcendentals=0
    )


def own_call(me, near, far, presence, tables, each):
    forward, inverse, weights = tables
    window, lags = inverse.shape
    block, stations = presence.shape[0] // 2, presence.shape[1]
    count = len(own_list(block))
    return pl.pallas_call(
        functools.partial(own_kernel, each),
        out_shape=(
            jax.ShapeDtypeStruct((block, stations, window), jnp.float32),
            jax.ShapeDtypeStruct((2 * count * stations, lags), jnp.bfloat16),
            jax.ShapeDtypeStruct((stations, own_rows(block)), jnp.float32),
        ),
        in_specs=[SMEM] + [VMEM] * 6,
        out_specs=(VMEM,) * 3,
        scratch_shapes=[pltpu.VMEM((count * stations, window), jnp.bfloat16)],
        compiler_params=PARAMS,
        cost_estimate=cost(count * stations, lags, window, near.shape[0] * 2, 8_000_000),
    )(me, near, far, presence, forward, inverse, weights)


def halo_call(me, traces, own, presence, tables, each, is_far):
    forward, inverse, weights = tables
    window, lags = inverse.shape
    block, stations = own.shape[:2]
    count = triangle(block // 2)
    return pl.pallas_call(
        functools.partial(halo_kernel, each, is_far),
        out_shape=(
            jax.ShapeDtypeStruct((count * stations, lags), jnp.bfloat16),
            jax.ShapeDtypeStruct((stations, halo_rows(block)), jnp.float32),
        ),
        in_specs=[SMEM] + [VMEM] * 6,
        out_specs=(VMEM,) * 2,
        scratch_shapes=[
            pltpu.VMEM((block // 2, stations, window), jnp.float32),
            pltpu.VMEM((count * stations, window), jnp.bfloat16),
        ],
        compiler_params=PARAMS,
        cost_estimate=cost(count * stations, lags, window, traces.shape[0], 4_000_000),
    )(me, traces, own, presence, forward, inverse, weights)


def sum_call(peaks, rows):
    return pl.pallas_call(
        sum_kernel,
        out_shape=jax.ShapeDtypeStruct(rows.shape, jnp.float32),
        in_specs=[VMEM] * 4,
        out_specs=VMEM,
        cost_estimate=pl.CostEstimate(flops=100_000, bytes_accessed=100_000, transcendentals=0),
    )(*peaks, rows)


def pick_call(rows, tables, starts, stations, held):
    lags = tables[0].shape[1]
    pairs = rows.shape[0]
    group = LANES
    return pl.pallas_call(
        functools.partial(pick_kernel, group, starts),
        grid=(pairs // group,),
        out_shape=jax.ShapeDtypeStruct((pairs * stations, lags), jnp.bfloat16),
        in_specs=[SMEM] + [VMEM] * len(tables),
        out_specs=pl.BlockSpec((group * stations, lags), lambda i: (i, 0)),
        scratch_shapes=[pltpu.VMEM((held, stations, lags), jnp.float32)],
        compiler_params=PARAMS,
        cost_estimate=pl.CostEstimate(flops=10_000_000, bytes_accessed=10_000_000, transcendentals=0),
    )(rows, *tables)


def table_row(first, second, me, each, block):
    band = block // 2
    low, apart = jnp.minimum(first, second), jnp.abs(first - second)
    past = jnp.maximum(low - band, 0)
    index = jnp.minimum(low, band) * band + past * (band - 1) - past * (past - 1) // 2 + apart - 1
    inside = jnp.where(second > first, index, len(own_list(block)) + index)
    high = second >= block
    u = jnp.where(high, first - band, band - 1 - first)
    h = jnp.where(high, second - block, -1 - second)
    near = high == (me * each < band)
    outside = jnp.where(near, own_rows(block), own_rows(block) + halo_rows(block)) + u * (u + 1) // 2 + h
    return jnp.where(high | (second < 0), outside, inside)


def banded(waveforms, pair_events, pair_valid, presence, start, block, tables):
    sta_count = lax.axis_size("sta")
    each = waveforms.shape[0]
    share = waveforms.shape[1] // sta_count
    (near, far, near_halo, far_halo), me = exchange(waveforms, sta_count)
    band = block // 2
    window_presence = lax.dynamic_slice_in_dim(
        jnp.pad(presence, ((band, band), (0, 0))), start, 2 * block, axis=0
    )
    held = jnp.broadcast_to(window_presence.astype(jnp.float32)[:, :, None], (2 * block, share, LANES))
    place = pair_events - start
    row = table_row(place[:, 0], place[:, 1], me, each, block)
    zero = 2 * len(own_list(block))
    starts = (0, own_rows(block), own_rows(block) + halo_rows(block))
    last = starts[2] + triangle(band)
    row = jnp.clip(jnp.where(pair_valid > 0, row, zero), 0, last - 1).astype(jnp.int32)

    at = me.reshape(1).astype(jnp.int32)
    own, own_table, own_peaks = own_call(at, near, far, held, tables, each)
    near_table, near_peaks = halo_call(at, near_halo, own, held, tables, each, False)
    far_table, far_peaks = halo_call(at, far_halo, own, held, tables, each, True)
    peaks = sum_call((own_peaks, near_peaks, far_peaks), row.reshape(-1, LANES))
    correlation = pick_call(row, (own_table, near_table, far_table), starts, share, last)
    return correlation, peaks.reshape(-1)


def by_slot(waveforms, pair_events, pair_valid, presence, start, block, tables):
    share = presence.shape[1]
    traces = exchange_whole(waveforms)
    place = pair_events - start
    slot = jnp.where((place >= 0) & (place < block), 0, block) + place % block
    gained = jnp.where(pair_valid > 0, slot[:, 0], 2 * block)
    slots = jnp.stack([slot[:, 0], slot[:, 1], gained]).astype(jnp.int32)
    held = jnp.arange(2 * block, dtype=jnp.int32)
    held = jnp.where(held < block, held, jnp.where(held < block + block // 2, held, held - 2 * block))
    held = jnp.clip(start + held, 0, presence.shape[0] - 1)
    slot_presence = jnp.broadcast_to(
        jnp.take(presence.astype(jnp.float32), held, axis=0)[:, :, None], (2 * block, share, LANES)
    )
    correlation, peaks = pair_call(slots, traces, slot_presence, tables)
    return correlation, peaks.reshape(-1)


def body(waveforms, pair_events, pair_valid, presence):
    sta_count = lax.axis_size("sta")
    local_events, stations, window = waveforms.shape
    share = stations // sta_count
    block = sta_count * local_events
    start = lax.axis_index("evt") * block
    tables = spectral_tables(window, LAGS)

    few = presence.astype(jnp.bfloat16)
    event = jnp.arange(presence.shape[0], dtype=jnp.int32)
    first, second = (
        jnp.dot((pair_events[:, i:i + 1] == event).astype(jnp.bfloat16), few, preferred_element_type=jnp.float32)
        for i in (0, 1)
    )
    counts = jnp.sum(first * second, axis=1) * pair_valid.astype(jnp.float32)

    dense = sta_count == 8 and block * block <= pair_events.shape[0]
    plan = banded if dense else by_slot
    correlation, peaks = plan(waveforms, pair_events, pair_valid, presence, start, block, tables)
    sums = jnp.stack([peaks, counts])
    if dense:
        step = sta_count // 2
        while step:
            sums = sums + lax.ppermute(sums, "sta", [(i, i ^ step) for i in range(sta_count)])
            step //= 2
    else:
        sums = lax.psum(sums, "sta")
    pair_peak = sums[0] / jnp.maximum(sums[1], 1.0)
    return correlation.reshape(-1, share, LAGS), pair_peak


def solution(mesh):
    return jax.shard_map(
        body,
        mesh=mesh,
        in_specs=(P(("evt", "sta"), None, None), P("evt", None), P("evt"), P(None, "sta")),
        out_specs=(P("evt", "sta", None), P("evt")),
        check_vma=False,
    )
```

```python
import functools
import math

import jax
import jax.numpy as jnp
import numpy as np
from jax import lax
from jax.experimental import pallas as pl
from jax.experimental.pallas import tpu as pltpu
from jax.sharding import PartitionSpec as P

LAGS = 256
LANES = 128


def spectral_tables(window, lag_count):
    half = window // 2
    sample = np.arange(window, dtype=np.int64)
    bins = np.arange(half, dtype=np.int64)
    angle = (sample[:, None] * bins[None, :] % window) * (2.0 * math.pi / window)
    forward = np.concatenate([np.cos(angle), -np.sin(angle)], axis=1) / math.sqrt(window)
    shifts = np.arange(lag_count, dtype=np.int64) - lag_count // 2
    lag_angle = (bins[:, None] * shifts[None, :] % window) * (2.0 * math.pi / window)
    factor = np.where(bins == 0, 1.0, 2.0)[:, None]
    inverse = np.concatenate([factor * np.cos(lag_angle), -factor * np.sin(lag_angle)], axis=0)
    weights = np.concatenate([factor[:, 0], factor[:, 0]])[None, :]
    return (
        jnp.asarray(forward.astype(jnp.bfloat16)),
        jnp.asarray(inverse.astype(jnp.bfloat16)),
        jnp.asarray(weights.astype(np.float32)),
    )


def pair_kernel(
    group, chunk, parts, slots_ref, *refs
):
    traces = refs[:parts]
    (
        presence_ref, forward_ref, inverse_ref, weights_ref,
        out_ref, peak_ref,
        spec_ref, gain_ref, lhs_ref,
    ) = refs[parts:]
    stations, window = spec_ref.shape[1:]
    half = window // 2
    events = spec_ref.shape[0]

    @pl.when(pl.program_id(0) == 0)
    def _():
        start = 0
        for ref in traces:
            rows = ref.shape[0]
            count = rows // stations
            result = jnp.dot(ref[...], forward_ref[...], preferred_element_type=jnp.float32)
            rounded = result.astype(jnp.bfloat16).astype(jnp.float32)
            spec_ref[pl.ds(start, count)] = rounded.reshape(count, stations, window)
            power = jnp.square(rounded) * weights_ref[...]
            energy = jnp.sum(power, axis=1, keepdims=True) + 1e-06
            gain = jnp.broadcast_to(lax.rsqrt(energy), (rows, LANES))
            gain = gain.reshape(count, stations, LANES) * presence_ref[pl.ds(start, count)]
            gain_ref[pl.ds(start, count)] = gain
            start += count
        gain_ref[events] = jnp.zeros((stations, LANES), jnp.float32)

    base = pl.program_id(0) * group
    lane = lax.broadcasted_iota(jnp.int32, (stations, LANES), 1)

    def cross(pair):
        first = spec_ref[slots_ref[0, pair]]
        second = spec_ref[slots_ref[1, pair]]
        ra, ia = first[:, :half], first[:, half:]
        rb, ib = second[:, :half], second[:, half:]
        return jnp.concatenate([ra * rb + ia * ib, ra * ib - ia * rb], axis=1)

    def one_chunk(index, peaks):
        first_pair = base + index * chunk
        for j in range(0, chunk, 2):
            both = jnp.concatenate([cross(first_pair + j), cross(first_pair + j + 1)], axis=0)
            lhs_ref[pl.ds(j * stations, 2 * stations), :] = both.astype(jnp.bfloat16)
        lagged = jnp.dot(lhs_ref[...], inverse_ref[...], preferred_element_type=jnp.float32)
        for j in range(0, chunk, 2):
            rows = []
            for i in (j, j + 1):
                pair = first_pair + i
                gain = gain_ref[slots_ref[2, pair]] * gain_ref[slots_ref[1, pair]]
                scaled = lagged[i * stations:(i + 1) * stations] * jnp.concatenate([gain, gain], axis=1)
                rows.append(scaled)
                top = jnp.max(scaled, axis=1, keepdims=True)
                peaks = jnp.where(lane == index * chunk + i, top, peaks)
            block = jnp.concatenate(rows, axis=0).astype(jnp.bfloat16)
            start = pl.multiple_of(index * chunk * stations, chunk * stations) + j * stations
            out_ref[pl.ds(start, 2 * stations), :] = block
        return peaks

    peaks = lax.fori_loop(0, group // chunk, one_chunk, jnp.zeros((stations, LANES), jnp.float32))
    peak_ref[0] = jnp.sum(peaks, axis=0, keepdims=True)


def pair_call(slots, traces, presence, tables):
    forward, inverse, weights = tables
    window = forward.shape[0]
    lags = inverse.shape[1]
    pairs = slots.shape[1]
    events, stations = presence.shape[:2]
    group = LANES
    chunk = 32
    vmem = pl.BlockSpec(memory_space=pltpu.VMEM)
    return pl.pallas_call(
        functools.partial(pair_kernel, group, chunk, len(traces)),
        grid=(pairs // group,),
        out_shape=(
            jax.ShapeDtypeStruct((pairs * stations, lags), jnp.bfloat16),
            jax.ShapeDtypeStruct((pairs // group, 1, group), jnp.float32),
        ),
        in_specs=[pl.BlockSpec(memory_space=pltpu.SMEM)] + [vmem] * (len(traces) + 4),
        out_specs=(
            pl.BlockSpec((group * stations, lags), lambda i: (i, 0)),
            pl.BlockSpec((1, 1, group), lambda i: (i, 0, 0)),
        ),
        scratch_shapes=[
            pltpu.VMEM((events, stations, window), jnp.float32),
            pltpu.VMEM((events + 1, stations, LANES), jnp.float32),
            pltpu.VMEM((chunk * stations, window), jnp.bfloat16),
        ],
        compiler_params=pltpu.CompilerParams(vmem_limit_bytes=56 * 1024 * 1024),
        cost_estimate=pl.CostEstimate(flops=4_500_000_000, bytes_accessed=8_000_000, transcendentals=0),
    )(slots, *traces, presence, forward, inverse, weights)


def exchange(waveforms, sta_count):
    events, stations, window = waveforms.shape
    share = stations // sta_count
    blocks = waveforms.reshape(events, sta_count, share, window)
    me = lax.axis_index("sta")
    half = sta_count // 2
    evt_count = lax.axis_size("evt")
    toward, away = [], []
    for e in range(evt_count):
        for s in range(sta_count):
            step = -1 if s < half else 1
            for pairs, target in ((toward, e + step), (away, e - step)):
                if 0 <= target < evt_count:
                    pairs.append((s * evt_count + e, s * evt_count + target))
    pieces = [lax.dynamic_index_in_dim(blocks, me, axis=1, keepdims=False)]
    for j in range(1, sta_count):
        piece = lax.dynamic_index_in_dim(blocks, me ^ j, axis=1, keepdims=False)
        pieces.append(lax.ppermute(piece, "sta", [(i, i ^ j) for i in range(sta_count)]))
    rows = half * events * share
    near = jnp.concatenate(pieces[:half], axis=0).reshape(rows, window)
    far = jnp.concatenate(pieces[half:], axis=0).reshape(rows, window)
    near_halo = lax.ppermute(near, ("sta", "evt"), toward)
    far_halo = lax.ppermute(far, ("sta", "evt"), away)
    return (near, far, near_halo, far_halo), me


def exchange_whole(waveforms):
    window = waveforms.shape[2]
    arrived = lax.all_to_all(waveforms, "sta", split_axis=1, concat_axis=0, tiled=True)
    arrived = arrived.reshape(-1, window)
    half = arrived.shape[0] // 2
    count = lax.axis_size("evt")
    down = [(i, i - 1) for i in range(1, count)]
    up = [(i, i + 1) for i in range(count - 1)]
    next_low = lax.ppermute(arrived[:half], "evt", down)
    last_high = lax.ppermute(arrived[half:], "evt", up)
    return arrived, next_low, last_high


def triangle(count):
    return count * (count + 1) // 2


def own_list(block):
    band = block // 2
    return [(x, y) for x in range(block) for y in range(x + 1, min(x + band, block - 1) + 1)]


class Rows:
    def __init__(self, block):
        self.own = len(own_list(block))
        self.zero = 2 * self.own
        self.near = self.zero + 8
        self.far = self.near + triangle(block // 2)
        self.end = self.far + triangle(block // 2)
        self.lanes = -(-self.end // LANES) * LANES


def cross_spectra(first, second):
    half = first.shape[1] // 2
    ra, ia = first[:, :half], first[:, half:]
    rb, ib = second[:, :half], second[:, half:]
    return jnp.concatenate([ra * rb + ia * ib, ra * ib - ia * rb], axis=1)


def scaled_spectra(traces_ref, me, each, place, presence_ref, present, forward_ref, weights_ref, spec_ref):
    stations, window = spec_ref.shape[1:]
    events = traces_ref.shape[0] // stations
    pieces = events // each
    result = jnp.dot(traces_ref[...], forward_ref[...], preferred_element_type=jnp.float32)
    rounded = result.astype(jnp.bfloat16).astype(jnp.float32)
    energy = jnp.sum(jnp.square(rounded) * weights_ref[...], axis=1, keepdims=True) + 1e-06
    gain = jnp.broadcast_to(lax.rsqrt(energy), (events * stations, LANES)).reshape(events, stations, LANES)
    rounded = rounded.reshape(events, stations, window)
    for j in range(pieces):
        shift = ((me ^ j) & (pieces - 1)) * each
        piece = slice(j * each, (j + 1) * each)
        scale = gain[piece] * presence_ref[pl.ds(present + shift, each)]
        scale = jnp.concatenate([scale] * (window // LANES), axis=2)
        spec_ref[pl.ds(place + shift, each)] = rounded[piece] * scale


def build(lhs_ref, low, pairs, first_of, second_of):
    for i in range(0, len(pairs), 2):
        both = [cross_spectra(first_of(x), second_of(y)) for x, y in pairs[i:i + 2]]
        rows = 2 * both[0].shape[0]
        lhs_ref[pl.ds((low + i) * rows // 2, rows), :] = jnp.concatenate(both, axis=0).astype(jnp.bfloat16)


def keep(table_ref, peaks, values, row):
    stations, lags = table_ref.shape[1:]
    lane = lax.broadcasted_iota(jnp.int32, (stations, LANES), 1)
    count = values.shape[0] // stations
    for i in range(count):
        top = jnp.max(values[i * stations:(i + 1) * stations], axis=1, keepdims=True)
        at, within = divmod(row + i, LANES)
        peaks[at] = jnp.where(lane == within, top, peaks[at])
    table_ref[pl.ds(row, count)] = values.reshape(count, stations, lags).astype(jnp.bfloat16)


def no_peaks(rows, stations):
    return [jnp.zeros((stations, LANES), jnp.float32) for _ in range(rows.lanes // LANES)]


def prepare_kernel(
    each, block, at_ref, events_ref, valid_ref, presence_ref, forward_ref, inverse_ref,
    row_ref, count_ref, held_ref, forward_out, inverse_out, sems,
):
    copies = [
        pltpu.make_async_copy(forward_ref, forward_out, sems.at[0]),
        pltpu.make_async_copy(inverse_ref, inverse_out, sems.at[1]),
    ]
    for copy in copies:
        copy.start()
    me, start = at_ref[0], at_ref[1]
    lines = row_ref.shape[0]

    def stacked(ref, line):
        return jnp.concatenate([ref[line:line + 1, i * LANES:(i + 1) * LANES] for i in range(lines)], axis=0)

    first, second, valid = stacked(events_ref, 0), stacked(events_ref, 1), stacked(valid_ref, 0)
    rows = Rows(block)
    row = table_row(first - start, second - start, me, each, block, rows)
    row = jnp.where(valid > 0, row, rows.zero)
    row_ref[...] = jnp.clip(row, 0, rows.end - 1)

    presence = presence_ref[...]
    stations, events = presence.shape
    bits = jnp.zeros((1, events), jnp.int32)
    for s in range(stations):
        bits = bits + presence[s:s + 1] * (1 << s)
    bits = jnp.broadcast_to(bits, (lines, events))
    both = jnp.take_along_axis(bits, first, axis=1) & jnp.take_along_axis(bits, second, axis=1)
    count = jnp.zeros_like(both)
    for s in range(stations):
        count = count + (lax.shift_right_logical(both, s) & 1)
    count_ref[...] = (count * valid).astype(jnp.float32)

    lane = lax.broadcasted_iota(jnp.int32, presence.shape, 1)
    present = presence.astype(jnp.float32)
    for i in range(held_ref.shape[0]):
        mine = jnp.where(lane == start - block // 2 + i, present, 0.0)
        held_ref[i] = jnp.broadcast_to(jnp.sum(mine, axis=1, keepdims=True), (stations, LANES))
    for copy in copies:
        copy.wait()


def own_pairs(spec_ref, inverse_ref, table_ref, peaks, lhs_ref):
    block, stations, window = spec_ref.shape
    half = window // 2
    pairs = own_list(block)
    chunk = 64
    for low in range(0, len(pairs), chunk):
        some = pairs[low:low + chunk]
        held = {x: spec_ref[x] for x, _ in some}
        build(lhs_ref, low, some, lambda x: held[x], lambda y: spec_ref[y])
        rows = pl.ds(low * stations, len(some) * stations)
        even = jnp.dot(lhs_ref[rows, :half], inverse_ref[:half], preferred_element_type=jnp.float32)
        odd = jnp.dot(lhs_ref[rows, half:], inverse_ref[half:], preferred_element_type=jnp.float32)
        keep(table_ref, peaks, even + odd, low)
        keep(table_ref, peaks, even - odd, len(pairs) + low)


def halo_pairs(high, own_ref, spec_ref, inverse_ref, table_ref, peaks, lhs_ref, row):
    band, stations = spec_ref.shape[:2]

    def own(u):
        return own_ref[jnp.where(high, band + u, band - 1 - u)]

    def other(h):
        return spec_ref[jnp.where(high, h, band - 1 - h)]

    pairs = [(u, h) for u in range(band) for h in range(u + 1)]
    chunk = 68
    for low in range(0, len(pairs), chunk):
        some = pairs[low:low + chunk]
        held = {u: own(u) for u, _ in some}
        build(lhs_ref, low, some, lambda u: held[u], other)
        rows = pl.ds(low * stations, len(some) * stations)
        lagged = jnp.dot(lhs_ref[rows, :], inverse_ref[...], preferred_element_type=jnp.float32)
        keep(table_ref, peaks, lagged, row + low)


def first_kernel(
    each, at_ref, near_ref, far_ref, halo_ref, presence_ref, forward_ref, inverse_ref, weights_ref,
    spec_ref, table_ref, peak_ref, other_ref, lhs_ref,
):
    block, stations, window = spec_ref.shape
    band = block // 2
    me = at_ref[0]
    low_half = me * each < band
    mine = jnp.where(low_half, 0, band)
    for ref, place in ((near_ref, mine), (far_ref, band - mine)):
        scaled_spectra(
            ref, me, each, place, presence_ref, band + place, forward_ref, weights_ref, spec_ref
        )
    edge = jnp.where(low_half, 3 * band, 0)
    scaled_spectra(halo_ref, me, each, 0, presence_ref, edge, forward_ref, weights_ref, other_ref)
    rows = Rows(block)
    peaks = no_peaks(rows, stations)
    own_pairs(spec_ref, inverse_ref, table_ref, peaks, lhs_ref)
    halo_pairs(low_half, spec_ref, other_ref, inverse_ref, table_ref, peaks, lhs_ref, rows.near)
    table_ref[rows.zero] = jnp.zeros(table_ref.shape[1:], table_ref.dtype)
    peak_ref[...] = jnp.concatenate(peaks, axis=1)


def last_kernel(
    each, at_ref, halo_ref, own_ref, presence_ref, forward_ref, inverse_ref, weights_ref, peak_ref, row_ref, count_ref,
    held_table_ref, table_ref, sums_ref, other_ref, lhs_ref,
):
    del held_table_ref
    block, stations, window = own_ref.shape
    band = block // 2
    me = at_ref[0]
    high = me * each >= band
    edge = jnp.where(high, 3 * band, 0)
    scaled_spectra(halo_ref, me, each, 0, presence_ref, edge, forward_ref, weights_ref, other_ref)
    rows = Rows(block)
    peaks = no_peaks(rows, stations)
    halo_pairs(high, own_ref, other_ref, inverse_ref, table_ref, peaks, lhs_ref, rows.far)
    row = row_ref[...]
    lanes = row & (LANES - 1)
    total = jnp.zeros(row.shape, jnp.float32)
    for at, late in enumerate(peaks):
        line = jnp.sum(peak_ref[:, at * LANES:(at + 1) * LANES] + late, axis=0, keepdims=True)
        picked = jnp.take_along_axis(jnp.broadcast_to(line, row.shape), lanes, axis=1)
        total = jnp.where(lax.shift_right_logical(row, 7) == at, picked, total)
    sums_ref[0] = total
    sums_ref[1] = count_ref[...]


def pick_kernel(group, skip, row_ref, table_ref, *refs):
    out_ref = refs[-1]
    base = (pl.program_id(0) + skip) * group
    for j in range(group):
        out_ref[j] = table_ref[row_ref[base + j]]


VMEM = pl.BlockSpec(memory_space=pltpu.VMEM)
SMEM = pl.BlockSpec(memory_space=pltpu.SMEM)
PARAMS = pltpu.CompilerParams(vmem_limit_bytes=20 * 1024 * 1024)


def cost(rows, lags, window, traces, moved):
    return pl.CostEstimate(
        flops=2 * window * (rows * lags + traces * window), bytes_accessed=moved, transcendentals=0
    )


def prepare_call(at, pair_events, pair_valid, presence, tables, each, block):
    forward, inverse = tables[:2]
    pairs = pair_events.shape[0]
    stations = presence.shape[1]
    line = (pairs // LANES, LANES)
    anywhere = pl.BlockSpec(memory_space=pl.ANY)
    return pl.pallas_call(
        functools.partial(prepare_kernel, each, block),
        out_shape=(
            jax.ShapeDtypeStruct(line, jnp.int32),
            jax.ShapeDtypeStruct(line, jnp.float32),
            jax.ShapeDtypeStruct((2 * block, stations, LANES), jnp.float32),
            jax.ShapeDtypeStruct(forward.shape, forward.dtype),
            jax.ShapeDtypeStruct(inverse.shape, inverse.dtype),
        ),
        in_specs=[SMEM] + [VMEM] * 3 + [anywhere] * 2,
        out_specs=(VMEM,) * 5,
        scratch_shapes=[pltpu.SemaphoreType.DMA((2,))],
        compiler_params=PARAMS,
        cost_estimate=pl.CostEstimate(flops=1_000_000, bytes_accessed=5_000_000, transcendentals=0),
    )(at, pair_events.T, pair_valid.reshape(1, pairs), presence.T, forward, inverse)


def first_call(at, near, far, halo, presence, tables, each, block):
    forward, inverse, weights = tables
    window, lags = inverse.shape
    stations = presence.shape[1]
    rows = Rows(block)
    return pl.pallas_call(
        functools.partial(first_kernel, each),
        out_shape=(
            jax.ShapeDtypeStruct((block, stations, window), jnp.float32),
            jax.ShapeDtypeStruct((rows.end, stations, lags), jnp.bfloat16),
            jax.ShapeDtypeStruct((stations, rows.lanes), jnp.float32),
        ),
        in_specs=[SMEM] + [VMEM] * 7,
        out_specs=(VMEM,) * 3,
        scratch_shapes=[
            pltpu.VMEM((block // 2, stations, window), jnp.float32),
            pltpu.VMEM((rows.own * stations, window), jnp.bfloat16),
        ],
        compiler_params=PARAMS,
        cost_estimate=cost(rows.far * stations, lags, window, near.shape[0] * 3, 8_000_000),
    )(at, near, far, halo, presence, forward, inverse, weights)


def last_call(at, halo, own, presence, tables, peaks, row, count, table, each):
    forward, inverse, weights = tables
    window, lags = inverse.shape
    block, stations = own.shape[:2]
    pairs = triangle(block // 2)
    return pl.pallas_call(
        functools.partial(last_kernel, each),
        out_shape=(
            jax.ShapeDtypeStruct(table.shape, table.dtype),
            jax.ShapeDtypeStruct((2,) + row.shape, jnp.float32),
        ),
        in_specs=[SMEM] + [VMEM] * 10,
        out_specs=(VMEM,) * 2,
        scratch_shapes=[
            pltpu.VMEM((block // 2, stations, window), jnp.float32),
            pltpu.VMEM((pairs * stations, window), jnp.bfloat16),
        ],
        input_output_aliases={10: 0},
        compiler_params=PARAMS,
        cost_estimate=cost(pairs * stations, lags, window, halo.shape[0], 4_000_000),
    )(at, halo, own, presence, forward, inverse, weights, peaks, row, count, table)


def pick_call(row, table, held, skip, steps):
    pairs = row.shape[0]
    block = (LANES,) + table.shape[1:]
    return pl.pallas_call(
        functools.partial(pick_kernel, LANES, skip),
        grid=(steps,),
        out_shape=jax.ShapeDtypeStruct((pairs,) + table.shape[1:], table.dtype),
        in_specs=[SMEM, VMEM] + [pl.BlockSpec(memory_space=pl.ANY)] * len(held),
        out_specs=pl.BlockSpec(block, lambda i: (i + skip, 0, 0)),
        input_output_aliases={2: 0} if held else {},
        compiler_params=PARAMS,
        cost_estimate=pl.CostEstimate(flops=1_000_000, bytes_accessed=3_000_000 * steps, transcendentals=0),
    )(row, table, *held)


def table_row(first, second, me, each, block, rows):
    band = block // 2
    low, apart = jnp.minimum(first, second), jnp.abs(first - second)
    past = jnp.maximum(low - band, 0)
    index = jnp.minimum(low, band) * band + past * (band - 1) - (past * (past - 1) >> 1) + apart - 1
    inside = jnp.where(second > first, index, rows.own + index)
    high = second >= block
    u = jnp.where(high, first - band, band - 1 - first)
    h = jnp.where(high, second - block, -1 - second)
    near = jnp.where(high, 1, 0) == jnp.where(me * each < band, 1, 0)
    outside = jnp.where(near, rows.near, rows.far) + (u * (u + 1) >> 1) + h
    return jnp.where(high | (second < 0), outside, inside)


def banded(waveforms, pair_events, pair_valid, presence, start, block, tables):
    each = waveforms.shape[0]
    (near, far, near_halo, far_halo), me = exchange(waveforms, lax.axis_size("sta"))
    at = jnp.stack([me, start]).astype(jnp.int32)
    near, at = lax.optimization_barrier((near, at))
    row, count, held, forward, inverse = prepare_call(at, pair_events, pair_valid, presence, tables, each, block)
    tables = (forward, inverse, tables[2])
    own, table, peaks = first_call(at, near, far, near_halo, held, tables, each, block)
    table, sums = last_call(at, far_halo, own, held, tables, peaks, row, count, table, each)

    row = row.reshape(-1)
    groups = row.shape[0] // LANES
    correlation = ()
    step, skip = lax.axis_size("sta") // 2, 0
    while step:
        arrived = lax.ppermute(sums, "sta", [(i, i ^ step) for i in range(lax.axis_size("sta"))])
        steps = -(-(groups - skip) // step.bit_length())
        correlation = (pick_call(row, table, correlation, skip, steps),)
        sums, correlation = lax.optimization_barrier((sums + arrived, correlation))
        skip += steps
        step //= 2
    return correlation[0], sums


def by_slot(waveforms, pair_events, pair_valid, presence, start, block, tables):
    share = presence.shape[1]
    traces = exchange_whole(waveforms)
    place = pair_events - start
    slot = jnp.where((place >= 0) & (place < block), 0, block) + place % block
    gained = jnp.where(pair_valid > 0, slot[:, 0], 2 * block)
    slots = jnp.stack([slot[:, 0], slot[:, 1], gained]).astype(jnp.int32)
    held = jnp.arange(2 * block, dtype=jnp.int32)
    held = jnp.where(held < block, held, jnp.where(held < block + block // 2, held, held - 2 * block))
    held = jnp.clip(start + held, 0, presence.shape[0] - 1)
    slot_presence = jnp.broadcast_to(
        jnp.take(presence.astype(jnp.float32), held, axis=0)[:, :, None], (2 * block, share, LANES)
    )
    few = presence.astype(jnp.bfloat16)
    event = jnp.arange(presence.shape[0], dtype=jnp.int32)
    first, second = (
        jnp.dot((pair_events[:, i:i + 1] == event).astype(jnp.bfloat16), few, preferred_element_type=jnp.float32)
        for i in (0, 1)
    )
    counts = jnp.sum(first * second, axis=1) * pair_valid.astype(jnp.float32)
    correlation, peaks = pair_call(slots, traces, slot_presence, tables)
    sums = lax.psum(jnp.stack([peaks.reshape(-1), counts]), "sta")
    return correlation.reshape(-1, share, correlation.shape[1]), sums


def body(waveforms, pair_events, pair_valid, presence):
    sta_count = lax.axis_size("sta")
    local_events, stations, window = waveforms.shape
    block = sta_count * local_events
    start = lax.axis_index("evt") * block
    tables = spectral_tables(window, LAGS)
    args = (waveforms, pair_events, pair_valid, presence, start, block, tables)
    dense = sta_count == 8 and presence.shape[0] == LANES and block * block <= pair_events.shape[0]
    correlation, sums = (banded if dense else by_slot)(*args)
    pair_peak = sums[0] / jnp.maximum(sums[1], 1.0)
    return correlation, pair_peak.reshape(-1)


def solution(mesh):
    return jax.shard_map(
        body,
        mesh=mesh,
        in_specs=(P(("evt", "sta"), None, None), P("evt", None), P("evt"), P(None, "sta")),
        out_specs=(P("evt", "sta", None), P("evt")),
        check_vma=False,
    )
```

```python
import functools
import math

import jax
import jax.numpy as jnp
import numpy as np
from jax import lax
from jax.experimental import pallas as pl
from jax.experimental.pallas import tpu as pltpu
from jax.sharding import PartitionSpec as P

LAGS = 256
LANES = 128


def spectral_tables(window, lag_count):
    half = window // 2
    sample = np.arange(window, dtype=np.int64)
    bins = np.arange(half, dtype=np.int64)
    angle = (sample[:, None] * bins[None, :] % window) * (2.0 * math.pi / window)
    forward = np.concatenate([np.cos(angle), -np.sin(angle)], axis=1) / math.sqrt(window)
    shifts = np.arange(lag_count, dtype=np.int64) - lag_count // 2
    lag_angle = (bins[:, None] * shifts[None, :] % window) * (2.0 * math.pi / window)
    factor = np.where(bins == 0, 1.0, 2.0)[:, None]
    inverse = np.concatenate([factor * np.cos(lag_angle), -factor * np.sin(lag_angle)], axis=0)
    weights = np.concatenate([factor[:, 0], factor[:, 0]])[None, :]
    return (
        jnp.asarray(forward.astype(jnp.bfloat16)),
        jnp.asarray(inverse.astype(jnp.bfloat16)),
        jnp.asarray(weights.astype(np.float32)),
    )


def pair_kernel(
    group, chunk, parts, slots_ref, *refs
):
    traces = refs[:parts]
    (
        presence_ref, forward_ref, inverse_ref, weights_ref,
        out_ref, peak_ref,
        spec_ref, gain_ref, lhs_ref,
    ) = refs[parts:]
    stations, window = spec_ref.shape[1:]
    half = window // 2
    events = spec_ref.shape[0]

    @pl.when(pl.program_id(0) == 0)
    def _():
        start = 0
        for ref in traces:
            rows = ref.shape[0]
            count = rows // stations
            result = jnp.dot(ref[...], forward_ref[...], preferred_element_type=jnp.float32)
            rounded = result.astype(jnp.bfloat16).astype(jnp.float32)
            spec_ref[pl.ds(start, count)] = rounded.reshape(count, stations, window)
            power = jnp.square(rounded) * weights_ref[...]
            energy = jnp.sum(power, axis=1, keepdims=True) + 1e-06
            gain = jnp.broadcast_to(lax.rsqrt(energy), (rows, LANES))
            gain = gain.reshape(count, stations, LANES) * presence_ref[pl.ds(start, count)]
            gain_ref[pl.ds(start, count)] = gain
            start += count
        gain_ref[events] = jnp.zeros((stations, LANES), jnp.float32)

    base = pl.program_id(0) * group
    lane = lax.broadcasted_iota(jnp.int32, (stations, LANES), 1)

    def cross(pair):
        first = spec_ref[slots_ref[0, pair]]
        second = spec_ref[slots_ref[1, pair]]
        ra, ia = first[:, :half], first[:, half:]
        rb, ib = second[:, :half], second[:, half:]
        return jnp.concatenate([ra * rb + ia * ib, ra * ib - ia * rb], axis=1)

    def one_chunk(index, peaks):
        first_pair = base + index * chunk
        for j in range(0, chunk, 2):
            both = jnp.concatenate([cross(first_pair + j), cross(first_pair + j + 1)], axis=0)
            lhs_ref[pl.ds(j * stations, 2 * stations), :] = both.astype(jnp.bfloat16)
        lagged = jnp.dot(lhs_ref[...], inverse_ref[...], preferred_element_type=jnp.float32)
        for j in range(0, chunk, 2):
            rows = []
            for i in (j, j + 1):
                pair = first_pair + i
                gain = gain_ref[slots_ref[2, pair]] * gain_ref[slots_ref[1, pair]]
                scaled = lagged[i * stations:(i + 1) * stations] * jnp.concatenate([gain, gain], axis=1)
                rows.append(scaled)
                top = jnp.max(scaled, axis=1, keepdims=True)
                peaks = jnp.where(lane == index * chunk + i, top, peaks)
            block = jnp.concatenate(rows, axis=0).astype(jnp.bfloat16)
            start = pl.multiple_of(index * chunk * stations, chunk * stations) + j * stations
            out_ref[pl.ds(start, 2 * stations), :] = block
        return peaks

    peaks = lax.fori_loop(0, group // chunk, one_chunk, jnp.zeros((stations, LANES), jnp.float32))
    peak_ref[0] = jnp.sum(peaks, axis=0, keepdims=True)


def pair_call(slots, traces, presence, tables):
    forward, inverse, weights = tables
    window = forward.shape[0]
    lags = inverse.shape[1]
    pairs = slots.shape[1]
    events, stations = presence.shape[:2]
    group = LANES
    chunk = 32
    vmem = pl.BlockSpec(memory_space=pltpu.VMEM)
    return pl.pallas_call(
        functools.partial(pair_kernel, group, chunk, len(traces)),
        grid=(pairs // group,),
        out_shape=(
            jax.ShapeDtypeStruct((pairs * stations, lags), jnp.bfloat16),
            jax.ShapeDtypeStruct((pairs // group, 1, group), jnp.float32),
        ),
        in_specs=[pl.BlockSpec(memory_space=pltpu.SMEM)] + [vmem] * (len(traces) + 4),
        out_specs=(
            pl.BlockSpec((group * stations, lags), lambda i: (i, 0)),
            pl.BlockSpec((1, 1, group), lambda i: (i, 0, 0)),
        ),
        scratch_shapes=[
            pltpu.VMEM((events, stations, window), jnp.float32),
            pltpu.VMEM((events + 1, stations, LANES), jnp.float32),
            pltpu.VMEM((chunk * stations, window), jnp.bfloat16),
        ],
        compiler_params=pltpu.CompilerParams(vmem_limit_bytes=56 * 1024 * 1024),
        cost_estimate=pl.CostEstimate(flops=4_500_000_000, bytes_accessed=8_000_000, transcendentals=0),
    )(slots, *traces, presence, forward, inverse, weights)


def exchange(waveforms, sta_count):
    events, stations, window = waveforms.shape
    share = stations // sta_count
    blocks = waveforms.reshape(events, sta_count, share, window)
    me = lax.axis_index("sta")
    half = sta_count // 2
    evt_count = lax.axis_size("evt")
    toward, away = [], []
    for e in range(evt_count):
        for s in range(sta_count):
            step = -1 if s < half else 1
            for pairs, target in ((toward, e + step), (away, e - step)):
                if 0 <= target < evt_count:
                    pairs.append((s * evt_count + e, s * evt_count + target))
    pieces = [lax.dynamic_index_in_dim(blocks, me, axis=1, keepdims=False)]
    for j in range(1, sta_count):
        piece = lax.dynamic_index_in_dim(blocks, me ^ j, axis=1, keepdims=False)
        pieces.append(lax.ppermute(piece, "sta", [(i, i ^ j) for i in range(sta_count)]))
    rows = half * events * share
    near = jnp.concatenate(pieces[:half], axis=0).reshape(rows, window)
    far = jnp.concatenate(pieces[half:], axis=0).reshape(rows, window)
    return near, far, toward, away


def exchange_whole(waveforms):
    window = waveforms.shape[2]
    arrived = lax.all_to_all(waveforms, "sta", split_axis=1, concat_axis=0, tiled=True)
    arrived = arrived.reshape(-1, window)
    half = arrived.shape[0] // 2
    count = lax.axis_size("evt")
    down = [(i, i - 1) for i in range(1, count)]
    up = [(i, i + 1) for i in range(count - 1)]
    next_low = lax.ppermute(arrived[:half], "evt", down)
    last_high = lax.ppermute(arrived[half:], "evt", up)
    return arrived, next_low, last_high


def triangle(count):
    return count * (count + 1) // 2


def own_list(block):
    band = block // 2
    return [(x, y) for x in range(block) for y in range(x + 1, min(x + band, block - 1) + 1)]


class Rows:
    def __init__(self, block):
        self.own = len(own_list(block))
        self.zero = 2 * self.own
        self.near = self.zero + 8
        self.far = self.near + triangle(block // 2)
        self.end = self.far + triangle(block // 2)
        self.lanes = -(-self.end // LANES) * LANES


def cross_spectra(first, second):
    half = first.shape[1] // 2
    ra, ia = first[:, :half], first[:, half:]
    rb, ib = second[:, :half], second[:, half:]
    return jnp.concatenate([ra * rb + ia * ib, ra * ib - ia * rb], axis=1)


def scaled_spectra(traces_ref, me, each, place, presence_ref, present, forward_ref, weights_ref, spec_ref):
    stations, window = spec_ref.shape[1:]
    events = traces_ref.shape[0] // stations
    pieces = events // each
    result = jnp.dot(traces_ref[...], forward_ref[...], preferred_element_type=jnp.float32)
    rounded = result.astype(jnp.bfloat16).astype(jnp.float32)
    energy = jnp.sum(jnp.square(rounded) * weights_ref[...], axis=1, keepdims=True) + 1e-06
    gain = jnp.broadcast_to(lax.rsqrt(energy), (events * stations, LANES)).reshape(events, stations, LANES)
    rounded = rounded.reshape(events, stations, window)
    for j in range(pieces):
        shift = ((me ^ j) & (pieces - 1)) * each
        piece = slice(j * each, (j + 1) * each)
        scale = gain[piece] * presence_ref[pl.ds(present + shift, each)]
        scale = jnp.concatenate([scale] * (window // LANES), axis=2)
        spec_ref[pl.ds(place + shift, each)] = rounded[piece] * scale


def build(lhs_ref, low, pairs, first_of, second_of):
    for i in range(0, len(pairs), 2):
        both = [cross_spectra(first_of(x), second_of(y)) for x, y in pairs[i:i + 2]]
        rows = 2 * both[0].shape[0]
        lhs_ref[pl.ds((low + i) * rows // 2, rows), :] = jnp.concatenate(both, axis=0).astype(jnp.bfloat16)


def keep(table_ref, peaks, values, row):
    stations, lags = table_ref.shape[1:]
    lane = lax.broadcasted_iota(jnp.int32, (stations, LANES), 1)
    count = values.shape[0] // stations
    for i in range(count):
        top = jnp.max(values[i * stations:(i + 1) * stations], axis=1, keepdims=True)
        at, within = divmod(row + i, LANES)
        peaks[at] = jnp.where(lane == within, top, peaks[at])
    table_ref[pl.ds(row, count)] = values.reshape(count, stations, lags).astype(jnp.bfloat16)


def no_peaks(rows, stations):
    return [jnp.zeros((stations, LANES), jnp.float32) for _ in range(rows.lanes // LANES)]


def prepare_kernel(
    each, block, events_ref, valid_ref, presence_ref, forward_ref, inverse_ref,
    row_ref, count_ref, held_ref, forward_out, inverse_out, events_in, valid_in, presence_in, sems,
):
    copies = [
        pltpu.make_async_copy(events_ref, events_in, sems.at[0]),
        pltpu.make_async_copy(valid_ref, valid_in, sems.at[1]),
        pltpu.make_async_copy(presence_ref, presence_in, sems.at[2]),
        pltpu.make_async_copy(forward_ref, forward_out, sems.at[3]),
        pltpu.make_async_copy(inverse_ref, inverse_out, sems.at[4]),
    ]
    for copy in copies:
        copy.start()
    me, start = lax.axis_index("sta"), lax.axis_index("evt") * block
    for copy in copies[:3]:
        copy.wait()
    lines = row_ref.shape[0]

    def stacked(ref, line):
        return jnp.concatenate([ref[line:line + 1, i * LANES:(i + 1) * LANES] for i in range(lines)], axis=0)

    first, second, valid = stacked(events_in, 0), stacked(events_in, 1), stacked(valid_in, 0)
    rows = Rows(block)
    row = table_row(first - start, second - start, me, each, block, rows)
    row = jnp.where(valid > 0, row, rows.zero)
    row_ref[...] = jnp.clip(row, 0, rows.end - 1)

    presence = presence_in[...]
    stations, events = presence.shape
    bits = jnp.zeros((1, events), jnp.int32)
    for s in range(stations):
        bits = bits + presence[s:s + 1] * (1 << s)
    bits = jnp.broadcast_to(bits, (lines, events))
    both = jnp.take_along_axis(bits, first, axis=1) & jnp.take_along_axis(bits, second, axis=1)
    count = jnp.zeros_like(both)
    for s in range(stations):
        count = count + (lax.shift_right_logical(both, s) & 1)
    count_ref[...] = (count * valid).astype(jnp.float32)

    lane = lax.broadcasted_iota(jnp.int32, presence.shape, 1)
    present = presence.astype(jnp.float32)
    for i in range(held_ref.shape[0]):
        mine = jnp.where(lane == start - block // 2 + i, present, 0.0)
        held_ref[i] = jnp.broadcast_to(jnp.sum(mine, axis=1, keepdims=True), (stations, LANES))
    for copy in copies[3:]:
        copy.wait()


def own_pairs(spec_ref, inverse_ref, table_ref, peaks, lhs_ref):
    block, stations, window = spec_ref.shape
    half = window // 2
    pairs = own_list(block)
    chunk = 64
    for low in range(0, len(pairs), chunk):
        some = pairs[low:low + chunk]
        held = {x: spec_ref[x] for x, _ in some}
        build(lhs_ref, low, some, lambda x: held[x], lambda y: spec_ref[y])
        rows = pl.ds(low * stations, len(some) * stations)
        even = jnp.dot(lhs_ref[rows, :half], inverse_ref[:half], preferred_element_type=jnp.float32)
        odd = jnp.dot(lhs_ref[rows, half:], inverse_ref[half:], preferred_element_type=jnp.float32)
        keep(table_ref, peaks, even + odd, low)
        keep(table_ref, peaks, even - odd, len(pairs) + low)


def halo_pairs(high, own_ref, spec_ref, inverse_ref, table_ref, peaks, lhs_ref, row):
    band, stations = spec_ref.shape[:2]

    def own(u):
        return own_ref[jnp.where(high, band + u, band - 1 - u)]

    def other(h):
        return spec_ref[jnp.where(high, h, band - 1 - h)]

    pairs = [(u, h) for u in range(band) for h in range(u + 1)]
    chunk = 68
    for low in range(0, len(pairs), chunk):
        some = pairs[low:low + chunk]
        held = {u: own(u) for u, _ in some}
        build(lhs_ref, low, some, lambda u: held[u], other)
        rows = pl.ds(low * stations, len(some) * stations)
        lagged = jnp.dot(lhs_ref[rows, :], inverse_ref[...], preferred_element_type=jnp.float32)
        keep(table_ref, peaks, lagged, row + low)


def own_kernel(
    each, near_ref, far_ref, presence_ref, forward_ref, inverse_ref, weights_ref,
    spec_ref, table_ref, peak_ref, lhs_ref,
):
    block, stations, window = spec_ref.shape
    band = block // 2
    me = lax.axis_index("sta")
    mine = jnp.where(me * each < band, 0, band)
    for ref, place in ((near_ref, mine), (far_ref, band - mine)):
        scaled_spectra(
            ref, me, each, place, presence_ref, band + place, forward_ref, weights_ref, spec_ref
        )
    rows = Rows(block)
    peaks = no_peaks(rows, stations)
    own_pairs(spec_ref, inverse_ref, table_ref, peaks, lhs_ref)
    table_ref[rows.zero] = jnp.zeros(table_ref.shape[1:], table_ref.dtype)
    peak_ref[...] = jnp.concatenate(peaks, axis=1)


def near_kernel(
    each, halo_ref, own_ref, presence_ref, forward_ref, inverse_ref, weights_ref, own_peak_ref,
    held_table_ref, table_ref, peak_ref, other_ref, lhs_ref,
):
    del held_table_ref
    block, stations, window = own_ref.shape
    band = block // 2
    me = lax.axis_index("sta")
    high = me * each < band
    edge = jnp.where(high, 3 * band, 0)
    scaled_spectra(halo_ref, me, each, 0, presence_ref, edge, forward_ref, weights_ref, other_ref)
    rows = Rows(block)
    peaks = no_peaks(rows, stations)
    halo_pairs(high, own_ref, other_ref, inverse_ref, table_ref, peaks, lhs_ref, rows.near)
    peak_ref[...] = own_peak_ref[...] + jnp.concatenate(peaks, axis=1)


def last_kernel(
    each, halo_ref, own_ref, presence_ref, forward_ref, inverse_ref, weights_ref, peak_ref, row_ref, count_ref,
    held_table_ref, table_ref, sums_ref, other_ref, lhs_ref,
):
    del held_table_ref
    block, stations, window = own_ref.shape
    band = block // 2
    me = lax.axis_index("sta")
    high = me * each >= band
    edge = jnp.where(high, 3 * band, 0)
    scaled_spectra(halo_ref, me, each, 0, presence_ref, edge, forward_ref, weights_ref, other_ref)
    rows = Rows(block)
    peaks = no_peaks(rows, stations)
    halo_pairs(high, own_ref, other_ref, inverse_ref, table_ref, peaks, lhs_ref, rows.far)
    row = row_ref[...]
    lanes = row & (LANES - 1)
    total = jnp.zeros(row.shape, jnp.float32)
    for at, late in enumerate(peaks):
        line = jnp.sum(peak_ref[:, at * LANES:(at + 1) * LANES] + late, axis=0, keepdims=True)
        picked = jnp.take_along_axis(jnp.broadcast_to(line, row.shape), lanes, axis=1)
        total = jnp.where(lax.shift_right_logical(row, 7) == at, picked, total)
    sums_ref[0] = total
    sums_ref[1] = count_ref[...]


def pick_kernel(group, skip, row_ref, table_ref, *refs):
    out_ref = refs[-1]
    base = (pl.program_id(0) + skip) * group
    for j in range(group):
        out_ref[j] = table_ref[row_ref[base + j]]


VMEM = pl.BlockSpec(memory_space=pltpu.VMEM)
SMEM = pl.BlockSpec(memory_space=pltpu.SMEM)
PARAMS = pltpu.CompilerParams(vmem_limit_bytes=20 * 1024 * 1024)


def cost(rows, lags, window, traces, moved):
    return pl.CostEstimate(
        flops=2 * window * (rows * lags + traces * window), bytes_accessed=moved, transcendentals=0
    )


def prepare_call(pair_events, pair_valid, presence, tables, each, block):
    forward, inverse = tables[:2]
    pairs = pair_events.shape[0]
    stations = presence.shape[1]
    line = (pairs // LANES, LANES)
    anywhere = pl.BlockSpec(memory_space=pltpu.HBM)
    return pl.pallas_call(
        functools.partial(prepare_kernel, each, block),
        out_shape=(
            jax.ShapeDtypeStruct(line, jnp.int32),
            jax.ShapeDtypeStruct(line, jnp.float32),
            jax.ShapeDtypeStruct((2 * block, stations, LANES), jnp.float32),
            jax.ShapeDtypeStruct(forward.shape, forward.dtype),
            jax.ShapeDtypeStruct(inverse.shape, inverse.dtype),
        ),
        in_specs=[anywhere] * 5,
        out_specs=(VMEM,) * 5,
        scratch_shapes=[
            pltpu.VMEM((2, pairs), jnp.int32),
            pltpu.VMEM((1, pairs), jnp.int32),
            pltpu.VMEM(presence.shape[::-1], jnp.int32),
            pltpu.SemaphoreType.DMA((5,)),
        ],
        compiler_params=PARAMS,
        cost_estimate=pl.CostEstimate(flops=1_000_000, bytes_accessed=5_000_000, transcendentals=0),
    )(pair_events.T, pair_valid.reshape(1, pairs), presence.T, forward, inverse)


def own_call(near, far, presence, tables, each, block):
    forward, inverse, weights = tables
    window, lags = inverse.shape
    stations = presence.shape[1]
    rows = Rows(block)
    return pl.pallas_call(
        functools.partial(own_kernel, each),
        out_shape=(
            jax.ShapeDtypeStruct((block, stations, window), jnp.float32),
            jax.ShapeDtypeStruct((rows.end, stations, lags), jnp.bfloat16),
            jax.ShapeDtypeStruct((stations, rows.lanes), jnp.float32),
        ),
        in_specs=[VMEM] * 6,
        out_specs=(VMEM,) * 3,
        scratch_shapes=[pltpu.VMEM((rows.own * stations, window), jnp.bfloat16)],
        compiler_params=PARAMS,
        cost_estimate=cost(rows.own * stations, lags, window, near.shape[0] * 2, 8_000_000),
    )(near, far, presence, forward, inverse, weights)


def near_call(halo, own, presence, tables, peaks, table, each):
    forward, inverse, weights = tables
    window, lags = inverse.shape
    block, stations = own.shape[:2]
    pairs = triangle(block // 2)
    return pl.pallas_call(
        functools.partial(near_kernel, each),
        out_shape=(
            jax.ShapeDtypeStruct(table.shape, table.dtype),
            jax.ShapeDtypeStruct(peaks.shape, peaks.dtype),
        ),
        in_specs=[VMEM] * 8,
        out_specs=(VMEM,) * 2,
        scratch_shapes=[
            pltpu.VMEM((block // 2, stations, window), jnp.float32),
            pltpu.VMEM((pairs * stations, window), jnp.bfloat16),
        ],
        input_output_aliases={7: 0},
        compiler_params=PARAMS,
        cost_estimate=cost(pairs * stations, lags, window, halo.shape[0], 4_000_000),
    )(halo, own, presence, forward, inverse, weights, peaks, table)


def last_call(halo, own, presence, tables, peaks, row, count, table, each):
    forward, inverse, weights = tables
    window, lags = inverse.shape
    block, stations = own.shape[:2]
    pairs = triangle(block // 2)
    return pl.pallas_call(
        functools.partial(last_kernel, each),
        out_shape=(
            jax.ShapeDtypeStruct(table.shape, table.dtype),
            jax.ShapeDtypeStruct((2,) + row.shape, jnp.float32),
        ),
        in_specs=[VMEM] * 10,
        out_specs=(VMEM,) * 2,
        scratch_shapes=[
            pltpu.VMEM((block // 2, stations, window), jnp.float32),
            pltpu.VMEM((pairs * stations, window), jnp.bfloat16),
        ],
        input_output_aliases={9: 0},
        compiler_params=PARAMS,
        cost_estimate=cost(pairs * stations, lags, window, halo.shape[0], 4_000_000),
    )(halo, own, presence, forward, inverse, weights, peaks, row, count, table)


def pick_call(row, table, held, skip, steps):
    pairs = row.shape[0]
    block = (LANES,) + table.shape[1:]
    return pl.pallas_call(
        functools.partial(pick_kernel, LANES, skip),
        grid=(steps,),
        out_shape=jax.ShapeDtypeStruct((pairs,) + table.shape[1:], table.dtype),
        in_specs=[SMEM, VMEM] + [pl.BlockSpec(memory_space=pl.ANY)] * len(held),
        out_specs=pl.BlockSpec(block, lambda i: (i + skip, 0, 0)),
        input_output_aliases={2: 0} if held else {},
        compiler_params=PARAMS,
        cost_estimate=pl.CostEstimate(flops=1_000_000, bytes_accessed=3_000_000 * steps, transcendentals=0),
    )(row, table, *held)


def table_row(first, second, me, each, block, rows):
    band = block // 2
    low, apart = jnp.minimum(first, second), jnp.abs(first - second)
    past = jnp.maximum(low - band, 0)
    index = jnp.minimum(low, band) * band + past * (band - 1) - (past * (past - 1) >> 1) + apart - 1
    inside = jnp.where(second > first, index, rows.own + index)
    high = second >= block
    u = jnp.where(high, first - band, band - 1 - first)
    h = jnp.where(high, second - block, -1 - second)
    near = jnp.where(high, 1, 0) == jnp.where(me * each < band, 1, 0)
    outside = jnp.where(near, rows.near, rows.far) + (u * (u + 1) >> 1) + h
    return jnp.where(high | (second < 0), outside, inside)


def banded(waveforms, pair_events, pair_valid, presence, block, tables):
    each = waveforms.shape[0]
    near, far, toward, away = exchange(waveforms, lax.axis_size("sta"))
    ready = prepare_call(pair_events, pair_valid, presence, tables, each, block)
    far, ready = lax.optimization_barrier((far, ready))
    near_halo = lax.ppermute(near, ("sta", "evt"), toward)
    far_halo = lax.ppermute(far, ("sta", "evt"), away)
    row, count, held, forward, inverse = ready
    tables = (forward, inverse, tables[2])
    own, table, peaks = own_call(near, far, held, tables, each, block)
    table, peaks = near_call(near_halo, own, held, tables, peaks, table, each)
    table, sums = last_call(far_halo, own, held, tables, peaks, row, count, table, each)

    row = row.reshape(-1)
    groups = row.shape[0] // LANES
    correlation = ()
    step, skip = lax.axis_size("sta") // 2, 0
    while step:
        arrived = lax.ppermute(sums, "sta", [(i, i ^ step) for i in range(lax.axis_size("sta"))])
        steps = -(-(groups - skip) // step.bit_length())
        correlation = (pick_call(row, table, correlation, skip, steps),)
        sums, correlation = lax.optimization_barrier((sums + arrived, correlation))
        skip += steps
        step //= 2
    return correlation[0], sums


def by_slot(waveforms, pair_events, pair_valid, presence, block, tables):
    share = presence.shape[1]
    start = lax.axis_index("evt") * block
    traces = exchange_whole(waveforms)
    place = pair_events - start
    slot = jnp.where((place >= 0) & (place < block), 0, block) + place % block
    gained = jnp.where(pair_valid > 0, slot[:, 0], 2 * block)
    slots = jnp.stack([slot[:, 0], slot[:, 1], gained]).astype(jnp.int32)
    held = jnp.arange(2 * block, dtype=jnp.int32)
    held = jnp.where(held < block, held, jnp.where(held < block + block // 2, held, held - 2 * block))
    held = jnp.clip(start + held, 0, presence.shape[0] - 1)
    slot_presence = jnp.broadcast_to(
        jnp.take(presence.astype(jnp.float32), held, axis=0)[:, :, None], (2 * block, share, LANES)
    )
    few = presence.astype(jnp.bfloat16)
    event = jnp.arange(presence.shape[0], dtype=jnp.int32)
    first, second = (
        jnp.dot((pair_events[:, i:i + 1] == event).astype(jnp.bfloat16), few, preferred_element_type=jnp.float32)
        for i in (0, 1)
    )
    counts = jnp.sum(first * second, axis=1) * pair_valid.astype(jnp.float32)
    correlation, peaks = pair_call(slots, traces, slot_presence, tables)
    sums = lax.psum(jnp.stack([peaks.reshape(-1), counts]), "sta")
    return correlation.reshape(-1, share, correlation.shape[1]), sums


def body(waveforms, pair_events, pair_valid, presence):
    sta_count = lax.axis_size("sta")
    local_events, stations, window = waveforms.shape
    block = sta_count * local_events
    tables = spectral_tables(window, LAGS)
    args = (waveforms, pair_events, pair_valid, presence, block, tables)
    dense = sta_count == 8 and presence.shape[0] == LANES and block * block <= pair_events.shape[0]
    correlation, sums = (banded if dense else by_slot)(*args)
    pair_peak = sums[0] / jnp.maximum(sums[1], 1.0)
    return correlation, pair_peak.reshape(-1)


def solution(mesh):
    return jax.shard_map(
        body,
        mesh=mesh,
        in_specs=(P(("evt", "sta"), None, None), P("evt", None), P("evt"), P(None, "sta")),
        out_specs=(P("evt", "sta", None), P("evt")),
        check_vma=False,
    )
```

```python
import functools
import math

import jax
import jax.numpy as jnp
import numpy as np
from jax import lax
from jax.experimental import pallas as pl
from jax.experimental.pallas import tpu as pltpu
from jax.sharding import PartitionSpec as P

LAGS = 256
LANES = 128


def spectral_tables(window, lag_count):
    half = window // 2
    sample = np.arange(window, dtype=np.int64)
    bins = np.arange(half, dtype=np.int64)
    angle = (sample[:, None] * bins[None, :] % window) * (2.0 * math.pi / window)
    forward = np.concatenate([np.cos(angle), -np.sin(angle)], axis=1) / math.sqrt(window)
    shifts = np.arange(lag_count, dtype=np.int64) - lag_count // 2
    lag_angle = (bins[:, None] * shifts[None, :] % window) * (2.0 * math.pi / window)
    factor = np.where(bins == 0, 1.0, 2.0)[:, None]
    inverse = np.concatenate([factor * np.cos(lag_angle), -factor * np.sin(lag_angle)], axis=0)
    weights = np.concatenate([factor[:, 0], factor[:, 0]])[None, :]
    return forward.astype(jnp.bfloat16), inverse.astype(jnp.bfloat16), weights.astype(np.float32)


def pair_kernel(
    group, chunk, parts, slots_ref, *refs
):
    traces = refs[:parts]
    (
        presence_ref, forward_ref, inverse_ref, weights_ref,
        out_ref, peak_ref,
        spec_ref, gain_ref, lhs_ref,
    ) = refs[parts:]
    stations, window = spec_ref.shape[1:]
    half = window // 2
    events = spec_ref.shape[0]

    @pl.when(pl.program_id(0) == 0)
    def _():
        start = 0
        for ref in traces:
            rows = ref.shape[0]
            count = rows // stations
            result = jnp.dot(ref[...], forward_ref[...], preferred_element_type=jnp.float32)
            rounded = result.astype(jnp.bfloat16).astype(jnp.float32)
            spec_ref[pl.ds(start, count)] = rounded.reshape(count, stations, window)
            power = jnp.square(rounded) * weights_ref[...]
            energy = jnp.sum(power, axis=1, keepdims=True) + 1e-06
            gain = jnp.broadcast_to(lax.rsqrt(energy), (rows, LANES))
            gain = gain.reshape(count, stations, LANES) * presence_ref[pl.ds(start, count)]
            gain_ref[pl.ds(start, count)] = gain
            start += count
        gain_ref[events] = jnp.zeros((stations, LANES), jnp.float32)

    base = pl.program_id(0) * group
    lane = lax.broadcasted_iota(jnp.int32, (stations, LANES), 1)

    def cross(pair):
        first = spec_ref[slots_ref[0, pair]]
        second = spec_ref[slots_ref[1, pair]]
        ra, ia = first[:, :half], first[:, half:]
        rb, ib = second[:, :half], second[:, half:]
        return jnp.concatenate([ra * rb + ia * ib, ra * ib - ia * rb], axis=1)

    def one_chunk(index, peaks):
        first_pair = base + index * chunk
        for j in range(0, chunk, 2):
            both = jnp.concatenate([cross(first_pair + j), cross(first_pair + j + 1)], axis=0)
            lhs_ref[pl.ds(j * stations, 2 * stations), :] = both.astype(jnp.bfloat16)
        lagged = jnp.dot(lhs_ref[...], inverse_ref[...], preferred_element_type=jnp.float32)
        for j in range(0, chunk, 2):
            rows = []
            for i in (j, j + 1):
                pair = first_pair + i
                gain = gain_ref[slots_ref[2, pair]] * gain_ref[slots_ref[1, pair]]
                scaled = lagged[i * stations:(i + 1) * stations] * jnp.concatenate([gain, gain], axis=1)
                rows.append(scaled)
                top = jnp.max(scaled, axis=1, keepdims=True)
                peaks = jnp.where(lane == index * chunk + i, top, peaks)
            block = jnp.concatenate(rows, axis=0).astype(jnp.bfloat16)
            start = pl.multiple_of(index * chunk * stations, chunk * stations) + j * stations
            out_ref[pl.ds(start, 2 * stations), :] = block
        return peaks

    peaks = lax.fori_loop(0, group // chunk, one_chunk, jnp.zeros((stations, LANES), jnp.float32))
    peak_ref[0] = jnp.sum(peaks, axis=0, keepdims=True)


def pair_call(slots, traces, presence, tables):
    forward, inverse, weights = tables
    window = forward.shape[0]
    lags = inverse.shape[1]
    pairs = slots.shape[1]
    events, stations = presence.shape[:2]
    group = LANES
    chunk = 32
    vmem = pl.BlockSpec(memory_space=pltpu.VMEM)
    return pl.pallas_call(
        functools.partial(pair_kernel, group, chunk, len(traces)),
        grid=(pairs // group,),
        out_shape=(
            jax.ShapeDtypeStruct((pairs * stations, lags), jnp.bfloat16),
            jax.ShapeDtypeStruct((pairs // group, 1, group), jnp.float32),
        ),
        in_specs=[pl.BlockSpec(memory_space=pltpu.SMEM)] + [vmem] * (len(traces) + 4),
        out_specs=(
            pl.BlockSpec((group * stations, lags), lambda i: (i, 0)),
            pl.BlockSpec((1, 1, group), lambda i: (i, 0, 0)),
        ),
        scratch_shapes=[
            pltpu.VMEM((events, stations, window), jnp.float32),
            pltpu.VMEM((events + 1, stations, LANES), jnp.float32),
            pltpu.VMEM((chunk * stations, window), jnp.bfloat16),
        ],
        compiler_params=pltpu.CompilerParams(vmem_limit_bytes=56 * 1024 * 1024),
        cost_estimate=pl.CostEstimate(flops=4_500_000_000, bytes_accessed=8_000_000, transcendentals=0),
    )(slots, *traces, presence, forward, inverse, weights)


def exchange(waveforms, sta_count, tables):
    events, stations, window = waveforms.shape
    share = stations // sta_count
    blocks = waveforms.reshape(events, sta_count, share, window)
    me = lax.axis_index("sta")
    half = sta_count // 2
    evt_count = lax.axis_size("evt")
    toward, away = [], []
    for e in range(evt_count):
        for s in range(sta_count):
            step = -1 if s < half else 1
            for pairs, target in ((toward, e + step), (away, e - step)):
                if 0 <= target < evt_count:
                    pairs.append((s * evt_count + e, s * evt_count + target))
    def for_station(i):
        return lax.dynamic_index_in_dim(blocks, i, axis=1, keepdims=False)

    def swap(piece, j):
        return lax.ppermute(piece, "sta", [(i, i ^ j) for i in range(sta_count)])

    later = [swap(for_station(me ^ j), j) for j in range(half, sta_count)]
    across = swap(jnp.stack([for_station(me ^ 2), for_station(me ^ 3)]), 2)
    beside = swap(jnp.concatenate([for_station(me ^ 1), across[1]], axis=0), 1)
    later[3], tables = lax.optimization_barrier((later[3], tables))
    tables = bring_call(tables)
    pieces = [for_station(me), beside[:events], across[0], beside[events:]] + later
    rows = half * events * share
    near = jnp.concatenate(pieces[:half], axis=0).reshape(rows, window)
    far = jnp.concatenate(pieces[half:], axis=0).reshape(rows, window)
    return near, far, toward, away, tables


def exchange_whole(waveforms):
    window = waveforms.shape[2]
    arrived = lax.all_to_all(waveforms, "sta", split_axis=1, concat_axis=0, tiled=True)
    arrived = arrived.reshape(-1, window)
    half = arrived.shape[0] // 2
    count = lax.axis_size("evt")
    down = [(i, i - 1) for i in range(1, count)]
    up = [(i, i + 1) for i in range(count - 1)]
    next_low = lax.ppermute(arrived[:half], "evt", down)
    last_high = lax.ppermute(arrived[half:], "evt", up)
    return arrived, next_low, last_high


def triangle(count):
    return count * (count + 1) // 2


def own_list(block):
    band = block // 2
    return [(x, y) for x in range(block) for y in range(x + 1, min(x + band, block - 1) + 1)]


class Rows:
    def __init__(self, block):
        self.own = len(own_list(block))
        self.zero = 2 * self.own
        self.near = self.zero + 8
        self.far = self.near + triangle(block // 2)
        self.end = self.far + triangle(block // 2)
        self.lanes = -(-self.end // LANES) * LANES


def cross_spectra(first, second):
    half = first.shape[1] // 2
    ra, ia = first[:, :half], first[:, half:]
    rb, ib = second[:, :half], second[:, half:]
    return jnp.concatenate([ra * rb + ia * ib, ra * ib - ia * rb], axis=1)


def scaled_spectra(traces_ref, me, each, place, presence_ref, present, tables_ref, weights_ref, spec_ref):
    stations, window = spec_ref.shape[1:]
    events = traces_ref.shape[0] // stations
    pieces = events // each
    result = jnp.dot(traces_ref[...], tables_ref[:, :window], preferred_element_type=jnp.float32)
    rounded = result.astype(jnp.bfloat16).astype(jnp.float32)
    energy = jnp.sum(jnp.square(rounded) * weights_ref[...], axis=1, keepdims=True) + 1e-06
    gain = jnp.broadcast_to(lax.rsqrt(energy), (events * stations, LANES)).reshape(events, stations, LANES)
    rounded = rounded.reshape(events, stations, window)
    for j in range(pieces):
        shift = ((me ^ j) & (pieces - 1)) * each
        piece = slice(j * each, (j + 1) * each)
        scale = gain[piece] * presence_ref[pl.ds(present + shift, each)]
        scale = jnp.concatenate([scale] * (window // LANES), axis=2)
        spec_ref[pl.ds(place + shift, each)] = rounded[piece] * scale


def build(lhs_ref, low, pairs, first_of, second_of):
    for i in range(0, len(pairs), 2):
        both = [cross_spectra(first_of(x), second_of(y)) for x, y in pairs[i:i + 2]]
        rows = 2 * both[0].shape[0]
        lhs_ref[pl.ds((low + i) * rows // 2, rows), :] = jnp.concatenate(both, axis=0).astype(jnp.bfloat16)


def keep(table_ref, peaks, values, row):
    stations, lags = table_ref.shape[1:]
    lane = lax.broadcasted_iota(jnp.int32, (stations, LANES), 1)
    count = values.shape[0] // stations
    for i in range(count):
        top = jnp.max(values[i * stations:(i + 1) * stations], axis=1, keepdims=True)
        at, within = divmod(row + i, LANES)
        peaks[at] = jnp.where(lane == within, top, peaks[at])
    table_ref[pl.ds(row, count)] = values.reshape(count, stations, lags).astype(jnp.bfloat16)


def no_peaks(rows, stations):
    return [jnp.zeros((stations, LANES), jnp.float32) for _ in range(rows.lanes // LANES)]


def prepare_kernel(
    each, block, packed_ref, row_ref, count_ref, held_ref,
):
    me, start = lax.axis_index("sta"), lax.axis_index("evt") * block
    lines = row_ref.shape[0]

    def stacked(line):
        return jnp.concatenate(
            [packed_ref[line:line + 1, i * LANES:(i + 1) * LANES] for i in range(lines)], axis=0
        )

    first, second, valid = stacked(0), stacked(1), stacked(2)
    rows = Rows(block)
    row = table_row(first - start, second - start, me, each, block, rows)
    row = jnp.where(valid > 0, row, rows.zero)
    row_ref[...] = jnp.clip(row, 0, rows.end - 1)

    presence = packed_ref[3:, :LANES]
    stations, events = presence.shape
    bits = jnp.zeros((1, events), jnp.int32)
    for s in range(stations):
        bits = bits + presence[s:s + 1] * (1 << s)
    bits = jnp.broadcast_to(bits, (lines, events))
    both = jnp.take_along_axis(bits, first, axis=1) & jnp.take_along_axis(bits, second, axis=1)
    count = jnp.zeros_like(both)
    for s in range(stations):
        count = count + (lax.shift_right_logical(both, s) & 1)
    count_ref[...] = (count * valid).astype(jnp.float32)

    lane = lax.broadcasted_iota(jnp.int32, presence.shape, 1)
    present = presence.astype(jnp.float32)
    for i in range(held_ref.shape[0]):
        mine = jnp.where(lane == start - block // 2 + i, present, 0.0)
        held_ref[i] = jnp.broadcast_to(jnp.sum(mine, axis=1, keepdims=True), (stations, LANES))


def bring_kernel(tables_ref, tables_out, sem):
    copy = pltpu.make_async_copy(tables_ref, tables_out, sem)
    copy.start()
    copy.wait()


def own_pairs(spec_ref, tables_ref, table_ref, peaks, lhs_ref):
    block, stations, window = spec_ref.shape
    half = window // 2
    pairs = own_list(block)
    chunk = 64
    for low in range(0, len(pairs), chunk):
        some = pairs[low:low + chunk]
        held = {x: spec_ref[x] for x, _ in some}
        build(lhs_ref, low, some, lambda x: held[x], lambda y: spec_ref[y])
        rows = pl.ds(low * stations, len(some) * stations)
        even = jnp.dot(lhs_ref[rows, :half], tables_ref[:half, window:], preferred_element_type=jnp.float32)
        odd = jnp.dot(lhs_ref[rows, half:], tables_ref[half:, window:], preferred_element_type=jnp.float32)
        keep(table_ref, peaks, even + odd, low)
        keep(table_ref, peaks, even - odd, len(pairs) + low)


def halo_pairs(high, own_ref, spec_ref, tables_ref, table_ref, peaks, lhs_ref, row):
    band, stations, window = spec_ref.shape

    def own(u):
        return own_ref[jnp.where(high, band + u, band - 1 - u)]

    def other(h):
        return spec_ref[jnp.where(high, h, band - 1 - h)]

    pairs = [(u, h) for u in range(band) for h in range(u + 1)]
    chunk = 68
    for low in range(0, len(pairs), chunk):
        some = pairs[low:low + chunk]
        held = {u: own(u) for u, _ in some}
        build(lhs_ref, low, some, lambda u: held[u], other)
        rows = pl.ds(low * stations, len(some) * stations)
        lagged = jnp.dot(lhs_ref[rows, :], tables_ref[:, window:], preferred_element_type=jnp.float32)
        keep(table_ref, peaks, lagged, row + low)


def own_kernel(
    each, near_ref, far_ref, presence_ref, tables_ref, weights_ref,
    spec_ref, table_ref, peak_ref, lhs_ref,
):
    block, stations, window = spec_ref.shape
    band = block // 2
    me = lax.axis_index("sta")
    mine = jnp.where(me * each < band, 0, band)
    for ref, place in ((near_ref, mine), (far_ref, band - mine)):
        scaled_spectra(
            ref, me, each, place, presence_ref, band + place, tables_ref, weights_ref, spec_ref
        )
    rows = Rows(block)
    peaks = no_peaks(rows, stations)
    own_pairs(spec_ref, tables_ref, table_ref, peaks, lhs_ref)
    table_ref[rows.zero] = jnp.zeros(table_ref.shape[1:], table_ref.dtype)
    peak_ref[...] = jnp.concatenate(peaks, axis=1)


def middle_kernel(
    each, halo_ref, own_ref, presence_ref, tables_ref, weights_ref, own_peak_ref,
    held_table_ref, table_ref, peak_ref, other_ref, lhs_ref,
):
    del held_table_ref
    block, stations, window = own_ref.shape
    band = block // 2
    me = lax.axis_index("sta")
    high = me * each < band
    edge = jnp.where(high, 3 * band, 0)
    scaled_spectra(halo_ref, me, each, 0, presence_ref, edge, tables_ref, weights_ref, other_ref)
    rows = Rows(block)
    peaks = no_peaks(rows, stations)
    halo_pairs(high, own_ref, other_ref, tables_ref, table_ref, peaks, lhs_ref, rows.near)
    peak_ref[...] = own_peak_ref[...] + jnp.concatenate(peaks, axis=1)


def last_kernel(
    each, halo_ref, own_ref, presence_ref, tables_ref, weights_ref, peak_ref, row_ref, count_ref,
    held_table_ref, table_ref, sums_ref, other_ref, lhs_ref,
):
    del held_table_ref
    block, stations, window = own_ref.shape
    band = block // 2
    me = lax.axis_index("sta")
    high = me * each >= band
    edge = jnp.where(high, 3 * band, 0)
    scaled_spectra(halo_ref, me, each, 0, presence_ref, edge, tables_ref, weights_ref, other_ref)
    rows = Rows(block)
    peaks = no_peaks(rows, stations)
    halo_pairs(high, own_ref, other_ref, tables_ref, table_ref, peaks, lhs_ref, rows.far)
    row = row_ref[...]
    lanes = row & (LANES - 1)
    total = jnp.zeros(row.shape, jnp.float32)
    for at, late in enumerate(peaks):
        line = jnp.sum(peak_ref[:, at * LANES:(at + 1) * LANES] + late, axis=0, keepdims=True)
        picked = jnp.take_along_axis(jnp.broadcast_to(line, row.shape), lanes, axis=1)
        total = jnp.where(lax.shift_right_logical(row, 7) == at, picked, total)
    sums_ref[0] = total
    sums_ref[1] = count_ref[...]


def pick_kernel(start, group, row_ref, table_ref, *refs):
    out_ref, picked_ref, sems = refs[-3:]
    copies = []
    for low in range(0, picked_ref.shape[0], group):
        for i in range(low, low + group):
            picked_ref[i] = table_ref[row_ref[start + i]]
        copies.append(pltpu.make_async_copy(
            picked_ref.at[pl.ds(low, group)], out_ref.at[pl.ds(start + low, group)], sems.at[low // group]
        ))
        copies[-1].start()
    for copy in copies:
        copy.wait()


VMEM = pl.BlockSpec(memory_space=pltpu.VMEM)
SMEM = pl.BlockSpec(memory_space=pltpu.SMEM)
PARAMS = pltpu.CompilerParams(vmem_limit_bytes=20 * 1024 * 1024)


def cost(rows, lags, window, traces, moved):
    return pl.CostEstimate(
        flops=2 * window * (rows * lags + traces * window), bytes_accessed=moved, transcendentals=0
    )


def prepare_call(pair_events, pair_valid, presence, each, block):
    pairs = pair_events.shape[0]
    events, stations = presence.shape
    packed = jnp.concatenate(
        [pair_events.T, pair_valid[None], jnp.pad(presence.T, ((0, 0), (0, pairs - events)))], axis=0
    )
    line = (pairs // LANES, LANES)
    return pl.pallas_call(
        functools.partial(prepare_kernel, each, block),
        out_shape=(
            jax.ShapeDtypeStruct(line, jnp.int32),
            jax.ShapeDtypeStruct(line, jnp.float32),
            jax.ShapeDtypeStruct((2 * block, stations, LANES), jnp.float32),
        ),
        in_specs=[VMEM],
        out_specs=(VMEM,) * 3,
        compiler_params=PARAMS,
        cost_estimate=pl.CostEstimate(flops=1_000_000, bytes_accessed=1_000_000, transcendentals=0),
    )(packed)


def bring_call(tables):
    return pl.pallas_call(
        bring_kernel,
        out_shape=jax.ShapeDtypeStruct(tables.shape, tables.dtype),
        in_specs=[pl.BlockSpec(memory_space=pl.ANY)],
        out_specs=VMEM,
        scratch_shapes=[pltpu.SemaphoreType.DMA],
        compiler_params=PARAMS,
        cost_estimate=pl.CostEstimate(flops=0, bytes_accessed=5_000_000, transcendentals=0),
    )(tables)


def own_call(near, far, presence, tables, each, block):
    table_of, weights = tables
    window = table_of.shape[0]
    lags = table_of.shape[1] - window
    stations = presence.shape[1]
    rows = Rows(block)
    return pl.pallas_call(
        functools.partial(own_kernel, each),
        out_shape=(
            jax.ShapeDtypeStruct((block, stations, window), jnp.float32),
            jax.ShapeDtypeStruct((rows.end, stations, lags), jnp.bfloat16),
            jax.ShapeDtypeStruct((stations, rows.lanes), jnp.float32),
        ),
        in_specs=[VMEM] * 5,
        out_specs=(VMEM,) * 3,
        scratch_shapes=[pltpu.VMEM((rows.own * stations, window), jnp.bfloat16)],
        compiler_params=PARAMS,
        cost_estimate=cost(rows.own * stations, lags, window, near.shape[0] * 2, 8_000_000),
    )(near, far, presence, table_of, weights)


def middle_call(halo, own, presence, tables, peaks, table, each):
    table_of, weights = tables
    window = table_of.shape[0]
    lags = table_of.shape[1] - window
    block, stations = own.shape[:2]
    pairs = triangle(block // 2)
    return pl.pallas_call(
        functools.partial(middle_kernel, each),
        out_shape=(
            jax.ShapeDtypeStruct(table.shape, table.dtype),
            jax.ShapeDtypeStruct(peaks.shape, peaks.dtype),
        ),
        in_specs=[VMEM] * 7,
        out_specs=(VMEM,) * 2,
        scratch_shapes=[
            pltpu.VMEM((block // 2, stations, window), jnp.float32),
            pltpu.VMEM((pairs * stations, window), jnp.bfloat16),
        ],
        input_output_aliases={6: 0},
        compiler_params=PARAMS,
        cost_estimate=cost(pairs * stations, lags, window, halo.shape[0], 4_000_000),
    )(halo, own, presence, table_of, weights, peaks, table)


def last_call(halo, own, presence, tables, peaks, row, count, table, each):
    table_of, weights = tables
    window = table_of.shape[0]
    lags = table_of.shape[1] - window
    block, stations = own.shape[:2]
    pairs = triangle(block // 2)
    return pl.pallas_call(
        functools.partial(last_kernel, each),
        out_shape=(
            jax.ShapeDtypeStruct(table.shape, table.dtype),
            jax.ShapeDtypeStruct((2,) + row.shape, jnp.float32),
        ),
        in_specs=[VMEM] * 9,
        out_specs=(VMEM,) * 2,
        scratch_shapes=[
            pltpu.VMEM((block // 2, stations, window), jnp.float32),
            pltpu.VMEM((pairs * stations, window), jnp.bfloat16),
        ],
        input_output_aliases={8: 0},
        compiler_params=PARAMS,
        cost_estimate=cost(pairs * stations, lags, window, halo.shape[0], 4_000_000),
    )(halo, own, presence, table_of, weights, peaks, row, count, table)


def pick_call(row, table, held, start, count):
    group = 64
    anywhere = pl.BlockSpec(memory_space=pl.ANY)
    return pl.pallas_call(
        functools.partial(pick_kernel, start, group),
        out_shape=jax.ShapeDtypeStruct(row.shape + table.shape[1:], table.dtype),
        in_specs=[SMEM, VMEM] + [anywhere] * len(held),
        out_specs=anywhere,
        scratch_shapes=[
            pltpu.VMEM((count,) + table.shape[1:], table.dtype),
            pltpu.SemaphoreType.DMA((count // group,)),
        ],
        input_output_aliases={2: 0} if held else {},
        compiler_params=PARAMS,
        cost_estimate=pl.CostEstimate(flops=0, bytes_accessed=count * 20_000, transcendentals=0),
    )(row, table, *held)


def table_row(first, second, me, each, block, rows):
    band = block // 2
    low, apart = jnp.minimum(first, second), jnp.abs(first - second)
    past = jnp.maximum(low - band, 0)
    index = jnp.minimum(low, band) * band + past * (band - 1) - (past * (past - 1) >> 1) + apart - 1
    inside = jnp.where(second > first, index, rows.own + index)
    high = second >= block
    u = jnp.where(high, first - band, band - 1 - first)
    h = jnp.where(high, second - block, -1 - second)
    near = jnp.where(high, 1, 0) == jnp.where(me * each < band, 1, 0)
    outside = jnp.where(near, rows.near, rows.far) + (u * (u + 1) >> 1) + h
    return jnp.where(high | (second < 0), outside, inside)


def banded(waveforms, pair_events, pair_valid, presence, block):
    each = waveforms.shape[0]
    forward, inverse, weights = spectral_tables(waveforms.shape[2], LAGS)
    tables = (jnp.asarray(np.concatenate([forward, inverse], axis=1)), jnp.asarray(weights))
    near, far, toward, away, brought = exchange(waveforms, lax.axis_size("sta"), tables[0])
    ready = prepare_call(pair_events, pair_valid, presence, each, block)
    far, ready, brought = lax.optimization_barrier((far, ready, brought))
    tables = (brought, tables[1])
    near_tied, tables = lax.optimization_barrier((near, tables))
    near_halo = lax.ppermute(near_tied, ("sta", "evt"), toward)
    far_halo = lax.ppermute(far, ("sta", "evt"), away)
    row, count, held = ready
    own, table, peaks = own_call(near, far, held, tables, each, block)
    table, peaks = middle_call(near_halo, own, held, tables, peaks, table, each)
    table, sums = last_call(far_halo, own, held, tables, peaks, row, count, table, each)

    row = row.reshape(-1)
    groups = row.shape[0] // LANES
    correlation = ()
    step, skip = lax.axis_size("sta") // 2, 0
    while step:
        arrived = lax.ppermute(sums, "sta", [(i, i ^ step) for i in range(lax.axis_size("sta"))])
        steps = -(-(groups - skip) // step.bit_length())
        correlation = (pick_call(row, table, correlation, skip * LANES, steps * LANES),)
        sums, correlation = lax.optimization_barrier((sums + arrived, correlation))
        skip += steps
        step //= 2
    return correlation[0], sums


def by_slot(waveforms, pair_events, pair_valid, presence, block):
    share = presence.shape[1]
    start = lax.axis_index("evt") * block
    traces = exchange_whole(waveforms)
    place = pair_events - start
    slot = jnp.where((place >= 0) & (place < block), 0, block) + place % block
    gained = jnp.where(pair_valid > 0, slot[:, 0], 2 * block)
    slots = jnp.stack([slot[:, 0], slot[:, 1], gained]).astype(jnp.int32)
    held = jnp.arange(2 * block, dtype=jnp.int32)
    held = jnp.where(held < block, held, jnp.where(held < block + block // 2, held, held - 2 * block))
    held = jnp.clip(start + held, 0, presence.shape[0] - 1)
    slot_presence = jnp.broadcast_to(
        jnp.take(presence.astype(jnp.float32), held, axis=0)[:, :, None], (2 * block, share, LANES)
    )
    few = presence.astype(jnp.bfloat16)
    event = jnp.arange(presence.shape[0], dtype=jnp.int32)
    first, second = (
        jnp.dot((pair_events[:, i:i + 1] == event).astype(jnp.bfloat16), few, preferred_element_type=jnp.float32)
        for i in (0, 1)
    )
    counts = jnp.sum(first * second, axis=1) * pair_valid.astype(jnp.float32)
    tables = tuple(jnp.asarray(x) for x in spectral_tables(waveforms.shape[2], LAGS))
    correlation, peaks = pair_call(slots, traces, slot_presence, tables)
    sums = lax.psum(jnp.stack([peaks.reshape(-1), counts]), "sta")
    return correlation.reshape(-1, share, correlation.shape[1]), sums


def body(waveforms, pair_events, pair_valid, presence):
    sta_count = lax.axis_size("sta")
    local_events, stations, window = waveforms.shape
    block = sta_count * local_events
    args = (waveforms, pair_events, pair_valid, presence, block)
    dense = sta_count == 8 and presence.shape[0] == LANES and block * block <= pair_events.shape[0]
    correlation, sums = (banded if dense else by_slot)(*args)
    pair_peak = sums[0] / jnp.maximum(sums[1], 1.0)
    return correlation, pair_peak.reshape(-1)


def solution(mesh):
    return jax.shard_map(
        body,
        mesh=mesh,
        in_specs=(P(("evt", "sta"), None, None), P("evt", None), P("evt"), P(None, "sta")),
        out_specs=(P("evt", "sta", None), P("evt")),
        check_vma=False,
    )
```

```python
import functools
import math

import jax
import jax.numpy as jnp
import numpy as np
from jax import lax
from jax.experimental import pallas as pl
from jax.experimental.pallas import tpu as pltpu
from jax.sharding import PartitionSpec as P

LAGS = 256
LANES = 128


def spectral_tables(window, lag_count):
    half = window // 2
    sample = np.arange(window, dtype=np.int64)
    bins = np.arange(half, dtype=np.int64)
    angle = (sample[:, None] * bins[None, :] % window) * (2.0 * math.pi / window)
    forward = np.concatenate([np.cos(angle), -np.sin(angle)], axis=1) / math.sqrt(window)
    shifts = np.arange(lag_count, dtype=np.int64) - lag_count // 2
    lag_angle = (bins[:, None] * shifts[None, :] % window) * (2.0 * math.pi / window)
    factor = np.where(bins == 0, 1.0, 2.0)[:, None]
    inverse = np.concatenate([factor * np.cos(lag_angle), -factor * np.sin(lag_angle)], axis=0)
    weights = np.concatenate([factor[:, 0], factor[:, 0]])[None, :]
    return forward.astype(jnp.bfloat16), inverse.astype(jnp.bfloat16), weights.astype(np.float32)


def pair_kernel(
    group, chunk, parts, slots_ref, *refs
):
    traces = refs[:parts]
    (
        presence_ref, forward_ref, inverse_ref, weights_ref,
        out_ref, peak_ref,
        spec_ref, gain_ref, lhs_ref,
    ) = refs[parts:]
    stations, window = spec_ref.shape[1:]
    half = window // 2
    events = spec_ref.shape[0]

    @pl.when(pl.program_id(0) == 0)
    def _():
        start = 0
        for ref in traces:
            rows = ref.shape[0]
            count = rows // stations
            result = jnp.dot(ref[...], forward_ref[...], preferred_element_type=jnp.float32)
            rounded = result.astype(jnp.bfloat16).astype(jnp.float32)
            spec_ref[pl.ds(start, count)] = rounded.reshape(count, stations, window)
            power = jnp.square(rounded) * weights_ref[...]
            energy = jnp.sum(power, axis=1, keepdims=True) + 1e-06
            gain = jnp.broadcast_to(lax.rsqrt(energy), (rows, LANES))
            gain = gain.reshape(count, stations, LANES) * presence_ref[pl.ds(start, count)]
            gain_ref[pl.ds(start, count)] = gain
            start += count
        gain_ref[events] = jnp.zeros((stations, LANES), jnp.float32)

    base = pl.program_id(0) * group
    lane = lax.broadcasted_iota(jnp.int32, (stations, LANES), 1)

    def cross(pair):
        first = spec_ref[slots_ref[0, pair]]
        second = spec_ref[slots_ref[1, pair]]
        ra, ia = first[:, :half], first[:, half:]
        rb, ib = second[:, :half], second[:, half:]
        return jnp.concatenate([ra * rb + ia * ib, ra * ib - ia * rb], axis=1)

    def one_chunk(index, peaks):
        first_pair = base + index * chunk
        for j in range(0, chunk, 2):
            both = jnp.concatenate([cross(first_pair + j), cross(first_pair + j + 1)], axis=0)
            lhs_ref[pl.ds(j * stations, 2 * stations), :] = both.astype(jnp.bfloat16)
        lagged = jnp.dot(lhs_ref[...], inverse_ref[...], preferred_element_type=jnp.float32)
        for j in range(0, chunk, 2):
            rows = []
            for i in (j, j + 1):
                pair = first_pair + i
                gain = gain_ref[slots_ref[2, pair]] * gain_ref[slots_ref[1, pair]]
                scaled = lagged[i * stations:(i + 1) * stations] * jnp.concatenate([gain, gain], axis=1)
                rows.append(scaled)
                top = jnp.max(scaled, axis=1, keepdims=True)
                peaks = jnp.where(lane == index * chunk + i, top, peaks)
            block = jnp.concatenate(rows, axis=0).astype(jnp.bfloat16)
            start = pl.multiple_of(index * chunk * stations, chunk * stations) + j * stations
            out_ref[pl.ds(start, 2 * stations), :] = block
        return peaks

    peaks = lax.fori_loop(0, group // chunk, one_chunk, jnp.zeros((stations, LANES), jnp.float32))
    peak_ref[0] = jnp.sum(peaks, axis=0, keepdims=True)


def pair_call(slots, traces, presence, tables):
    forward, inverse, weights = tables
    window = forward.shape[0]
    lags = inverse.shape[1]
    pairs = slots.shape[1]
    events, stations = presence.shape[:2]
    group = LANES
    chunk = 32
    vmem = pl.BlockSpec(memory_space=pltpu.VMEM)
    return pl.pallas_call(
        functools.partial(pair_kernel, group, chunk, len(traces)),
        grid=(pairs // group,),
        out_shape=(
            jax.ShapeDtypeStruct((pairs * stations, lags), jnp.bfloat16),
            jax.ShapeDtypeStruct((pairs // group, 1, group), jnp.float32),
        ),
        in_specs=[pl.BlockSpec(memory_space=pltpu.SMEM)] + [vmem] * (len(traces) + 4),
        out_specs=(
            pl.BlockSpec((group * stations, lags), lambda i: (i, 0)),
            pl.BlockSpec((1, 1, group), lambda i: (i, 0, 0)),
        ),
        scratch_shapes=[
            pltpu.VMEM((events, stations, window), jnp.float32),
            pltpu.VMEM((events + 1, stations, LANES), jnp.float32),
            pltpu.VMEM((chunk * stations, window), jnp.bfloat16),
        ],
        compiler_params=pltpu.CompilerParams(vmem_limit_bytes=56 * 1024 * 1024),
        cost_estimate=pl.CostEstimate(flops=4_500_000_000, bytes_accessed=8_000_000, transcendentals=0),
    )(slots, *traces, presence, forward, inverse, weights)


def exchange(waveforms, sta_count, tables):
    events, stations, window = waveforms.shape
    share = stations // sta_count
    blocks = waveforms.reshape(events, sta_count, share, window)
    me = lax.axis_index("sta")
    half = sta_count // 2

    def for_station(i):
        return lax.dynamic_index_in_dim(blocks, i, axis=1, keepdims=False)

    def swap(piece, j):
        return lax.ppermute(piece, "sta", [(i, i ^ j) for i in range(sta_count)])

    later = [swap(for_station(me ^ j), j) for j in range(half, sta_count)]
    across = swap(jnp.stack([for_station(me ^ 2), for_station(me ^ 3)]), 2)
    beside = swap(jnp.concatenate([for_station(me ^ 1), across[1]], axis=0), 1)
    later[3], tables = lax.optimization_barrier((later[3], tables))
    tables = bring_call(tables)
    pieces = [for_station(me), beside[:events], across[0], beside[events:]] + later
    rows = half * events * share
    near = jnp.concatenate(pieces[:half], axis=0).reshape(rows, window)
    far = jnp.concatenate(pieces[half:], axis=0).reshape(rows, window)
    return near, far, tables


def exchange_whole(waveforms):
    window = waveforms.shape[2]
    arrived = lax.all_to_all(waveforms, "sta", split_axis=1, concat_axis=0, tiled=True)
    arrived = arrived.reshape(-1, window)
    half = arrived.shape[0] // 2
    count = lax.axis_size("evt")
    down = [(i, i - 1) for i in range(1, count)]
    up = [(i, i + 1) for i in range(count - 1)]
    next_low = lax.ppermute(arrived[:half], "evt", down)
    last_high = lax.ppermute(arrived[half:], "evt", up)
    return arrived, next_low, last_high


def triangle(count):
    return count * (count + 1) // 2


def own_list(block):
    band = block // 2
    return [(x, y) for x in range(block) for y in range(x + 1, min(x + band, block - 1) + 1)]


class Rows:
    def __init__(self, block):
        self.own = len(own_list(block))
        self.zero = 2 * self.own
        self.first = self.zero + 8
        self.second = self.first + triangle(block // 2)
        self.end = self.second + triangle(block // 2)
        self.lanes = -(-self.end // LANES) * LANES


def cross_spectra(first, second):
    half = first.shape[1] // 2
    ra, ia = first[:, :half], first[:, half:]
    rb, ib = second[:, :half], second[:, half:]
    return jnp.concatenate([ra * rb + ia * ib, ra * ib - ia * rb], axis=1)


def scaled_spectra(traces_ref, me, each, place, presence_ref, present, tables_ref, weights_ref, spec_ref):
    stations, window = spec_ref.shape[1:]
    events = traces_ref.shape[0] // stations
    pieces = events // each
    result = jnp.dot(traces_ref[...], tables_ref[:, :window], preferred_element_type=jnp.float32)
    rounded = result.astype(jnp.bfloat16).astype(jnp.float32)
    energy = jnp.sum(jnp.square(rounded) * weights_ref[...], axis=1, keepdims=True) + 1e-06
    gain = jnp.broadcast_to(lax.rsqrt(energy), (events * stations, LANES)).reshape(events, stations, LANES)
    rounded = rounded.reshape(events, stations, window)
    for j in range(pieces):
        shift = ((me ^ j) & (pieces - 1)) * each
        piece = slice(j * each, (j + 1) * each)
        scale = gain[piece] * presence_ref[pl.ds(present + shift, each)]
        scale = jnp.concatenate([scale] * (window // LANES), axis=2)
        spec_ref[pl.ds(place + shift, each)] = rounded[piece] * scale


def build(lhs_ref, low, pairs, first_of, second_of):
    for i in range(0, len(pairs), 2):
        both = [cross_spectra(first_of(x), second_of(y)) for x, y in pairs[i:i + 2]]
        rows = 2 * both[0].shape[0]
        lhs_ref[pl.ds((low + i) * rows // 2, rows), :] = jnp.concatenate(both, axis=0).astype(jnp.bfloat16)


def keep(table_ref, peaks, values, row):
    stations, lags = table_ref.shape[1:]
    lane = lax.broadcasted_iota(jnp.int32, (stations, LANES), 1)
    count = values.shape[0] // stations
    for i in range(count):
        top = jnp.max(values[i * stations:(i + 1) * stations], axis=1, keepdims=True)
        at, within = divmod(row + i, LANES)
        peaks[at] = jnp.where(lane == within, top, peaks[at])
    table_ref[pl.ds(row, count)] = values.reshape(count, stations, lags).astype(jnp.bfloat16)


def no_peaks(rows, stations):
    return [jnp.zeros((stations, LANES), jnp.float32) for _ in range(rows.lanes // LANES)]


def prepare_kernel(
    block, packed_ref, row_ref, count_ref, held_ref,
):
    place = lax.axis_index("evt")
    start = place * block
    lines = row_ref.shape[0]

    def stacked(line):
        return jnp.concatenate(
            [packed_ref[line:line + 1, i * LANES:(i + 1) * LANES] for i in range(lines)], axis=0
        )

    first, second, valid = stacked(0), stacked(1), stacked(2)
    rows = Rows(block)
    row = table_row(first - start, second - start, place, block, rows)
    row = jnp.where(valid > 0, row, rows.zero)
    row_ref[...] = jnp.clip(row, 0, rows.end - 1)

    presence = packed_ref[3:, :LANES]
    stations, events = presence.shape
    bits = jnp.zeros((1, events), jnp.int32)
    for s in range(stations):
        bits = bits + presence[s:s + 1] * (1 << s)
    bits = jnp.broadcast_to(bits, (lines, events))
    both = jnp.take_along_axis(bits, first, axis=1) & jnp.take_along_axis(bits, second, axis=1)
    count = jnp.zeros_like(both)
    for s in range(stations):
        count = count + (lax.shift_right_logical(both, s) & 1)
    count_ref[...] = (count * valid).astype(jnp.float32)

    lane = lax.broadcasted_iota(jnp.int32, presence.shape, 1)
    present = presence.astype(jnp.float32)
    for i in range(held_ref.shape[0]):
        mine = jnp.where(lane == start - block // 2 + i, present, 0.0)
        held_ref[i] = jnp.broadcast_to(jnp.sum(mine, axis=1, keepdims=True), (stations, LANES))


def bring_kernel(tables_ref, tables_out, sem):
    copy = pltpu.make_async_copy(tables_ref, tables_out, sem)
    copy.start()
    copy.wait()


def own_pairs(spec_ref, tables_ref, table_ref, peaks, lhs_ref):
    block, stations, window = spec_ref.shape
    half = window // 2
    pairs = own_list(block)
    chunk = 64
    for low in range(0, len(pairs), chunk):
        some = pairs[low:low + chunk]
        held = {x: spec_ref[x] for x, _ in some}
        build(lhs_ref, low, some, lambda x: held[x], lambda y: spec_ref[y])
        rows = pl.ds(low * stations, len(some) * stations)
        even = jnp.dot(lhs_ref[rows, :half], tables_ref[:half, window:], preferred_element_type=jnp.float32)
        odd = jnp.dot(lhs_ref[rows, half:], tables_ref[half:, window:], preferred_element_type=jnp.float32)
        keep(table_ref, peaks, even + odd, low)
        keep(table_ref, peaks, even - odd, len(pairs) + low)


def halo_pairs(high, own_ref, spec_ref, tables_ref, table_ref, peaks, lhs_ref, row):
    band, stations, window = spec_ref.shape

    def own(u):
        return own_ref[jnp.where(high, band + u, band - 1 - u)]

    def other(h):
        return spec_ref[jnp.where(high, h, band - 1 - h)]

    pairs = [(u, h) for u in range(band) for h in range(u + 1)]
    chunk = 68
    for low in range(0, len(pairs), chunk):
        some = pairs[low:low + chunk]
        held = {u: own(u) for u, _ in some}
        build(lhs_ref, low, some, lambda u: held[u], other)
        rows = pl.ds(low * stations, len(some) * stations)
        lagged = jnp.dot(lhs_ref[rows, :], tables_ref[:, window:], preferred_element_type=jnp.float32)
        keep(table_ref, peaks, lagged, row + low)


def own_kernel(
    each, near_ref, far_ref, presence_ref, tables_ref, weights_ref,
    spec_ref, table_ref, peak_ref, lhs_ref,
):
    block, stations, window = spec_ref.shape
    band = block // 2
    me = lax.axis_index("sta")
    mine = jnp.where(me * each < band, 0, band)
    for ref, place in ((near_ref, mine), (far_ref, band - mine)):
        scaled_spectra(
            ref, me, each, place, presence_ref, band + place, tables_ref, weights_ref, spec_ref
        )
    rows = Rows(block)
    peaks = no_peaks(rows, stations)
    own_pairs(spec_ref, tables_ref, table_ref, peaks, lhs_ref)
    table_ref[rows.zero] = jnp.zeros(table_ref.shape[1:], table_ref.dtype)
    peak_ref[...] = jnp.concatenate(peaks, axis=1)


def middle_kernel(
    each, halo_ref, own_ref, presence_ref, tables_ref, weights_ref, own_peak_ref,
    held_table_ref, table_ref, peak_ref, other_ref, lhs_ref,
):
    del held_table_ref
    block, stations, window = own_ref.shape
    band = block // 2
    me = lax.axis_index("sta")
    high = lax.axis_index("evt") % 2 == 0
    edge = jnp.where(high, 3 * band, 0)
    scaled_spectra(halo_ref, me, each, 0, presence_ref, edge, tables_ref, weights_ref, other_ref)
    rows = Rows(block)
    peaks = no_peaks(rows, stations)
    halo_pairs(high, own_ref, other_ref, tables_ref, table_ref, peaks, lhs_ref, rows.first)
    peak_ref[...] = own_peak_ref[...] + jnp.concatenate(peaks, axis=1)


def last_kernel(
    each, halo_ref, own_ref, presence_ref, tables_ref, weights_ref, peak_ref, row_ref, count_ref,
    held_table_ref, table_ref, sums_ref, other_ref, lhs_ref,
):
    del held_table_ref
    block, stations, window = own_ref.shape
    band = block // 2
    me = lax.axis_index("sta")
    high = lax.axis_index("evt") % 2 == 1
    edge = jnp.where(high, 3 * band, 0)
    scaled_spectra(halo_ref, me, each, 0, presence_ref, edge, tables_ref, weights_ref, other_ref)
    rows = Rows(block)
    peaks = no_peaks(rows, stations)
    halo_pairs(high, own_ref, other_ref, tables_ref, table_ref, peaks, lhs_ref, rows.second)
    row = row_ref[...]
    lanes = row & (LANES - 1)
    total = jnp.zeros(row.shape, jnp.float32)
    for at, late in enumerate(peaks):
        line = jnp.sum(peak_ref[:, at * LANES:(at + 1) * LANES] + late, axis=0, keepdims=True)
        picked = jnp.take_along_axis(jnp.broadcast_to(line, row.shape), lanes, axis=1)
        total = jnp.where(lax.shift_right_logical(row, 7) == at, picked, total)
    sums_ref[0] = total
    sums_ref[1] = count_ref[...]


def pick_kernel(start, group, row_ref, table_ref, *refs):
    out_ref, picked_ref, sems = refs[-3:]
    copies = []
    for low in range(0, picked_ref.shape[0], group):
        for i in range(low, low + group):
            picked_ref[i] = table_ref[row_ref[start + i]]
        copies.append(pltpu.make_async_copy(
            picked_ref.at[pl.ds(low, group)], out_ref.at[pl.ds(start + low, group)], sems.at[low // group]
        ))
        copies[-1].start()
    for copy in copies:
        copy.wait()


VMEM = pl.BlockSpec(memory_space=pltpu.VMEM)
SMEM = pl.BlockSpec(memory_space=pltpu.SMEM)
PARAMS = pltpu.CompilerParams(vmem_limit_bytes=20 * 1024 * 1024)


def cost(rows, lags, window, traces, moved):
    return pl.CostEstimate(
        flops=2 * window * (rows * lags + traces * window), bytes_accessed=moved, transcendentals=0
    )


def prepare_call(pair_events, pair_valid, presence, block):
    pairs = pair_events.shape[0]
    events, stations = presence.shape
    packed = jnp.concatenate(
        [pair_events.T, pair_valid[None], jnp.pad(presence.T, ((0, 0), (0, pairs - events)))], axis=0
    )
    line = (pairs // LANES, LANES)
    return pl.pallas_call(
        functools.partial(prepare_kernel, block),
        out_shape=(
            jax.ShapeDtypeStruct(line, jnp.int32),
            jax.ShapeDtypeStruct(line, jnp.float32),
            jax.ShapeDtypeStruct((2 * block, stations, LANES), jnp.float32),
        ),
        in_specs=[VMEM],
        out_specs=(VMEM,) * 3,
        compiler_params=PARAMS,
        cost_estimate=pl.CostEstimate(flops=1_000_000, bytes_accessed=1_000_000, transcendentals=0),
    )(packed)


def bring_call(tables):
    return pl.pallas_call(
        bring_kernel,
        out_shape=jax.ShapeDtypeStruct(tables.shape, tables.dtype),
        in_specs=[pl.BlockSpec(memory_space=pl.ANY)],
        out_specs=VMEM,
        scratch_shapes=[pltpu.SemaphoreType.DMA],
        compiler_params=PARAMS,
        cost_estimate=pl.CostEstimate(flops=0, bytes_accessed=5_000_000, transcendentals=0),
    )(tables)


def own_call(near, far, presence, tables, each, block):
    table_of, weights = tables
    window = table_of.shape[0]
    lags = table_of.shape[1] - window
    stations = presence.shape[1]
    rows = Rows(block)
    return pl.pallas_call(
        functools.partial(own_kernel, each),
        out_shape=(
            jax.ShapeDtypeStruct((block, stations, window), jnp.float32),
            jax.ShapeDtypeStruct((rows.end, stations, lags), jnp.bfloat16),
            jax.ShapeDtypeStruct((stations, rows.lanes), jnp.float32),
        ),
        in_specs=[VMEM] * 5,
        out_specs=(VMEM,) * 3,
        scratch_shapes=[pltpu.VMEM((rows.own * stations, window), jnp.bfloat16)],
        compiler_params=PARAMS,
        cost_estimate=cost(rows.own * stations, lags, window, near.shape[0] * 2, 8_000_000),
    )(near, far, presence, table_of, weights)


def middle_call(halo, own, presence, tables, peaks, table, each):
    table_of, weights = tables
    window = table_of.shape[0]
    lags = table_of.shape[1] - window
    block, stations = own.shape[:2]
    pairs = triangle(block // 2)
    return pl.pallas_call(
        functools.partial(middle_kernel, each),
        out_shape=(
            jax.ShapeDtypeStruct(table.shape, table.dtype),
            jax.ShapeDtypeStruct(peaks.shape, peaks.dtype),
        ),
        in_specs=[VMEM] * 7,
        out_specs=(VMEM,) * 2,
        scratch_shapes=[
            pltpu.VMEM((block // 2, stations, window), jnp.float32),
            pltpu.VMEM((pairs * stations, window), jnp.bfloat16),
        ],
        input_output_aliases={6: 0},
        compiler_params=PARAMS,
        cost_estimate=cost(pairs * stations, lags, window, halo.shape[0], 4_000_000),
    )(halo, own, presence, table_of, weights, peaks, table)


def last_call(halo, own, presence, tables, peaks, row, count, table, each):
    table_of, weights = tables
    window = table_of.shape[0]
    lags = table_of.shape[1] - window
    block, stations = own.shape[:2]
    pairs = triangle(block // 2)
    return pl.pallas_call(
        functools.partial(last_kernel, each),
        out_shape=(
            jax.ShapeDtypeStruct(table.shape, table.dtype),
            jax.ShapeDtypeStruct((2,) + row.shape, jnp.float32),
        ),
        in_specs=[VMEM] * 9,
        out_specs=(VMEM,) * 2,
        scratch_shapes=[
            pltpu.VMEM((block // 2, stations, window), jnp.float32),
            pltpu.VMEM((pairs * stations, window), jnp.bfloat16),
        ],
        input_output_aliases={8: 0},
        compiler_params=PARAMS,
        cost_estimate=cost(pairs * stations, lags, window, halo.shape[0], 4_000_000),
    )(halo, own, presence, table_of, weights, peaks, row, count, table)


def pick_call(row, table, held, start, count):
    group = 64
    anywhere = pl.BlockSpec(memory_space=pl.ANY)
    return pl.pallas_call(
        functools.partial(pick_kernel, start, group),
        out_shape=jax.ShapeDtypeStruct(row.shape + table.shape[1:], table.dtype),
        in_specs=[SMEM, VMEM] + [anywhere] * len(held),
        out_specs=anywhere,
        scratch_shapes=[
            pltpu.VMEM((count,) + table.shape[1:], table.dtype),
            pltpu.SemaphoreType.DMA((count // group,)),
        ],
        input_output_aliases={2: 0} if held else {},
        compiler_params=PARAMS,
        cost_estimate=pl.CostEstimate(flops=0, bytes_accessed=count * 20_000, transcendentals=0),
    )(row, table, *held)


def table_row(first, second, place, block, rows):
    band = block // 2
    low, apart = jnp.minimum(first, second), jnp.abs(first - second)
    past = jnp.maximum(low - band, 0)
    index = jnp.minimum(low, band) * band + past * (band - 1) - (past * (past - 1) >> 1) + apart - 1
    inside = jnp.where(second > first, index, rows.own + index)
    high = second >= block
    u = jnp.where(high, first - band, band - 1 - first)
    h = jnp.where(high, second - block, -1 - second)
    outside = jnp.where(jnp.where(high, 1, 0) == place % 2, rows.second, rows.first) + (u * (u + 1) >> 1) + h
    return jnp.where(high | (second < 0), outside, inside)


def banded(waveforms, pair_events, pair_valid, presence, block):
    each = waveforms.shape[0]
    forward, inverse, weights = spectral_tables(waveforms.shape[2], LAGS)
    tables = (jnp.asarray(np.concatenate([forward, inverse], axis=1)), jnp.asarray(weights))
    near, far, brought = exchange(waveforms, lax.axis_size("sta"), tables[0])
    ready = prepare_call(pair_events, pair_valid, presence, block)
    far, ready, brought = lax.optimization_barrier((far, ready, brought))
    tables = (brought, tables[1])
    me, place = lax.axis_index("sta"), lax.axis_index("evt")
    count = lax.axis_size("evt")
    inward = (place % 2 == 0) == (me * each < block // 2)

    def swapped(half, odd):
        links = [(i, i + 1) for i in range(odd, count - 1, 2)]
        return lax.ppermute(half, "evt", links + [(j, i) for i, j in links])

    first_halo = swapped(jnp.where(inward, far, near), 0)
    second_halo = swapped(jnp.where(inward, near, far), 1)
    row, count, held = ready
    own, table, peaks = own_call(near, far, held, tables, each, block)
    table, peaks = middle_call(first_halo, own, held, tables, peaks, table, each)
    table, sums = last_call(second_halo, own, held, tables, peaks, row, count, table, each)

    row = row.reshape(-1)
    groups = row.shape[0] // LANES
    correlation = ()
    step, skip = lax.axis_size("sta") // 2, 0
    while step:
        arrived = lax.ppermute(sums, "sta", [(i, i ^ step) for i in range(lax.axis_size("sta"))])
        steps = -(-(groups - skip) // step.bit_length())
        correlation = (pick_call(row, table, correlation, skip * LANES, steps * LANES),)
        sums, correlation = lax.optimization_barrier((sums + arrived, correlation))
        skip += steps
        step //= 2
    return correlation[0], sums


def by_slot(waveforms, pair_events, pair_valid, presence, block):
    share = presence.shape[1]
    start = lax.axis_index("evt") * block
    traces = exchange_whole(waveforms)
    place = pair_events - start
    slot = jnp.where((place >= 0) & (place < block), 0, block) + place % block
    gained = jnp.where(pair_valid > 0, slot[:, 0], 2 * block)
    slots = jnp.stack([slot[:, 0], slot[:, 1], gained]).astype(jnp.int32)
    held = jnp.arange(2 * block, dtype=jnp.int32)
    held = jnp.where(held < block, held, jnp.where(held < block + block // 2, held, held - 2 * block))
    held = jnp.clip(start + held, 0, presence.shape[0] - 1)
    slot_presence = jnp.broadcast_to(
        jnp.take(presence.astype(jnp.float32), held, axis=0)[:, :, None], (2 * block, share, LANES)
    )
    few = presence.astype(jnp.bfloat16)
    event = jnp.arange(presence.shape[0], dtype=jnp.int32)
    first, second = (
        jnp.dot((pair_events[:, i:i + 1] == event).astype(jnp.bfloat16), few, preferred_element_type=jnp.float32)
        for i in (0, 1)
    )
    counts = jnp.sum(first * second, axis=1) * pair_valid.astype(jnp.float32)
    tables = tuple(jnp.asarray(x) for x in spectral_tables(waveforms.shape[2], LAGS))
    correlation, peaks = pair_call(slots, traces, slot_presence, tables)
    sums = lax.psum(jnp.stack([peaks.reshape(-1), counts]), "sta")
    return correlation.reshape(-1, share, correlation.shape[1]), sums


def body(waveforms, pair_events, pair_valid, presence):
    sta_count = lax.axis_size("sta")
    local_events, stations, window = waveforms.shape
    block = sta_count * local_events
    args = (waveforms, pair_events, pair_valid, presence, block)
    dense = sta_count == 8 and presence.shape[0] == LANES and block * block <= pair_events.shape[0]
    correlation, sums = (banded if dense else by_slot)(*args)
    pair_peak = sums[0] / jnp.maximum(sums[1], 1.0)
    return correlation, pair_peak.reshape(-1)


def solution(mesh):
    return jax.shard_map(
        body,
        mesh=mesh,
        in_specs=(P(("evt", "sta"), None, None), P("evt", None), P("evt"), P(None, "sta")),
        out_specs=(P("evt", "sta", None), P("evt")),
        check_vma=False,
    )
```

```python
import functools
import math

import jax
import jax.numpy as jnp
import numpy as np
from jax import lax
from jax.experimental import pallas as pl
from jax.experimental.pallas import tpu as pltpu
from jax.sharding import PartitionSpec as P

LAGS = 256
LANES = 128


def spectral_tables(window, lag_count):
    half = window // 2
    sample = np.arange(window, dtype=np.int64)
    bins = np.arange(half, dtype=np.int64)
    angle = (sample[:, None] * bins[None, :] % window) * (2.0 * math.pi / window)
    forward = np.concatenate([np.cos(angle), -np.sin(angle)], axis=1) / math.sqrt(window)
    shifts = np.arange(lag_count, dtype=np.int64) - lag_count // 2
    lag_angle = (bins[:, None] * shifts[None, :] % window) * (2.0 * math.pi / window)
    factor = np.where(bins == 0, 1.0, 2.0)[:, None]
    inverse = np.concatenate([factor * np.cos(lag_angle), -factor * np.sin(lag_angle)], axis=0)
    weights = np.concatenate([factor[:, 0], factor[:, 0]])[None, :]
    return forward.astype(jnp.bfloat16), inverse.astype(jnp.bfloat16), weights.astype(np.float32)


def pair_kernel(
    group, chunk, parts, slots_ref, *refs
):
    traces = refs[:parts]
    (
        presence_ref, forward_ref, inverse_ref, weights_ref,
        out_ref, peak_ref,
        spec_ref, gain_ref, lhs_ref,
    ) = refs[parts:]
    stations, window = spec_ref.shape[1:]
    half = window // 2
    events = spec_ref.shape[0]

    @pl.when(pl.program_id(0) == 0)
    def _():
        start = 0
        for ref in traces:
            rows = ref.shape[0]
            count = rows // stations
            result = jnp.dot(ref[...], forward_ref[...], preferred_element_type=jnp.float32)
            rounded = result.astype(jnp.bfloat16).astype(jnp.float32)
            spec_ref[pl.ds(start, count)] = rounded.reshape(count, stations, window)
            power = jnp.square(rounded) * weights_ref[...]
            energy = jnp.sum(power, axis=1, keepdims=True) + 1e-06
            gain = jnp.broadcast_to(lax.rsqrt(energy), (rows, LANES))
            gain = gain.reshape(count, stations, LANES) * presence_ref[pl.ds(start, count)]
            gain_ref[pl.ds(start, count)] = gain
            start += count
        gain_ref[events] = jnp.zeros((stations, LANES), jnp.float32)

    base = pl.program_id(0) * group
    lane = lax.broadcasted_iota(jnp.int32, (stations, LANES), 1)

    def cross(pair):
        first = spec_ref[slots_ref[0, pair]]
        second = spec_ref[slots_ref[1, pair]]
        ra, ia = first[:, :half], first[:, half:]
        rb, ib = second[:, :half], second[:, half:]
        return jnp.concatenate([ra * rb + ia * ib, ra * ib - ia * rb], axis=1)

    def one_chunk(index, peaks):
        first_pair = base + index * chunk
        for j in range(0, chunk, 2):
            both = jnp.concatenate([cross(first_pair + j), cross(first_pair + j + 1)], axis=0)
            lhs_ref[pl.ds(j * stations, 2 * stations), :] = both.astype(jnp.bfloat16)
        lagged = jnp.dot(lhs_ref[...], inverse_ref[...], preferred_element_type=jnp.float32)
        for j in range(0, chunk, 2):
            rows = []
            for i in (j, j + 1):
                pair = first_pair + i
                gain = gain_ref[slots_ref[2, pair]] * gain_ref[slots_ref[1, pair]]
                scaled = lagged[i * stations:(i + 1) * stations] * jnp.concatenate([gain, gain], axis=1)
                rows.append(scaled)
                top = jnp.max(scaled, axis=1, keepdims=True)
                peaks = jnp.where(lane == index * chunk + i, top, peaks)
            block = jnp.concatenate(rows, axis=0).astype(jnp.bfloat16)
            start = pl.multiple_of(index * chunk * stations, chunk * stations) + j * stations
            out_ref[pl.ds(start, 2 * stations), :] = block
        return peaks

    peaks = lax.fori_loop(0, group // chunk, one_chunk, jnp.zeros((stations, LANES), jnp.float32))
    peak_ref[0] = jnp.sum(peaks, axis=0, keepdims=True)


def pair_call(slots, traces, presence, tables):
    forward, inverse, weights = tables
    window = forward.shape[0]
    lags = inverse.shape[1]
    pairs = slots.shape[1]
    events, stations = presence.shape[:2]
    group = LANES
    chunk = 32
    vmem = pl.BlockSpec(memory_space=pltpu.VMEM)
    return pl.pallas_call(
        functools.partial(pair_kernel, group, chunk, len(traces)),
        grid=(pairs // group,),
        out_shape=(
            jax.ShapeDtypeStruct((pairs * stations, lags), jnp.bfloat16),
            jax.ShapeDtypeStruct((pairs // group, 1, group), jnp.float32),
        ),
        in_specs=[pl.BlockSpec(memory_space=pltpu.SMEM)] + [vmem] * (len(traces) + 4),
        out_specs=(
            pl.BlockSpec((group * stations, lags), lambda i: (i, 0)),
            pl.BlockSpec((1, 1, group), lambda i: (i, 0, 0)),
        ),
        scratch_shapes=[
            pltpu.VMEM((events, stations, window), jnp.float32),
            pltpu.VMEM((events + 1, stations, LANES), jnp.float32),
            pltpu.VMEM((chunk * stations, window), jnp.bfloat16),
        ],
        compiler_params=pltpu.CompilerParams(vmem_limit_bytes=56 * 1024 * 1024),
        cost_estimate=pl.CostEstimate(flops=4_500_000_000, bytes_accessed=8_000_000, transcendentals=0),
    )(slots, *traces, presence, forward, inverse, weights)


def exchange(waveforms, sta_count, tables):
    events, stations, window = waveforms.shape
    share = stations // sta_count
    blocks = waveforms.reshape(events, sta_count, share, window)
    me = lax.axis_index("sta")
    half = sta_count // 2

    def for_station(i):
        return lax.dynamic_index_in_dim(blocks, i, axis=1, keepdims=False)

    def swap(piece, j):
        return lax.ppermute(piece, "sta", [(i, i ^ j) for i in range(sta_count)])

    later = [swap(for_station(me ^ j), j) for j in range(half, sta_count)]
    across = swap(jnp.stack([for_station(me ^ 2), for_station(me ^ 3)]), 2)
    beside = swap(jnp.concatenate([for_station(me ^ 1), across[1]], axis=0), 1)
    later[3], tables = lax.optimization_barrier((later[3], tables))
    tables = bring_call(tables)
    pieces = [for_station(me), beside[:events], across[0], beside[events:]] + later
    rows = half * events * share
    near = jnp.concatenate(pieces[:half], axis=0).reshape(rows, window)
    far = jnp.concatenate(pieces[half:], axis=0).reshape(rows, window)
    return near, far, tables


def exchange_whole(waveforms):
    window = waveforms.shape[2]
    arrived = lax.all_to_all(waveforms, "sta", split_axis=1, concat_axis=0, tiled=True)
    arrived = arrived.reshape(-1, window)
    half = arrived.shape[0] // 2
    count = lax.axis_size("evt")
    down = [(i, i - 1) for i in range(1, count)]
    up = [(i, i + 1) for i in range(count - 1)]
    next_low = lax.ppermute(arrived[:half], "evt", down)
    last_high = lax.ppermute(arrived[half:], "evt", up)
    return arrived, next_low, last_high


def triangle(count):
    return count * (count + 1) // 2


def own_list(block):
    band = block // 2
    return [(x, y) for x in range(block) for y in range(x + 1, min(x + band, block - 1) + 1)]


class Rows:
    def __init__(self, block):
        self.own = len(own_list(block))
        self.zero = 2 * self.own
        self.first = self.zero + 8
        self.second = self.first + triangle(block // 2)
        self.end = self.second + triangle(block // 2)
        self.lanes = -(-self.end // LANES) * LANES


def cross_spectra(first, second):
    half = first.shape[1] // 2
    ra, ia = first[:, :half], first[:, half:]
    rb, ib = second[:, :half], second[:, half:]
    return jnp.concatenate([ra * rb + ia * ib, ra * ib - ia * rb], axis=1)


def scaled_spectra(traces_ref, me, each, place, presence_ref, present, tables_ref, weights_ref, spec_ref):
    stations, window = spec_ref.shape[1:]
    events = traces_ref.shape[0] // stations
    pieces = events // each
    result = jnp.dot(traces_ref[...], tables_ref[:, :window], preferred_element_type=jnp.float32)
    rounded = result.astype(jnp.bfloat16).astype(jnp.float32)
    energy = jnp.sum(jnp.square(rounded) * weights_ref[...], axis=1, keepdims=True) + 1e-06
    gain = jnp.broadcast_to(lax.rsqrt(energy), (events * stations, LANES)).reshape(events, stations, LANES)
    rounded = rounded.reshape(events, stations, window)
    for j in range(pieces):
        shift = ((me ^ j) & (pieces - 1)) * each
        piece = slice(j * each, (j + 1) * each)
        scale = gain[piece] * presence_ref[pl.ds(present + shift, each)]
        scale = jnp.concatenate([scale] * (window // LANES), axis=2)
        spec_ref[pl.ds(place + shift, each)] = rounded[piece] * scale


def build(lhs_ref, low, pairs, first_of, second_of):
    for i in range(0, len(pairs), 2):
        both = [cross_spectra(first_of(x), second_of(y)) for x, y in pairs[i:i + 2]]
        rows = 2 * both[0].shape[0]
        lhs_ref[pl.ds((low + i) * rows // 2, rows), :] = jnp.concatenate(both, axis=0).astype(jnp.bfloat16)


def keep(table_ref, peaks, values, row):
    stations, lags = table_ref.shape[1:]
    lane = lax.broadcasted_iota(jnp.int32, (stations, LANES), 1)
    count = values.shape[0] // stations
    for i in range(count):
        top = jnp.max(values[i * stations:(i + 1) * stations], axis=1, keepdims=True)
        at, within = divmod(row + i, LANES)
        peaks[at] = jnp.where(lane == within, top, peaks[at])
    table_ref[pl.ds(row, count)] = values.reshape(count, stations, lags).astype(jnp.bfloat16)


def no_peaks(rows, stations):
    return [jnp.zeros((stations, LANES), jnp.float32) for _ in range(rows.lanes // LANES)]


def prepare_kernel(
    block, packed_ref, row_ref, count_ref, held_ref,
):
    place = lax.axis_index("evt")
    start = place * block
    lines = row_ref.shape[0]

    def stacked(line):
        return jnp.concatenate(
            [packed_ref[line:line + 1, i * LANES:(i + 1) * LANES] for i in range(lines)], axis=0
        )

    first, second, valid = stacked(0), stacked(1), stacked(2)
    rows = Rows(block)
    row = table_row(first - start, second - start, place, block, rows)
    row = jnp.where(valid > 0, row, rows.zero)
    row_ref[...] = jnp.clip(row, 0, rows.end - 1)

    presence = packed_ref[3:, :LANES]
    stations, events = presence.shape
    bits = jnp.zeros((1, events), jnp.int32)
    for s in range(stations):
        bits = bits + presence[s:s + 1] * (1 << s)
    bits = jnp.broadcast_to(bits, (lines, events))
    both = jnp.take_along_axis(bits, first, axis=1) & jnp.take_along_axis(bits, second, axis=1)
    count = jnp.zeros_like(both)
    for s in range(stations):
        count = count + (lax.shift_right_logical(both, s) & 1)
    count_ref[...] = (count * valid).astype(jnp.float32)

    lane = lax.broadcasted_iota(jnp.int32, presence.shape, 1)
    present = presence.astype(jnp.float32)
    for i in range(held_ref.shape[0]):
        mine = jnp.where(lane == start - block // 2 + i, present, 0.0)
        held_ref[i] = jnp.broadcast_to(jnp.sum(mine, axis=1, keepdims=True), (stations, LANES))


def bring_kernel(tables_ref, tables_out, sem):
    copy = pltpu.make_async_copy(tables_ref, tables_out, sem)
    copy.start()
    copy.wait()


def own_pairs(spec_ref, tables_ref, table_ref, peaks, lhs_ref):
    block, stations, window = spec_ref.shape
    half = window // 2
    pairs = own_list(block)
    chunk = 64
    for low in range(0, len(pairs), chunk):
        some = pairs[low:low + chunk]
        held = {x: spec_ref[x] for x, _ in some}
        build(lhs_ref, low, some, lambda x: held[x], lambda y: spec_ref[y])
        rows = pl.ds(low * stations, len(some) * stations)
        even = jnp.dot(lhs_ref[rows, :half], tables_ref[:half, window:], preferred_element_type=jnp.float32)
        odd = jnp.dot(lhs_ref[rows, half:], tables_ref[half:, window:], preferred_element_type=jnp.float32)
        keep(table_ref, peaks, even + odd, low)
        keep(table_ref, peaks, even - odd, len(pairs) + low)


def halo_pairs(high, own_ref, spec_ref, tables_ref, table_ref, peaks, lhs_ref, row):
    band, stations, window = spec_ref.shape

    def own(u):
        return own_ref[jnp.where(high, band + u, band - 1 - u)]

    def other(h):
        return spec_ref[jnp.where(high, h, band - 1 - h)]

    pairs = [(u, h) for u in range(band) for h in range(u + 1)]
    chunk = 68
    for low in range(0, len(pairs), chunk):
        some = pairs[low:low + chunk]
        held = {u: own(u) for u, _ in some}
        build(lhs_ref, low, some, lambda u: held[u], other)
        rows = pl.ds(low * stations, len(some) * stations)
        lagged = jnp.dot(lhs_ref[rows, :], tables_ref[:, window:], preferred_element_type=jnp.float32)
        keep(table_ref, peaks, lagged, row + low)


def own_kernel(
    each, near_ref, far_ref, presence_ref, tables_ref, weights_ref,
    spec_ref, table_ref, peak_ref, lhs_ref,
):
    block, stations, window = spec_ref.shape
    band = block // 2
    me = lax.axis_index("sta")
    mine = jnp.where(me * each < band, 0, band)
    for ref, place in ((near_ref, mine), (far_ref, band - mine)):
        scaled_spectra(
            ref, me, each, place, presence_ref, band + place, tables_ref, weights_ref, spec_ref
        )
    rows = Rows(block)
    peaks = no_peaks(rows, stations)
    own_pairs(spec_ref, tables_ref, table_ref, peaks, lhs_ref)
    table_ref[rows.zero] = jnp.zeros(table_ref.shape[1:], table_ref.dtype)
    peak_ref[...] = jnp.concatenate(peaks, axis=1)


def middle_kernel(
    each, halo_ref, own_ref, presence_ref, tables_ref, weights_ref, own_peak_ref,
    held_table_ref, table_ref, peak_ref, other_ref, lhs_ref,
):
    del held_table_ref
    block, stations, window = own_ref.shape
    band = block // 2
    me = lax.axis_index("sta")
    high = lax.axis_index("evt") % 2 == 0
    edge = jnp.where(high, 3 * band, 0)
    scaled_spectra(halo_ref, me, each, 0, presence_ref, edge, tables_ref, weights_ref, other_ref)
    rows = Rows(block)
    peaks = no_peaks(rows, stations)
    halo_pairs(high, own_ref, other_ref, tables_ref, table_ref, peaks, lhs_ref, rows.first)
    peak_ref[...] = own_peak_ref[...] + jnp.concatenate(peaks, axis=1)


def last_kernel(
    each, halo_ref, own_ref, presence_ref, tables_ref, weights_ref, peak_ref, row_ref, count_ref,
    held_table_ref, table_ref, sums_ref, other_ref, lhs_ref,
):
    del held_table_ref
    block, stations, window = own_ref.shape
    band = block // 2
    me = lax.axis_index("sta")
    high = lax.axis_index("evt") % 2 == 1
    edge = jnp.where(high, 3 * band, 0)
    scaled_spectra(halo_ref, me, each, 0, presence_ref, edge, tables_ref, weights_ref, other_ref)
    rows = Rows(block)
    peaks = no_peaks(rows, stations)
    halo_pairs(high, own_ref, other_ref, tables_ref, table_ref, peaks, lhs_ref, rows.second)
    row = row_ref[...]
    lanes = row & (LANES - 1)
    total = jnp.zeros(row.shape, jnp.float32)
    for at, late in enumerate(peaks):
        line = jnp.sum(peak_ref[:, at * LANES:(at + 1) * LANES] + late, axis=0, keepdims=True)
        picked = jnp.take_along_axis(jnp.broadcast_to(line, row.shape), lanes, axis=1)
        total = jnp.where(lax.shift_right_logical(row, 7) == at, picked, total)
    sums_ref[0] = total
    sums_ref[1] = count_ref[...]


def pick_kernel(start, group, row_ref, table_ref, *refs):
    out_ref, picked_ref, sems = refs[-3:]
    copies = []
    for low in range(0, picked_ref.shape[0], group):
        for i in range(low, low + group):
            picked_ref[i] = table_ref[row_ref[start + i]]
        copies.append(pltpu.make_async_copy(
            picked_ref.at[pl.ds(low, group)], out_ref.at[pl.ds(start + low, group)], sems.at[low // group]
        ))
        copies[-1].start()
    for copy in copies:
        copy.wait()


VMEM = pl.BlockSpec(memory_space=pltpu.VMEM)
SMEM = pl.BlockSpec(memory_space=pltpu.SMEM)
PARAMS = pltpu.CompilerParams(vmem_limit_bytes=20 * 1024 * 1024)


def cost(rows, lags, window, traces, moved):
    return pl.CostEstimate(
        flops=2 * window * (rows * lags + traces * window), bytes_accessed=moved, transcendentals=0
    )


def prepare_call(pair_events, pair_valid, presence, block):
    pairs = pair_events.shape[0]
    events, stations = presence.shape
    packed = jnp.concatenate(
        [pair_events.T, pair_valid[None], jnp.pad(presence.T, ((0, 0), (0, pairs - events)))], axis=0
    )
    line = (pairs // LANES, LANES)
    return pl.pallas_call(
        functools.partial(prepare_kernel, block),
        out_shape=(
            jax.ShapeDtypeStruct(line, jnp.int32),
            jax.ShapeDtypeStruct(line, jnp.float32),
            jax.ShapeDtypeStruct((2 * block, stations, LANES), jnp.float32),
        ),
        in_specs=[VMEM],
        out_specs=(VMEM,) * 3,
        compiler_params=PARAMS,
        cost_estimate=pl.CostEstimate(flops=1_000_000, bytes_accessed=1_000_000, transcendentals=0),
    )(packed)


def bring_call(tables):
    return pl.pallas_call(
        bring_kernel,
        out_shape=jax.ShapeDtypeStruct(tables.shape, tables.dtype),
        in_specs=[pl.BlockSpec(memory_space=pl.ANY)],
        out_specs=VMEM,
        scratch_shapes=[pltpu.SemaphoreType.DMA],
        compiler_params=PARAMS,
        cost_estimate=pl.CostEstimate(flops=0, bytes_accessed=5_000_000, transcendentals=0),
    )(tables)


def own_call(near, far, presence, tables, each, block):
    table_of, weights = tables
    window = table_of.shape[0]
    lags = table_of.shape[1] - window
    stations = presence.shape[1]
    rows = Rows(block)
    return pl.pallas_call(
        functools.partial(own_kernel, each),
        out_shape=(
            jax.ShapeDtypeStruct((block, stations, window), jnp.float32),
            jax.ShapeDtypeStruct((rows.end, stations, lags), jnp.bfloat16),
            jax.ShapeDtypeStruct((stations, rows.lanes), jnp.float32),
        ),
        in_specs=[VMEM] * 5,
        out_specs=(VMEM,) * 3,
        scratch_shapes=[pltpu.VMEM((rows.own * stations, window), jnp.bfloat16)],
        compiler_params=PARAMS,
        cost_estimate=cost(rows.own * stations, lags, window, near.shape[0] * 2, 8_000_000),
    )(near, far, presence, table_of, weights)


def middle_call(halo, own, presence, tables, peaks, table, each):
    table_of, weights = tables
    window = table_of.shape[0]
    lags = table_of.shape[1] - window
    block, stations = own.shape[:2]
    pairs = triangle(block // 2)
    return pl.pallas_call(
        functools.partial(middle_kernel, each),
        out_shape=(
            jax.ShapeDtypeStruct(table.shape, table.dtype),
            jax.ShapeDtypeStruct(peaks.shape, peaks.dtype),
        ),
        in_specs=[VMEM] * 7,
        out_specs=(VMEM,) * 2,
        scratch_shapes=[
            pltpu.VMEM((block // 2, stations, window), jnp.float32),
            pltpu.VMEM((pairs * stations, window), jnp.bfloat16),
        ],
        input_output_aliases={6: 0},
        compiler_params=PARAMS,
        cost_estimate=cost(pairs * stations, lags, window, halo.shape[0], 4_000_000),
    )(halo, own, presence, table_of, weights, peaks, table)


def last_call(halo, own, presence, tables, peaks, row, count, table, each):
    table_of, weights = tables
    window = table_of.shape[0]
    lags = table_of.shape[1] - window
    block, stations = own.shape[:2]
    pairs = triangle(block // 2)
    return pl.pallas_call(
        functools.partial(last_kernel, each),
        out_shape=(
            jax.ShapeDtypeStruct(table.shape, table.dtype),
            jax.ShapeDtypeStruct((2,) + row.shape, jnp.float32),
        ),
        in_specs=[VMEM] * 9,
        out_specs=(VMEM,) * 2,
        scratch_shapes=[
            pltpu.VMEM((block // 2, stations, window), jnp.float32),
            pltpu.VMEM((pairs * stations, window), jnp.bfloat16),
        ],
        input_output_aliases={8: 0},
        compiler_params=PARAMS,
        cost_estimate=cost(pairs * stations, lags, window, halo.shape[0], 4_000_000),
    )(halo, own, presence, table_of, weights, peaks, row, count, table)


def pick_call(row, table, held, start, count):
    group = 64
    anywhere = pl.BlockSpec(memory_space=pl.ANY)
    return pl.pallas_call(
        functools.partial(pick_kernel, start, group),
        out_shape=jax.ShapeDtypeStruct(row.shape + table.shape[1:], table.dtype),
        in_specs=[SMEM, VMEM] + [anywhere] * len(held),
        out_specs=anywhere,
        scratch_shapes=[
            pltpu.VMEM((count,) + table.shape[1:], table.dtype),
            pltpu.SemaphoreType.DMA((count // group,)),
        ],
        input_output_aliases={2: 0} if held else {},
        compiler_params=PARAMS,
        cost_estimate=pl.CostEstimate(flops=0, bytes_accessed=count * 20_000, transcendentals=0),
    )(row, table, *held)


def table_row(first, second, place, block, rows):
    band = block // 2
    low, apart = jnp.minimum(first, second), jnp.abs(first - second)
    past = jnp.maximum(low - band, 0)
    index = jnp.minimum(low, band) * band + past * (band - 1) - (past * (past - 1) >> 1) + apart - 1
    inside = jnp.where(second > first, index, rows.own + index)
    high = second >= block
    u = jnp.where(high, first - band, band - 1 - first)
    h = jnp.where(high, second - block, -1 - second)
    outside = jnp.where(jnp.where(high, 1, 0) == place % 2, rows.second, rows.first) + (u * (u + 1) >> 1) + h
    return jnp.where(high | (second < 0), outside, inside)


def banded(waveforms, pair_events, pair_valid, presence, block):
    each = waveforms.shape[0]
    forward, inverse, weights = spectral_tables(waveforms.shape[2], LAGS)
    tables = (jnp.asarray(np.concatenate([forward, inverse], axis=1)), jnp.asarray(weights))
    near, far, brought = exchange(waveforms, lax.axis_size("sta"), tables[0])
    ready = prepare_call(pair_events, pair_valid, presence, block)
    far, ready, brought = lax.optimization_barrier((far, ready, brought))
    tables = (brought, tables[1])
    me, place = lax.axis_index("sta"), lax.axis_index("evt")
    count = lax.axis_size("evt")
    inward = (place % 2 == 0) == (me * each < block // 2)

    def swapped(half, odd):
        links = [(i, i + 1) for i in range(odd, count - 1, 2)]
        return lax.ppermute(half, "evt", links + [(j, i) for i, j in links])

    first_halo = swapped(jnp.where(inward, far, near), 0)
    second_halo = swapped(jnp.where(inward, near, far), 1)
    row, count, held = ready
    own, table, peaks = own_call(near, far, held, tables, each, block)
    table, peaks = middle_call(first_halo, own, held, tables, peaks, table, each)
    table, sums = last_call(second_halo, own, held, tables, peaks, row, count, table, each)

    row = row.reshape(-1)
    sta_count = lax.axis_size("sta")

    def from_station(j):
        return lax.ppermute(sums, "sta", [(i, i ^ j) for i in range(sta_count)])

    split = row.shape[0] * 4 // 8
    beside, across, aslant = from_station(1), from_station(2), from_station(3)
    correlation = pick_call(row, table, (), 0, split)
    sums, correlation = lax.optimization_barrier(((sums + beside) + (across + aslant), correlation))
    arrived = from_station(4)
    correlation = pick_call(row, table, (correlation,), split, row.shape[0] - split)
    return correlation, sums + arrived


def by_slot(waveforms, pair_events, pair_valid, presence, block):
    share = presence.shape[1]
    start = lax.axis_index("evt") * block
    traces = exchange_whole(waveforms)
    place = pair_events - start
    slot = jnp.where((place >= 0) & (place < block), 0, block) + place % block
    gained = jnp.where(pair_valid > 0, slot[:, 0], 2 * block)
    slots = jnp.stack([slot[:, 0], slot[:, 1], gained]).astype(jnp.int32)
    held = jnp.arange(2 * block, dtype=jnp.int32)
    held = jnp.where(held < block, held, jnp.where(held < block + block // 2, held, held - 2 * block))
    held = jnp.clip(start + held, 0, presence.shape[0] - 1)
    slot_presence = jnp.broadcast_to(
        jnp.take(presence.astype(jnp.float32), held, axis=0)[:, :, None], (2 * block, share, LANES)
    )
    few = presence.astype(jnp.bfloat16)
    event = jnp.arange(presence.shape[0], dtype=jnp.int32)
    first, second = (
        jnp.dot((pair_events[:, i:i + 1] == event).astype(jnp.bfloat16), few, preferred_element_type=jnp.float32)
        for i in (0, 1)
    )
    counts = jnp.sum(first * second, axis=1) * pair_valid.astype(jnp.float32)
    tables = tuple(jnp.asarray(x) for x in spectral_tables(waveforms.shape[2], LAGS))
    correlation, peaks = pair_call(slots, traces, slot_presence, tables)
    sums = lax.psum(jnp.stack([peaks.reshape(-1), counts]), "sta")
    return correlation.reshape(-1, share, correlation.shape[1]), sums


def body(waveforms, pair_events, pair_valid, presence):
    sta_count = lax.axis_size("sta")
    local_events, stations, window = waveforms.shape
    block = sta_count * local_events
    args = (waveforms, pair_events, pair_valid, presence, block)
    dense = sta_count == 8 and presence.shape[0] == LANES and block * block <= pair_events.shape[0]
    correlation, sums = (banded if dense else by_slot)(*args)
    pair_peak = sums[0] / jnp.maximum(sums[1], 1.0)
    return correlation, pair_peak.reshape(-1)


def solution(mesh):
    return jax.shard_map(
        body,
        mesh=mesh,
        in_specs=(P(("evt", "sta"), None, None), P("evt", None), P("evt"), P(None, "sta")),
        out_specs=(P("evt", "sta", None), P("evt")),
        check_vma=False,
    )
```

```python
import functools
import math

import jax
import jax.numpy as jnp
import numpy as np
from jax import lax
from jax.experimental import pallas as pl
from jax.experimental.pallas import tpu as pltpu
from jax.sharding import PartitionSpec as P

LAGS = 256
LANES = 128


def spectral_tables(window, lag_count):
    half = window // 2
    sample = np.arange(window, dtype=np.int64)
    bins = np.arange(half, dtype=np.int64)
    angle = (sample[:, None] * bins[None, :] % window) * (2.0 * math.pi / window)
    forward = np.concatenate([np.cos(angle), -np.sin(angle)], axis=1) / math.sqrt(window)
    shifts = np.arange(lag_count, dtype=np.int64) - lag_count // 2
    lag_angle = (bins[:, None] * shifts[None, :] % window) * (2.0 * math.pi / window)
    factor = np.where(bins == 0, 1.0, 2.0)[:, None]
    inverse = np.concatenate([factor * np.cos(lag_angle), -factor * np.sin(lag_angle)], axis=0)
    weights = np.concatenate([factor[:, 0], factor[:, 0]])[None, :]
    return forward.astype(jnp.bfloat16), inverse.astype(jnp.bfloat16), weights.astype(np.float32)


def pair_kernel(
    group, chunk, parts, slots_ref, *refs
):
    traces = refs[:parts]
    (
        presence_ref, forward_ref, inverse_ref, weights_ref,
        out_ref, peak_ref,
        spec_ref, gain_ref, lhs_ref,
    ) = refs[parts:]
    stations, window = spec_ref.shape[1:]
    half = window // 2
    events = spec_ref.shape[0]

    @pl.when(pl.program_id(0) == 0)
    def _():
        start = 0
        for ref in traces:
            rows = ref.shape[0]
            count = rows // stations
            result = jnp.dot(ref[...], forward_ref[...], preferred_element_type=jnp.float32)
            rounded = result.astype(jnp.bfloat16).astype(jnp.float32)
            spec_ref[pl.ds(start, count)] = rounded.reshape(count, stations, window)
            power = jnp.square(rounded) * weights_ref[...]
            energy = jnp.sum(power, axis=1, keepdims=True) + 1e-06
            gain = jnp.broadcast_to(lax.rsqrt(energy), (rows, LANES))
            gain = gain.reshape(count, stations, LANES) * presence_ref[pl.ds(start, count)]
            gain_ref[pl.ds(start, count)] = gain
            start += count
        gain_ref[events] = jnp.zeros((stations, LANES), jnp.float32)

    base = pl.program_id(0) * group
    lane = lax.broadcasted_iota(jnp.int32, (stations, LANES), 1)

    def cross(pair):
        first = spec_ref[slots_ref[0, pair]]
        second = spec_ref[slots_ref[1, pair]]
        ra, ia = first[:, :half], first[:, half:]
        rb, ib = second[:, :half], second[:, half:]
        return jnp.concatenate([ra * rb + ia * ib, ra * ib - ia * rb], axis=1)

    def one_chunk(index, peaks):
        first_pair = base + index * chunk
        for j in range(0, chunk, 2):
            both = jnp.concatenate([cross(first_pair + j), cross(first_pair + j + 1)], axis=0)
            lhs_ref[pl.ds(j * stations, 2 * stations), :] = both.astype(jnp.bfloat16)
        lagged = jnp.dot(lhs_ref[...], inverse_ref[...], preferred_element_type=jnp.float32)
        for j in range(0, chunk, 2):
            rows = []
            for i in (j, j + 1):
                pair = first_pair + i
                gain = gain_ref[slots_ref[2, pair]] * gain_ref[slots_ref[1, pair]]
                scaled = lagged[i * stations:(i + 1) * stations] * jnp.concatenate([gain, gain], axis=1)
                rows.append(scaled)
                top = jnp.max(scaled, axis=1, keepdims=True)
                peaks = jnp.where(lane == index * chunk + i, top, peaks)
            block = jnp.concatenate(rows, axis=0).astype(jnp.bfloat16)
            start = pl.multiple_of(index * chunk * stations, chunk * stations) + j * stations
            out_ref[pl.ds(start, 2 * stations), :] = block
        return peaks

    peaks = lax.fori_loop(0, group // chunk, one_chunk, jnp.zeros((stations, LANES), jnp.float32))
    peak_ref[0] = jnp.sum(peaks, axis=0, keepdims=True)


def pair_call(slots, traces, presence, tables):
    forward, inverse, weights = tables
    window = forward.shape[0]
    lags = inverse.shape[1]
    pairs = slots.shape[1]
    events, stations = presence.shape[:2]
    group = LANES
    chunk = 32
    vmem = pl.BlockSpec(memory_space=pltpu.VMEM)
    return pl.pallas_call(
        functools.partial(pair_kernel, group, chunk, len(traces)),
        grid=(pairs // group,),
        out_shape=(
            jax.ShapeDtypeStruct((pairs * stations, lags), jnp.bfloat16),
            jax.ShapeDtypeStruct((pairs // group, 1, group), jnp.float32),
        ),
        in_specs=[pl.BlockSpec(memory_space=pltpu.SMEM)] + [vmem] * (len(traces) + 4),
        out_specs=(
            pl.BlockSpec((group * stations, lags), lambda i: (i, 0)),
            pl.BlockSpec((1, 1, group), lambda i: (i, 0, 0)),
        ),
        scratch_shapes=[
            pltpu.VMEM((events, stations, window), jnp.float32),
            pltpu.VMEM((events + 1, stations, LANES), jnp.float32),
            pltpu.VMEM((chunk * stations, window), jnp.bfloat16),
        ],
        compiler_params=pltpu.CompilerParams(vmem_limit_bytes=56 * 1024 * 1024),
        cost_estimate=pl.CostEstimate(flops=4_500_000_000, bytes_accessed=8_000_000, transcendentals=0),
    )(slots, *traces, presence, forward, inverse, weights)


def exchange(waveforms, sta_count, tables):
    events, stations, window = waveforms.shape
    share = stations // sta_count
    blocks = waveforms.reshape(events, sta_count, share, window)
    me = lax.axis_index("sta")
    half = sta_count // 2

    def for_station(i):
        return lax.dynamic_index_in_dim(blocks, i, axis=1, keepdims=False)

    def swap(piece, j):
        return lax.ppermute(piece, "sta", [(i, i ^ j) for i in range(sta_count)])

    later = [swap(for_station(me ^ j), j) for j in range(half, sta_count)]
    across = swap(jnp.stack([for_station(me ^ 2), for_station(me ^ 3)]), 2)
    beside = swap(jnp.concatenate([for_station(me ^ 1), across[1]], axis=0), 1)
    later[3], tables = lax.optimization_barrier((later[3], tables))
    tables = bring_call(tables)
    pieces = [for_station(me), beside[:events], across[0], beside[events:]] + later
    rows = half * events * share
    near = jnp.concatenate(pieces[:half], axis=0).reshape(rows, window)
    far = jnp.concatenate(pieces[half:], axis=0).reshape(rows, window)
    return near, far, tables


def exchange_whole(waveforms):
    window = waveforms.shape[2]
    arrived = lax.all_to_all(waveforms, "sta", split_axis=1, concat_axis=0, tiled=True)
    arrived = arrived.reshape(-1, window)
    half = arrived.shape[0] // 2
    count = lax.axis_size("evt")
    down = [(i, i - 1) for i in range(1, count)]
    up = [(i, i + 1) for i in range(count - 1)]
    next_low = lax.ppermute(arrived[:half], "evt", down)
    last_high = lax.ppermute(arrived[half:], "evt", up)
    return arrived, next_low, last_high


def triangle(count):
    return count * (count + 1) // 2


def own_list(block):
    band = block // 2
    return [(x, y) for x in range(block) for y in range(x + 1, min(x + band, block - 1) + 1)]


class Rows:
    def __init__(self, block):
        self.own = len(own_list(block))
        self.zero = 2 * self.own
        self.first = self.zero + 8
        self.second = self.first + triangle(block // 2)
        self.end = self.second + triangle(block // 2)
        self.lanes = -(-self.end // LANES) * LANES


def cross_spectra(first, second):
    half = first.shape[1] // 2
    ra, ia = first[:, :half], first[:, half:]
    rb, ib = second[:, :half], second[:, half:]
    return jnp.concatenate([ra * rb + ia * ib, ra * ib - ia * rb], axis=1)


def scaled_spectra(spectra_ref, me, each, place, presence_ref, present, weights_ref, spec_ref):
    stations, window = spec_ref.shape[1:]
    events = spectra_ref.shape[0] // stations
    pieces = events // each
    rounded = spectra_ref[...].astype(jnp.float32)
    energy = jnp.sum(jnp.square(rounded) * weights_ref[...], axis=1, keepdims=True) + 1e-06
    gain = jnp.broadcast_to(lax.rsqrt(energy), (events * stations, LANES)).reshape(events, stations, LANES)
    rounded = rounded.reshape(events, stations, window)
    for j in range(pieces):
        shift = ((me ^ j) & (pieces - 1)) * each
        piece = slice(j * each, (j + 1) * each)
        scale = gain[piece] * presence_ref[pl.ds(present + shift, each)]
        scale = jnp.concatenate([scale] * (window // LANES), axis=2)
        spec_ref[pl.ds(place + shift, each)] = rounded[piece] * scale


def build(lhs_ref, low, pairs, first_of, second_of):
    for i in range(0, len(pairs), 2):
        both = [cross_spectra(first_of(x), second_of(y)) for x, y in pairs[i:i + 2]]
        rows = 2 * both[0].shape[0]
        lhs_ref[pl.ds((low + i) * rows // 2, rows), :] = jnp.concatenate(both, axis=0).astype(jnp.bfloat16)


def keep(table_ref, peaks, values, row):
    stations, lags = table_ref.shape[1:]
    lane = lax.broadcasted_iota(jnp.int32, (stations, LANES), 1)
    count = values.shape[0] // stations
    for i in range(count):
        top = jnp.max(values[i * stations:(i + 1) * stations], axis=1, keepdims=True)
        at, within = divmod(row + i, LANES)
        peaks[at] = jnp.where(lane == within, top, peaks[at])
    table_ref[pl.ds(row, count)] = values.reshape(count, stations, lags).astype(jnp.bfloat16)


def no_peaks(rows, stations):
    return [jnp.zeros((stations, LANES), jnp.float32) for _ in range(rows.lanes // LANES)]


def prepare_kernel(
    block, packed_ref, row_ref, count_ref, held_ref,
):
    place = lax.axis_index("evt")
    start = place * block
    lines = row_ref.shape[0]

    def stacked(line):
        return jnp.concatenate(
            [packed_ref[line:line + 1, i * LANES:(i + 1) * LANES] for i in range(lines)], axis=0
        )

    first, second, valid = stacked(0), stacked(1), stacked(2)
    rows = Rows(block)
    row = table_row(first - start, second - start, place, block, rows)
    row = jnp.where(valid > 0, row, rows.zero)
    row_ref[...] = jnp.clip(row, 0, rows.end - 1)

    presence = packed_ref[3:, :LANES]
    stations, events = presence.shape
    bits = jnp.zeros((1, events), jnp.int32)
    for s in range(stations):
        bits = bits + presence[s:s + 1] * (1 << s)
    bits = jnp.broadcast_to(bits, (lines, events))
    both = jnp.take_along_axis(bits, first, axis=1) & jnp.take_along_axis(bits, second, axis=1)
    count = jnp.zeros_like(both)
    for s in range(stations):
        count = count + (lax.shift_right_logical(both, s) & 1)
    count_ref[...] = (count * valid).astype(jnp.float32)

    lane = lax.broadcasted_iota(jnp.int32, presence.shape, 1)
    present = presence.astype(jnp.float32)
    for i in range(held_ref.shape[0]):
        mine = jnp.where(lane == start - block // 2 + i, present, 0.0)
        held_ref[i] = jnp.broadcast_to(jnp.sum(mine, axis=1, keepdims=True), (stations, LANES))


def bring_kernel(tables_ref, tables_out, sem):
    copy = pltpu.make_async_copy(tables_ref, tables_out, sem)
    copy.start()
    copy.wait()


def spectra_kernel(near_ref, far_ref, tables_ref, near_out, far_out):
    window = tables_ref.shape[0]
    traces = jnp.concatenate([near_ref[...], far_ref[...]], axis=0)
    result = jnp.dot(traces, tables_ref[:, :window], preferred_element_type=jnp.float32).astype(jnp.bfloat16)
    near_out[...] = result[:near_ref.shape[0]]
    far_out[...] = result[near_ref.shape[0]:]


def own_pairs(spec_ref, tables_ref, table_ref, peaks, lhs_ref):
    block, stations, window = spec_ref.shape
    half = window // 2
    pairs = own_list(block)
    chunk = 64
    for low in range(0, len(pairs), chunk):
        some = pairs[low:low + chunk]
        held = {x: spec_ref[x] for x, _ in some}
        build(lhs_ref, low, some, lambda x: held[x], lambda y: spec_ref[y])
        rows = pl.ds(low * stations, len(some) * stations)
        even = jnp.dot(lhs_ref[rows, :half], tables_ref[:half, window:], preferred_element_type=jnp.float32)
        odd = jnp.dot(lhs_ref[rows, half:], tables_ref[half:, window:], preferred_element_type=jnp.float32)
        keep(table_ref, peaks, even + odd, low)
        keep(table_ref, peaks, even - odd, len(pairs) + low)


def halo_pairs(high, own_ref, spec_ref, tables_ref, table_ref, peaks, lhs_ref, row):
    band, stations, window = spec_ref.shape

    def own(u):
        return own_ref[jnp.where(high, band + u, band - 1 - u)]

    def other(h):
        return spec_ref[jnp.where(high, h, band - 1 - h)]

    pairs = [(u, h) for u in range(band) for h in range(u + 1)]
    chunk = 68
    for low in range(0, len(pairs), chunk):
        some = pairs[low:low + chunk]
        held = {u: own(u) for u, _ in some}
        build(lhs_ref, low, some, lambda u: held[u], other)
        rows = pl.ds(low * stations, len(some) * stations)
        lagged = jnp.dot(lhs_ref[rows, :], tables_ref[:, window:], preferred_element_type=jnp.float32)
        keep(table_ref, peaks, lagged, row + low)


def own_kernel(
    each, near_ref, far_ref, presence_ref, tables_ref, weights_ref,
    spec_ref, table_ref, peak_ref, lhs_ref,
):
    block, stations, window = spec_ref.shape
    band = block // 2
    me = lax.axis_index("sta")
    mine = jnp.where(me * each < band, 0, band)
    for ref, place in ((near_ref, mine), (far_ref, band - mine)):
        scaled_spectra(
            ref, me, each, place, presence_ref, band + place, weights_ref, spec_ref
        )
    rows = Rows(block)
    peaks = no_peaks(rows, stations)
    own_pairs(spec_ref, tables_ref, table_ref, peaks, lhs_ref)
    table_ref[rows.zero] = jnp.zeros(table_ref.shape[1:], table_ref.dtype)
    peak_ref[...] = jnp.concatenate(peaks, axis=1)


def middle_kernel(
    each, halo_ref, own_ref, presence_ref, tables_ref, weights_ref, own_peak_ref,
    held_table_ref, table_ref, peak_ref, other_ref, lhs_ref,
):
    del held_table_ref
    block, stations, window = own_ref.shape
    band = block // 2
    me = lax.axis_index("sta")
    high = lax.axis_index("evt") % 2 == 0
    edge = jnp.where(high, 3 * band, 0)
    scaled_spectra(halo_ref, me, each, 0, presence_ref, edge, weights_ref, other_ref)
    rows = Rows(block)
    peaks = no_peaks(rows, stations)
    halo_pairs(high, own_ref, other_ref, tables_ref, table_ref, peaks, lhs_ref, rows.first)
    peak_ref[...] = own_peak_ref[...] + jnp.concatenate(peaks, axis=1)


def last_kernel(
    each, halo_ref, own_ref, presence_ref, tables_ref, weights_ref, peak_ref, row_ref, count_ref,
    held_table_ref, table_ref, sums_ref, other_ref, lhs_ref,
):
    del held_table_ref
    block, stations, window = own_ref.shape
    band = block // 2
    me = lax.axis_index("sta")
    high = lax.axis_index("evt") % 2 == 1
    edge = jnp.where(high, 3 * band, 0)
    scaled_spectra(halo_ref, me, each, 0, presence_ref, edge, weights_ref, other_ref)
    rows = Rows(block)
    peaks = no_peaks(rows, stations)
    halo_pairs(high, own_ref, other_ref, tables_ref, table_ref, peaks, lhs_ref, rows.second)
    row = row_ref[...]
    lanes = row & (LANES - 1)
    total = jnp.zeros(row.shape, jnp.float32)
    for at, late in enumerate(peaks):
        line = jnp.sum(peak_ref[:, at * LANES:(at + 1) * LANES] + late, axis=0, keepdims=True)
        picked = jnp.take_along_axis(jnp.broadcast_to(line, row.shape), lanes, axis=1)
        total = jnp.where(lax.shift_right_logical(row, 7) == at, picked, total)
    sums_ref[0] = total
    sums_ref[1] = count_ref[...]


def pick_kernel(start, group, row_ref, table_ref, *refs):
    out_ref, picked_ref, sems = refs[-3:]
    copies = []
    for low in range(0, picked_ref.shape[0], group):
        for i in range(low, low + group):
            picked_ref[i] = table_ref[row_ref[start + i]]
        copies.append(pltpu.make_async_copy(
            picked_ref.at[pl.ds(low, group)], out_ref.at[pl.ds(start + low, group)], sems.at[low // group]
        ))
        copies[-1].start()
    for copy in copies:
        copy.wait()


VMEM = pl.BlockSpec(memory_space=pltpu.VMEM)
SMEM = pl.BlockSpec(memory_space=pltpu.SMEM)
PARAMS = pltpu.CompilerParams(vmem_limit_bytes=20 * 1024 * 1024)


def cost(rows, lags, window, traces, moved):
    return pl.CostEstimate(
        flops=2 * window * (rows * lags + traces * window), bytes_accessed=moved, transcendentals=0
    )


def prepare_call(pair_events, pair_valid, presence, block):
    pairs = pair_events.shape[0]
    events, stations = presence.shape
    packed = jnp.concatenate(
        [pair_events.T, pair_valid[None], jnp.pad(presence.T, ((0, 0), (0, pairs - events)))], axis=0
    )
    line = (pairs // LANES, LANES)
    return pl.pallas_call(
        functools.partial(prepare_kernel, block),
        out_shape=(
            jax.ShapeDtypeStruct(line, jnp.int32),
            jax.ShapeDtypeStruct(line, jnp.float32),
            jax.ShapeDtypeStruct((2 * block, stations, LANES), jnp.float32),
        ),
        in_specs=[VMEM],
        out_specs=(VMEM,) * 3,
        compiler_params=PARAMS,
        cost_estimate=pl.CostEstimate(flops=1_000_000, bytes_accessed=1_000_000, transcendentals=0),
    )(packed)


def bring_call(tables):
    return pl.pallas_call(
        bring_kernel,
        out_shape=jax.ShapeDtypeStruct(tables.shape, tables.dtype),
        in_specs=[pl.BlockSpec(memory_space=pl.ANY)],
        out_specs=VMEM,
        scratch_shapes=[pltpu.SemaphoreType.DMA],
        compiler_params=PARAMS,
        cost_estimate=pl.CostEstimate(flops=0, bytes_accessed=5_000_000, transcendentals=0),
    )(tables)


def spectra_call(near, far, tables):
    return pl.pallas_call(
        spectra_kernel,
        out_shape=tuple(jax.ShapeDtypeStruct(x.shape, x.dtype) for x in (near, far)),
        in_specs=[VMEM] * 3,
        out_specs=(VMEM,) * 2,
        compiler_params=PARAMS,
        cost_estimate=cost(0, 0, near.shape[1], 2 * near.shape[0], 3_000_000),
    )(near, far, tables)


def own_call(near, far, presence, tables, each, block):
    table_of, weights = tables
    window = table_of.shape[0]
    lags = table_of.shape[1] - window
    stations = presence.shape[1]
    rows = Rows(block)
    return pl.pallas_call(
        functools.partial(own_kernel, each),
        out_shape=(
            jax.ShapeDtypeStruct((block, stations, window), jnp.float32),
            jax.ShapeDtypeStruct((rows.end, stations, lags), jnp.bfloat16),
            jax.ShapeDtypeStruct((stations, rows.lanes), jnp.float32),
        ),
        in_specs=[VMEM] * 5,
        out_specs=(VMEM,) * 3,
        scratch_shapes=[pltpu.VMEM((rows.own * stations, window), jnp.bfloat16)],
        compiler_params=PARAMS,
        cost_estimate=cost(rows.own * stations, lags, window, near.shape[0] * 2, 8_000_000),
    )(near, far, presence, table_of, weights)


def middle_call(halo, own, presence, tables, peaks, table, each):
    table_of, weights = tables
    window = table_of.shape[0]
    lags = table_of.shape[1] - window
    block, stations = own.shape[:2]
    pairs = triangle(block // 2)
    return pl.pallas_call(
        functools.partial(middle_kernel, each),
        out_shape=(
            jax.ShapeDtypeStruct(table.shape, table.dtype),
            jax.ShapeDtypeStruct(peaks.shape, peaks.dtype),
        ),
        in_specs=[VMEM] * 7,
        out_specs=(VMEM,) * 2,
        scratch_shapes=[
            pltpu.VMEM((block // 2, stations, window), jnp.float32),
            pltpu.VMEM((pairs * stations, window), jnp.bfloat16),
        ],
        input_output_aliases={6: 0},
        compiler_params=PARAMS,
        cost_estimate=cost(pairs * stations, lags, window, halo.shape[0], 4_000_000),
    )(halo, own, presence, table_of, weights, peaks, table)


def last_call(halo, own, presence, tables, peaks, row, count, table, each):
    table_of, weights = tables
    window = table_of.shape[0]
    lags = table_of.shape[1] - window
    block, stations = own.shape[:2]
    pairs = triangle(block // 2)
    return pl.pallas_call(
        functools.partial(last_kernel, each),
        out_shape=(
            jax.ShapeDtypeStruct(table.shape, table.dtype),
            jax.ShapeDtypeStruct((2,) + row.shape, jnp.float32),
        ),
        in_specs=[VMEM] * 9,
        out_specs=(VMEM,) * 2,
        scratch_shapes=[
            pltpu.VMEM((block // 2, stations, window), jnp.float32),
            pltpu.VMEM((pairs * stations, window), jnp.bfloat16),
        ],
        input_output_aliases={8: 0},
        compiler_params=PARAMS,
        cost_estimate=cost(pairs * stations, lags, window, halo.shape[0], 4_000_000),
    )(halo, own, presence, table_of, weights, peaks, row, count, table)


def pick_call(row, table, held, start, count):
    group = 64
    anywhere = pl.BlockSpec(memory_space=pl.ANY)
    return pl.pallas_call(
        functools.partial(pick_kernel, start, group),
        out_shape=jax.ShapeDtypeStruct(row.shape + table.shape[1:], table.dtype),
        in_specs=[SMEM, VMEM] + [anywhere] * len(held),
        out_specs=anywhere,
        scratch_shapes=[
            pltpu.VMEM((count,) + table.shape[1:], table.dtype),
            pltpu.SemaphoreType.DMA((count // group,)),
        ],
        input_output_aliases={2: 0} if held else {},
        compiler_params=PARAMS,
        cost_estimate=pl.CostEstimate(flops=0, bytes_accessed=count * 20_000, transcendentals=0),
    )(row, table, *held)


def table_row(first, second, place, block, rows):
    band = block // 2
    low, apart = jnp.minimum(first, second), jnp.abs(first - second)
    past = jnp.maximum(low - band, 0)
    index = jnp.minimum(low, band) * band + past * (band - 1) - (past * (past - 1) >> 1) + apart - 1
    inside = jnp.where(second > first, index, rows.own + index)
    high = second >= block
    u = jnp.where(high, first - band, band - 1 - first)
    h = jnp.where(high, second - block, -1 - second)
    outside = jnp.where(jnp.where(high, 1, 0) == place % 2, rows.second, rows.first) + (u * (u + 1) >> 1) + h
    return jnp.where(high | (second < 0), outside, inside)


def banded(waveforms, pair_events, pair_valid, presence, block):
    each = waveforms.shape[0]
    forward, inverse, weights = spectral_tables(waveforms.shape[2], LAGS)
    tables = (jnp.asarray(np.concatenate([forward, inverse], axis=1)), jnp.asarray(weights))
    near, far, brought = exchange(waveforms, lax.axis_size("sta"), tables[0])
    ready = prepare_call(pair_events, pair_valid, presence, block)
    far, ready, brought = lax.optimization_barrier((far, ready, brought))
    tables = (brought, tables[1])
    near, far = spectra_call(near, far, brought)
    me, place = lax.axis_index("sta"), lax.axis_index("evt")
    count = lax.axis_size("evt")
    inward = (place % 2 == 0) == (me * each < block // 2)

    def swapped(half, odd):
        links = [(i, i + 1) for i in range(odd, count - 1, 2)]
        return lax.ppermute(half, "evt", links + [(j, i) for i, j in links])

    first_halo = swapped(jnp.where(inward, far, near), 0)
    second_halo = swapped(jnp.where(inward, near, far), 1)
    row, count, held = ready
    own, table, peaks = own_call(near, far, held, tables, each, block)
    table, peaks = middle_call(first_halo, own, held, tables, peaks, table, each)
    table, sums = last_call(second_halo, own, held, tables, peaks, row, count, table, each)

    row = row.reshape(-1)
    sta_count = lax.axis_size("sta")

    def from_station(j):
        return lax.ppermute(sums, "sta", [(i, i ^ j) for i in range(sta_count)])

    split = row.shape[0] * 4 // 8
    beside, across, aslant = from_station(1), from_station(2), from_station(3)
    correlation = pick_call(row, table, (), 0, split)
    sums, correlation = lax.optimization_barrier(((sums + beside) + (across + aslant), correlation))
    arrived = from_station(4)
    correlation = pick_call(row, table, (correlation,), split, row.shape[0] - split)
    return correlation, sums + arrived


def by_slot(waveforms, pair_events, pair_valid, presence, block):
    share = presence.shape[1]
    start = lax.axis_index("evt") * block
    traces = exchange_whole(waveforms)
    place = pair_events - start
    slot = jnp.where((place >= 0) & (place < block), 0, block) + place % block
    gained = jnp.where(pair_valid > 0, slot[:, 0], 2 * block)
    slots = jnp.stack([slot[:, 0], slot[:, 1], gained]).astype(jnp.int32)
    held = jnp.arange(2 * block, dtype=jnp.int32)
    held = jnp.where(held < block, held, jnp.where(held < block + block // 2, held, held - 2 * block))
    held = jnp.clip(start + held, 0, presence.shape[0] - 1)
    slot_presence = jnp.broadcast_to(
        jnp.take(presence.astype(jnp.float32), held, axis=0)[:, :, None], (2 * block, share, LANES)
    )
    few = presence.astype(jnp.bfloat16)
    event = jnp.arange(presence.shape[0], dtype=jnp.int32)
    first, second = (
        jnp.dot((pair_events[:, i:i + 1] == event).astype(jnp.bfloat16), few, preferred_element_type=jnp.float32)
        for i in (0, 1)
    )
    counts = jnp.sum(first * second, axis=1) * pair_valid.astype(jnp.float32)
    tables = tuple(jnp.asarray(x) for x in spectral_tables(waveforms.shape[2], LAGS))
    correlation, peaks = pair_call(slots, traces, slot_presence, tables)
    sums = lax.psum(jnp.stack([peaks.reshape(-1), counts]), "sta")
    return correlation.reshape(-1, share, correlation.shape[1]), sums


def body(waveforms, pair_events, pair_valid, presence):
    sta_count = lax.axis_size("sta")
    local_events, stations, window = waveforms.shape
    block = sta_count * local_events
    args = (waveforms, pair_events, pair_valid, presence, block)
    dense = sta_count == 8 and presence.shape[0] == LANES and block * block <= pair_events.shape[0]
    correlation, sums = (banded if dense else by_slot)(*args)
    pair_peak = sums[0] / jnp.maximum(sums[1], 1.0)
    return correlation, pair_peak.reshape(-1)


def solution(mesh):
    return jax.shard_map(
        body,
        mesh=mesh,
        in_specs=(P(("evt", "sta"), None, None), P("evt", None), P("evt"), P(None, "sta")),
        out_specs=(P("evt", "sta", None), P("evt")),
        check_vma=False,
    )
```

```python
import functools
import math

import jax
import jax.numpy as jnp
import numpy as np
from jax import lax
from jax.experimental import pallas as pl
from jax.experimental.pallas import tpu as pltpu
from jax.sharding import PartitionSpec as P

LAGS = 256
LANES = 128


def spectral_tables(window, lag_count):
    half = window // 2
    sample = np.arange(window, dtype=np.int64)
    bins = np.arange(half, dtype=np.int64)
    angle = (sample[:, None] * bins[None, :] % window) * (2.0 * math.pi / window)
    forward = np.concatenate([np.cos(angle), -np.sin(angle)], axis=1) / math.sqrt(window)
    shifts = np.arange(lag_count, dtype=np.int64) - lag_count // 2
    lag_angle = (bins[:, None] * shifts[None, :] % window) * (2.0 * math.pi / window)
    factor = np.where(bins == 0, 1.0, 2.0)[:, None]
    inverse = np.concatenate([factor * np.cos(lag_angle), -factor * np.sin(lag_angle)], axis=0)
    weights = np.concatenate([factor[:, 0], factor[:, 0]])[None, :]
    return forward.astype(jnp.bfloat16), inverse.astype(jnp.bfloat16), weights.astype(np.float32)


def pair_kernel(
    group, chunk, parts, slots_ref, *refs
):
    traces = refs[:parts]
    (
        presence_ref, forward_ref, inverse_ref, weights_ref,
        out_ref, peak_ref,
        spec_ref, gain_ref, lhs_ref,
    ) = refs[parts:]
    stations, window = spec_ref.shape[1:]
    half = window // 2
    events = spec_ref.shape[0]

    @pl.when(pl.program_id(0) == 0)
    def _():
        start = 0
        for ref in traces:
            rows = ref.shape[0]
            count = rows // stations
            result = jnp.dot(ref[...], forward_ref[...], preferred_element_type=jnp.float32)
            rounded = result.astype(jnp.bfloat16).astype(jnp.float32)
            spec_ref[pl.ds(start, count)] = rounded.reshape(count, stations, window)
            power = jnp.square(rounded) * weights_ref[...]
            energy = jnp.sum(power, axis=1, keepdims=True) + 1e-06
            gain = jnp.broadcast_to(lax.rsqrt(energy), (rows, LANES))
            gain = gain.reshape(count, stations, LANES) * presence_ref[pl.ds(start, count)]
            gain_ref[pl.ds(start, count)] = gain
            start += count
        gain_ref[events] = jnp.zeros((stations, LANES), jnp.float32)

    base = pl.program_id(0) * group
    lane = lax.broadcasted_iota(jnp.int32, (stations, LANES), 1)

    def cross(pair):
        first = spec_ref[slots_ref[0, pair]]
        second = spec_ref[slots_ref[1, pair]]
        ra, ia = first[:, :half], first[:, half:]
        rb, ib = second[:, :half], second[:, half:]
        return jnp.concatenate([ra * rb + ia * ib, ra * ib - ia * rb], axis=1)

    def one_chunk(index, peaks):
        first_pair = base + index * chunk
        for j in range(0, chunk, 2):
            both = jnp.concatenate([cross(first_pair + j), cross(first_pair + j + 1)], axis=0)
            lhs_ref[pl.ds(j * stations, 2 * stations), :] = both.astype(jnp.bfloat16)
        lagged = jnp.dot(lhs_ref[...], inverse_ref[...], preferred_element_type=jnp.float32)
        for j in range(0, chunk, 2):
            rows = []
            for i in (j, j + 1):
                pair = first_pair + i
                gain = gain_ref[slots_ref[2, pair]] * gain_ref[slots_ref[1, pair]]
                scaled = lagged[i * stations:(i + 1) * stations] * jnp.concatenate([gain, gain], axis=1)
                rows.append(scaled)
                top = jnp.max(scaled, axis=1, keepdims=True)
                peaks = jnp.where(lane == index * chunk + i, top, peaks)
            block = jnp.concatenate(rows, axis=0).astype(jnp.bfloat16)
            start = pl.multiple_of(index * chunk * stations, chunk * stations) + j * stations
            out_ref[pl.ds(start, 2 * stations), :] = block
        return peaks

    peaks = lax.fori_loop(0, group // chunk, one_chunk, jnp.zeros((stations, LANES), jnp.float32))
    peak_ref[0] = jnp.sum(peaks, axis=0, keepdims=True)


def pair_call(slots, traces, presence, tables):
    forward, inverse, weights = tables
    window = forward.shape[0]
    lags = inverse.shape[1]
    pairs = slots.shape[1]
    events, stations = presence.shape[:2]
    group = LANES
    chunk = 32
    vmem = pl.BlockSpec(memory_space=pltpu.VMEM)
    return pl.pallas_call(
        functools.partial(pair_kernel, group, chunk, len(traces)),
        grid=(pairs // group,),
        out_shape=(
            jax.ShapeDtypeStruct((pairs * stations, lags), jnp.bfloat16),
            jax.ShapeDtypeStruct((pairs // group, 1, group), jnp.float32),
        ),
        in_specs=[pl.BlockSpec(memory_space=pltpu.SMEM)] + [vmem] * (len(traces) + 4),
        out_specs=(
            pl.BlockSpec((group * stations, lags), lambda i: (i, 0)),
            pl.BlockSpec((1, 1, group), lambda i: (i, 0, 0)),
        ),
        scratch_shapes=[
            pltpu.VMEM((events, stations, window), jnp.float32),
            pltpu.VMEM((events + 1, stations, LANES), jnp.float32),
            pltpu.VMEM((chunk * stations, window), jnp.bfloat16),
        ],
        compiler_params=pltpu.CompilerParams(vmem_limit_bytes=56 * 1024 * 1024),
        cost_estimate=pl.CostEstimate(flops=4_500_000_000, bytes_accessed=8_000_000, transcendentals=0),
    )(slots, *traces, presence, forward, inverse, weights)


def exchange(waveforms, sta_count, tables):
    events, stations, window = waveforms.shape
    share = stations // sta_count
    blocks = waveforms.reshape(events, sta_count, share, window)
    me = lax.axis_index("sta")
    half = sta_count // 2

    def for_station(i):
        return lax.dynamic_index_in_dim(blocks, i, axis=1, keepdims=False)

    def swap(piece, j):
        return lax.ppermute(piece, "sta", [(i, i ^ j) for i in range(sta_count)])

    later = [swap(for_station(me ^ j), j) for j in range(half, sta_count)]
    across = swap(jnp.stack([for_station(me ^ 2), for_station(me ^ 3)]), 2)
    beside = swap(jnp.concatenate([for_station(me ^ 1), across[1]], axis=0), 1)
    later[3], tables = lax.optimization_barrier((later[3], tables))
    tables = bring_call(tables)
    pieces = [for_station(me), beside[:events], across[0], beside[events:]] + later
    rows = half * events * share
    near = jnp.concatenate(pieces[:half], axis=0).reshape(rows, window)
    far = jnp.concatenate(pieces[half:], axis=0).reshape(rows, window)
    return near, far, tables


def exchange_whole(waveforms):
    window = waveforms.shape[2]
    arrived = lax.all_to_all(waveforms, "sta", split_axis=1, concat_axis=0, tiled=True)
    arrived = arrived.reshape(-1, window)
    half = arrived.shape[0] // 2
    count = lax.axis_size("evt")
    down = [(i, i - 1) for i in range(1, count)]
    up = [(i, i + 1) for i in range(count - 1)]
    next_low = lax.ppermute(arrived[:half], "evt", down)
    last_high = lax.ppermute(arrived[half:], "evt", up)
    return arrived, next_low, last_high


def triangle(count):
    return count * (count + 1) // 2


def own_list(block):
    band = block // 2
    return [(x, y) for x in range(block) for y in range(x + 1, min(x + band, block - 1) + 1)]


class Rows:
    def __init__(self, block):
        self.own = len(own_list(block))
        self.zero = 2 * self.own
        self.first = self.zero + 8
        self.second = self.first + triangle(block // 2)
        self.end = self.second + triangle(block // 2)
        self.lanes = -(-self.end // LANES) * LANES


def cross_spectra(first, second):
    half = first.shape[1] // 2
    ra, ia = first[:, :half], first[:, half:]
    rb, ib = second[:, :half], second[:, half:]
    return jnp.concatenate([ra * rb + ia * ib, ra * ib - ia * rb], axis=1)


def scaled_spectra(traces_ref, me, each, place, presence_ref, present, tables_ref, weights_ref, spec_ref):
    stations, window = spec_ref.shape[1:]
    events = traces_ref.shape[0] // stations
    pieces = events // each
    result = jnp.dot(traces_ref[...], tables_ref[:, :window], preferred_element_type=jnp.float32)
    rounded = result.astype(jnp.bfloat16).astype(jnp.float32)
    energy = jnp.sum(jnp.square(rounded) * weights_ref[...], axis=1, keepdims=True) + 1e-06
    gain = jnp.broadcast_to(lax.rsqrt(energy), (events * stations, LANES)).reshape(events, stations, LANES)
    rounded = rounded.reshape(events, stations, window)
    for j in range(pieces):
        shift = ((me ^ j) & (pieces - 1)) * each
        piece = slice(j * each, (j + 1) * each)
        scale = gain[piece] * presence_ref[pl.ds(present + shift, each)]
        scale = jnp.concatenate([scale] * (window // LANES), axis=2)
        spec_ref[pl.ds(place + shift, each)] = rounded[piece] * scale


def build(lhs_ref, low, pairs, first_of, second_of):
    for i in range(0, len(pairs), 2):
        both = [cross_spectra(first_of(x), second_of(y)) for x, y in pairs[i:i + 2]]
        rows = 2 * both[0].shape[0]
        lhs_ref[pl.ds((low + i) * rows // 2, rows), :] = jnp.concatenate(both, axis=0).astype(jnp.bfloat16)


def keep(table_ref, peaks, values, row):
    stations, lags = table_ref.shape[1:]
    lane = lax.broadcasted_iota(jnp.int32, (stations, LANES), 1)
    count = values.shape[0] // stations
    for i in range(count):
        top = jnp.max(values[i * stations:(i + 1) * stations], axis=1, keepdims=True)
        at, within = divmod(row + i, LANES)
        peaks[at] = jnp.where(lane == within, top, peaks[at])
    table_ref[pl.ds(row, count)] = values.reshape(count, stations, lags).astype(jnp.bfloat16)


def no_peaks(rows, stations):
    return [jnp.zeros((stations, LANES), jnp.float32) for _ in range(rows.lanes // LANES)]


def prepare_kernel(
    block, packed_ref, row_ref, count_ref, held_ref,
):
    place = lax.axis_index("evt")
    start = place * block
    lines = row_ref.shape[0]

    def stacked(line):
        return jnp.concatenate(
            [packed_ref[line:line + 1, i * LANES:(i + 1) * LANES] for i in range(lines)], axis=0
        )

    first, second, valid = stacked(0), stacked(1), stacked(2)
    rows = Rows(block)
    row = table_row(first - start, second - start, place, block, rows)
    row = jnp.where(valid > 0, row, rows.zero)
    row_ref[...] = jnp.clip(row, 0, rows.end - 1)

    presence = packed_ref[3:, :LANES]
    stations, events = presence.shape
    bits = jnp.zeros((1, events), jnp.int32)
    for s in range(stations):
        bits = bits + presence[s:s + 1] * (1 << s)
    bits = jnp.broadcast_to(bits, (lines, events))
    both = jnp.take_along_axis(bits, first, axis=1) & jnp.take_along_axis(bits, second, axis=1)
    count = jnp.zeros_like(both)
    for s in range(stations):
        count = count + (lax.shift_right_logical(both, s) & 1)
    count_ref[...] = (count * valid).astype(jnp.float32)

    lane = lax.broadcasted_iota(jnp.int32, presence.shape, 1)
    present = presence.astype(jnp.float32)
    for i in range(held_ref.shape[0]):
        mine = jnp.where(lane == start - block // 2 + i, present, 0.0)
        held_ref[i] = jnp.broadcast_to(jnp.sum(mine, axis=1, keepdims=True), (stations, LANES))


def bring_kernel(tables_ref, tables_out, sem):
    copy = pltpu.make_async_copy(tables_ref, tables_out, sem)
    copy.start()
    copy.wait()


def own_pairs(spec_ref, tables_ref, table_ref, peaks, lhs_ref):
    block, stations, window = spec_ref.shape
    half = window // 2
    pairs = own_list(block)
    chunk = 64
    for low in range(0, len(pairs), chunk):
        some = pairs[low:low + chunk]
        held = {x: spec_ref[x] for x, _ in some}
        build(lhs_ref, low, some, lambda x: held[x], lambda y: spec_ref[y])
        rows = pl.ds(low * stations, len(some) * stations)
        even = jnp.dot(lhs_ref[rows, :half], tables_ref[:half, window:], preferred_element_type=jnp.float32)
        odd = jnp.dot(lhs_ref[rows, half:], tables_ref[half:, window:], preferred_element_type=jnp.float32)
        keep(table_ref, peaks, even + odd, low)
        keep(table_ref, peaks, even - odd, len(pairs) + low)


def halo_pairs(high, own_ref, spec_ref, tables_ref, table_ref, peaks, lhs_ref, row):
    band, stations, window = spec_ref.shape

    def own(u):
        return own_ref[jnp.where(high, band + u, band - 1 - u)]

    def other(h):
        return spec_ref[jnp.where(high, h, band - 1 - h)]

    pairs = [(u, h) for u in range(band) for h in range(u + 1)]
    chunk = 68
    for low in range(0, len(pairs), chunk):
        some = pairs[low:low + chunk]
        held = {u: own(u) for u, _ in some}
        build(lhs_ref, low, some, lambda u: held[u], other)
        rows = pl.ds(low * stations, len(some) * stations)
        lagged = jnp.dot(lhs_ref[rows, :], tables_ref[:, window:], preferred_element_type=jnp.float32)
        keep(table_ref, peaks, lagged, row + low)


def own_kernel(
    each, near_ref, far_ref, presence_ref, tables_ref, weights_ref,
    spec_ref, table_ref, peak_ref, lhs_ref,
):
    block, stations, window = spec_ref.shape
    band = block // 2
    me = lax.axis_index("sta")
    mine = jnp.where(me * each < band, 0, band)
    for ref, place in ((near_ref, mine), (far_ref, band - mine)):
        scaled_spectra(
            ref, me, each, place, presence_ref, band + place, tables_ref, weights_ref, spec_ref
        )
    rows = Rows(block)
    peaks = no_peaks(rows, stations)
    own_pairs(spec_ref, tables_ref, table_ref, peaks, lhs_ref)
    table_ref[rows.zero] = jnp.zeros(table_ref.shape[1:], table_ref.dtype)
    peak_ref[...] = jnp.concatenate(peaks, axis=1)


def middle_kernel(
    each, halo_ref, own_ref, presence_ref, tables_ref, weights_ref, own_peak_ref,
    held_table_ref, table_ref, peak_ref, other_ref, lhs_ref,
):
    del held_table_ref
    block, stations, window = own_ref.shape
    band = block // 2
    me = lax.axis_index("sta")
    high = lax.axis_index("evt") % 2 == 0
    edge = jnp.where(high, 3 * band, 0)
    scaled_spectra(halo_ref, me, each, 0, presence_ref, edge, tables_ref, weights_ref, other_ref)
    rows = Rows(block)
    peaks = no_peaks(rows, stations)
    halo_pairs(high, own_ref, other_ref, tables_ref, table_ref, peaks, lhs_ref, rows.first)
    peak_ref[...] = own_peak_ref[...] + jnp.concatenate(peaks, axis=1)


def last_kernel(
    each, halo_ref, own_ref, presence_ref, tables_ref, weights_ref, peak_ref, row_ref, count_ref,
    held_table_ref, table_ref, sums_ref, other_ref, lhs_ref,
):
    del held_table_ref
    block, stations, window = own_ref.shape
    band = block // 2
    me = lax.axis_index("sta")
    high = lax.axis_index("evt") % 2 == 1
    edge = jnp.where(high, 3 * band, 0)
    scaled_spectra(halo_ref, me, each, 0, presence_ref, edge, tables_ref, weights_ref, other_ref)
    rows = Rows(block)
    peaks = no_peaks(rows, stations)
    halo_pairs(high, own_ref, other_ref, tables_ref, table_ref, peaks, lhs_ref, rows.second)
    row = row_ref[...]
    lanes = row & (LANES - 1)
    total = jnp.zeros(row.shape, jnp.float32)
    for at, late in enumerate(peaks):
        line = jnp.sum(peak_ref[:, at * LANES:(at + 1) * LANES] + late, axis=0, keepdims=True)
        picked = jnp.take_along_axis(jnp.broadcast_to(line, row.shape), lanes, axis=1)
        total = jnp.where(lax.shift_right_logical(row, 7) == at, picked, total)
    sums_ref[0] = total
    sums_ref[1] = count_ref[...]


def pick_kernel(start, group, row_ref, table_ref, *refs):
    out_ref, picked_ref, sems = refs[-3:]
    copies = []
    for low in range(0, picked_ref.shape[0], group):
        for i in range(low, low + group):
            picked_ref[i] = table_ref[row_ref[start + i]]
        copies.append(pltpu.make_async_copy(
            picked_ref.at[pl.ds(low, group)], out_ref.at[pl.ds(start + low, group)], sems.at[low // group]
        ))
        copies[-1].start()
    for copy in copies:
        copy.wait()


VMEM = pl.BlockSpec(memory_space=pltpu.VMEM)
SMEM = pl.BlockSpec(memory_space=pltpu.SMEM)
PARAMS = pltpu.CompilerParams(vmem_limit_bytes=20 * 1024 * 1024)


def cost(rows, lags, window, traces, moved):
    return pl.CostEstimate(
        flops=2 * window * (rows * lags + traces * window), bytes_accessed=moved, transcendentals=0
    )


def prepare_call(pair_events, pair_valid, presence, block):
    pairs = pair_events.shape[0]
    events, stations = presence.shape
    packed = jnp.concatenate(
        [pair_events.T, pair_valid[None], jnp.pad(presence.T, ((0, 0), (0, pairs - events)))], axis=0
    )
    line = (pairs // LANES, LANES)
    return pl.pallas_call(
        functools.partial(prepare_kernel, block),
        out_shape=(
            jax.ShapeDtypeStruct(line, jnp.int32),
            jax.ShapeDtypeStruct(line, jnp.float32),
            jax.ShapeDtypeStruct((2 * block, stations, LANES), jnp.float32),
        ),
        in_specs=[VMEM],
        out_specs=(VMEM,) * 3,
        compiler_params=PARAMS,
        cost_estimate=pl.CostEstimate(flops=1_000_000, bytes_accessed=1_000_000, transcendentals=0),
    )(packed)


def bring_call(tables):
    return pl.pallas_call(
        bring_kernel,
        out_shape=jax.ShapeDtypeStruct(tables.shape, tables.dtype),
        in_specs=[pl.BlockSpec(memory_space=pl.ANY)],
        out_specs=VMEM,
        scratch_shapes=[pltpu.SemaphoreType.DMA],
        compiler_params=PARAMS,
        cost_estimate=pl.CostEstimate(flops=0, bytes_accessed=5_000_000, transcendentals=0),
    )(tables)


def own_call(near, far, presence, tables, each, block):
    table_of, weights = tables
    window = table_of.shape[0]
    lags = table_of.shape[1] - window
    stations = presence.shape[1]
    rows = Rows(block)
    return pl.pallas_call(
        functools.partial(own_kernel, each),
        out_shape=(
            jax.ShapeDtypeStruct((block, stations, window), jnp.float32),
            jax.ShapeDtypeStruct((rows.end, stations, lags), jnp.bfloat16),
            jax.ShapeDtypeStruct((stations, rows.lanes), jnp.float32),
        ),
        in_specs=[VMEM] * 5,
        out_specs=(VMEM,) * 3,
        scratch_shapes=[pltpu.VMEM((rows.own * stations, window), jnp.bfloat16)],
        compiler_params=PARAMS,
        cost_estimate=cost(rows.own * stations, lags, window, near.shape[0] * 2, 8_000_000),
    )(near, far, presence, table_of, weights)


def middle_call(halo, own, presence, tables, peaks, table, each):
    table_of, weights = tables
    window = table_of.shape[0]
    lags = table_of.shape[1] - window
    block, stations = own.shape[:2]
    pairs = triangle(block // 2)
    return pl.pallas_call(
        functools.partial(middle_kernel, each),
        out_shape=(
            jax.ShapeDtypeStruct(table.shape, table.dtype),
            jax.ShapeDtypeStruct(peaks.shape, peaks.dtype),
        ),
        in_specs=[VMEM] * 7,
        out_specs=(VMEM,) * 2,
        scratch_shapes=[
            pltpu.VMEM((block // 2, stations, window), jnp.float32),
            pltpu.VMEM((pairs * stations, window), jnp.bfloat16),
        ],
        input_output_aliases={6: 0},
        compiler_params=PARAMS,
        cost_estimate=cost(pairs * stations, lags, window, halo.shape[0], 4_000_000),
    )(halo, own, presence, table_of, weights, peaks, table)


def last_call(halo, own, presence, tables, peaks, row, count, table, each):
    table_of, weights = tables
    window = table_of.shape[0]
    lags = table_of.shape[1] - window
    block, stations = own.shape[:2]
    pairs = triangle(block // 2)
    return pl.pallas_call(
        functools.partial(last_kernel, each),
        out_shape=(
            jax.ShapeDtypeStruct(table.shape, table.dtype),
            jax.ShapeDtypeStruct((2,) + row.shape, jnp.float32),
        ),
        in_specs=[VMEM] * 9,
        out_specs=(VMEM,) * 2,
        scratch_shapes=[
            pltpu.VMEM((block // 2, stations, window), jnp.float32),
            pltpu.VMEM((pairs * stations, window), jnp.bfloat16),
        ],
        input_output_aliases={8: 0},
        compiler_params=PARAMS,
        cost_estimate=cost(pairs * stations, lags, window, halo.shape[0], 4_000_000),
    )(halo, own, presence, table_of, weights, peaks, row, count, table)


def pick_call(row, table, held, start, count):
    group = 64
    anywhere = pl.BlockSpec(memory_space=pl.ANY)
    return pl.pallas_call(
        functools.partial(pick_kernel, start, group),
        out_shape=jax.ShapeDtypeStruct(row.shape + table.shape[1:], table.dtype),
        in_specs=[SMEM, VMEM] + [anywhere] * len(held),
        out_specs=anywhere,
        scratch_shapes=[
            pltpu.VMEM((count,) + table.shape[1:], table.dtype),
            pltpu.SemaphoreType.DMA((count // group,)),
        ],
        input_output_aliases={2: 0} if held else {},
        compiler_params=PARAMS,
        cost_estimate=pl.CostEstimate(flops=0, bytes_accessed=count * 20_000, transcendentals=0),
    )(row, table, *held)


def table_row(first, second, place, block, rows):
    band = block // 2
    low, apart = jnp.minimum(first, second), jnp.abs(first - second)
    past = jnp.maximum(low - band, 0)
    index = jnp.minimum(low, band) * band + past * (band - 1) - (past * (past - 1) >> 1) + apart - 1
    inside = jnp.where(second > first, index, rows.own + index)
    high = second >= block
    u = jnp.where(high, first - band, band - 1 - first)
    h = jnp.where(high, second - block, -1 - second)
    outside = jnp.where(jnp.where(high, 1, 0) == place % 2, rows.second, rows.first) + (u * (u + 1) >> 1) + h
    return jnp.where(high | (second < 0), outside, inside)


def banded(waveforms, pair_events, pair_valid, presence, block):
    each = waveforms.shape[0]
    forward, inverse, weights = spectral_tables(waveforms.shape[2], LAGS)
    tables = (jnp.asarray(np.concatenate([forward, inverse], axis=1)), jnp.asarray(weights))
    near, far, brought = exchange(waveforms, lax.axis_size("sta"), tables[0])
    ready = prepare_call(pair_events, pair_valid, presence, block)
    far, ready, brought = lax.optimization_barrier((far, ready, brought))
    tables = (brought, tables[1])
    me, place = lax.axis_index("sta"), lax.axis_index("evt")
    count = lax.axis_size("evt")
    inward = (place % 2 == 0) == (me * each < block // 2)

    def swapped(half, odd):
        links = [(i, i + 1) for i in range(odd, count - 1, 2)]
        return lax.ppermute(half, "evt", links + [(j, i) for i, j in links])

    first_halo = swapped(jnp.where(inward, far, near), 0)
    second_halo = swapped(jnp.where(inward, near, far), 1)
    row, count, held = ready
    own, table, peaks = own_call(near, far, held, tables, each, block)
    table, peaks = middle_call(first_halo, own, held, tables, peaks, table, each)
    table, sums = last_call(second_halo, own, held, tables, peaks, row, count, table, each)

    row = row.reshape(-1)
    sta_count = lax.axis_size("sta")

    def from_station(j):
        return lax.ppermute(sums, "sta", [(i, i ^ j) for i in range(sta_count)])

    split = row.shape[0] * 6 // 8
    arrived = from_station(4)
    correlation = pick_call(row, table, (), 0, split)
    sums, correlation = lax.optimization_barrier((sums + arrived, correlation))
    beside, across, aslant = from_station(1), from_station(2), from_station(3)
    correlation = pick_call(row, table, (correlation,), split, row.shape[0] - split)
    return correlation, (sums + beside) + (across + aslant)


def by_slot(waveforms, pair_events, pair_valid, presence, block):
    share = presence.shape[1]
    start = lax.axis_index("evt") * block
    traces = exchange_whole(waveforms)
    place = pair_events - start
    slot = jnp.where((place >= 0) & (place < block), 0, block) + place % block
    gained = jnp.where(pair_valid > 0, slot[:, 0], 2 * block)
    slots = jnp.stack([slot[:, 0], slot[:, 1], gained]).astype(jnp.int32)
    held = jnp.arange(2 * block, dtype=jnp.int32)
    held = jnp.where(held < block, held, jnp.where(held < block + block // 2, held, held - 2 * block))
    held = jnp.clip(start + held, 0, presence.shape[0] - 1)
    slot_presence = jnp.broadcast_to(
        jnp.take(presence.astype(jnp.float32), held, axis=0)[:, :, None], (2 * block, share, LANES)
    )
    few = presence.astype(jnp.bfloat16)
    event = jnp.arange(presence.shape[0], dtype=jnp.int32)
    first, second = (
        jnp.dot((pair_events[:, i:i + 1] == event).astype(jnp.bfloat16), few, preferred_element_type=jnp.float32)
        for i in (0, 1)
    )
    counts = jnp.sum(first * second, axis=1) * pair_valid.astype(jnp.float32)
    tables = tuple(jnp.asarray(x) for x in spectral_tables(waveforms.shape[2], LAGS))
    correlation, peaks = pair_call(slots, traces, slot_presence, tables)
    sums = lax.psum(jnp.stack([peaks.reshape(-1), counts]), "sta")
    return correlation.reshape(-1, share, correlation.shape[1]), sums


def body(waveforms, pair_events, pair_valid, presence):
    sta_count = lax.axis_size("sta")
    local_events, stations, window = waveforms.shape
    block = sta_count * local_events
    args = (waveforms, pair_events, pair_valid, presence, block)
    dense = sta_count == 8 and presence.shape[0] == LANES and block * block <= pair_events.shape[0]
    correlation, sums = (banded if dense else by_slot)(*args)
    pair_peak = sums[0] / jnp.maximum(sums[1], 1.0)
    return correlation, pair_peak.reshape(-1)


def solution(mesh):
    return jax.shard_map(
        body,
        mesh=mesh,
        in_specs=(P(("evt", "sta"), None, None), P("evt", None), P("evt"), P(None, "sta")),
        out_specs=(P("evt", "sta", None), P("evt")),
        check_vma=False,
    )
```

```python
import functools
import math

import jax
import jax.numpy as jnp
import numpy as np
from jax import lax
from jax.experimental import pallas as pl
from jax.experimental.pallas import tpu as pltpu
from jax.sharding import PartitionSpec as P

LAGS = 256
LANES = 128


def spectral_tables(window, lag_count):
    half = window // 2
    sample = np.arange(window, dtype=np.int64)
    bins = np.arange(half, dtype=np.int64)
    angle = (sample[:, None] * bins[None, :] % window) * (2.0 * math.pi / window)
    forward = np.concatenate([np.cos(angle), -np.sin(angle)], axis=1) / math.sqrt(window)
    shifts = np.arange(lag_count, dtype=np.int64) - lag_count // 2
    lag_angle = (bins[:, None] * shifts[None, :] % window) * (2.0 * math.pi / window)
    factor = np.where(bins == 0, 1.0, 2.0)[:, None]
    inverse = np.concatenate([factor * np.cos(lag_angle), -factor * np.sin(lag_angle)], axis=0)
    weights = np.concatenate([factor[:, 0], factor[:, 0]])[None, :]
    return forward.astype(jnp.bfloat16), inverse.astype(jnp.bfloat16), weights.astype(np.float32)


def pair_kernel(
    group, chunk, parts, slots_ref, *refs
):
    traces = refs[:parts]
    (
        presence_ref, forward_ref, inverse_ref, weights_ref,
        out_ref, peak_ref,
        spec_ref, gain_ref, lhs_ref,
    ) = refs[parts:]
    stations, window = spec_ref.shape[1:]
    half = window // 2
    events = spec_ref.shape[0]

    @pl.when(pl.program_id(0) == 0)
    def _():
        start = 0
        for ref in traces:
            rows = ref.shape[0]
            count = rows // stations
            result = jnp.dot(ref[...], forward_ref[...], preferred_element_type=jnp.float32)
            rounded = result.astype(jnp.bfloat16).astype(jnp.float32)
            spec_ref[pl.ds(start, count)] = rounded.reshape(count, stations, window)
            power = jnp.square(rounded) * weights_ref[...]
            energy = jnp.sum(power, axis=1, keepdims=True) + 1e-06
            gain = jnp.broadcast_to(lax.rsqrt(energy), (rows, LANES))
            gain = gain.reshape(count, stations, LANES) * presence_ref[pl.ds(start, count)]
            gain_ref[pl.ds(start, count)] = gain
            start += count
        gain_ref[events] = jnp.zeros((stations, LANES), jnp.float32)

    base = pl.program_id(0) * group
    lane = lax.broadcasted_iota(jnp.int32, (stations, LANES), 1)

    def cross(pair):
        first = spec_ref[slots_ref[0, pair]]
        second = spec_ref[slots_ref[1, pair]]
        ra, ia = first[:, :half], first[:, half:]
        rb, ib = second[:, :half], second[:, half:]
        return jnp.concatenate([ra * rb + ia * ib, ra * ib - ia * rb], axis=1)

    def one_chunk(index, peaks):
        first_pair = base + index * chunk
        for j in range(0, chunk, 2):
            both = jnp.concatenate([cross(first_pair + j), cross(first_pair + j + 1)], axis=0)
            lhs_ref[pl.ds(j * stations, 2 * stations), :] = both.astype(jnp.bfloat16)
        lagged = jnp.dot(lhs_ref[...], inverse_ref[...], preferred_element_type=jnp.float32)
        for j in range(0, chunk, 2):
            rows = []
            for i in (j, j + 1):
                pair = first_pair + i
                gain = gain_ref[slots_ref[2, pair]] * gain_ref[slots_ref[1, pair]]
                scaled = lagged[i * stations:(i + 1) * stations] * jnp.concatenate([gain, gain], axis=1)
                rows.append(scaled)
                top = jnp.max(scaled, axis=1, keepdims=True)
                peaks = jnp.where(lane == index * chunk + i, top, peaks)
            block = jnp.concatenate(rows, axis=0).astype(jnp.bfloat16)
            start = pl.multiple_of(index * chunk * stations, chunk * stations) + j * stations
            out_ref[pl.ds(start, 2 * stations), :] = block
        return peaks

    peaks = lax.fori_loop(0, group // chunk, one_chunk, jnp.zeros((stations, LANES), jnp.float32))
    peak_ref[0] = jnp.sum(peaks, axis=0, keepdims=True)


def pair_call(slots, traces, presence, tables):
    forward, inverse, weights = tables
    window = forward.shape[0]
    lags = inverse.shape[1]
    pairs = slots.shape[1]
    events, stations = presence.shape[:2]
    group = LANES
    chunk = 32
    vmem = pl.BlockSpec(memory_space=pltpu.VMEM)
    return pl.pallas_call(
        functools.partial(pair_kernel, group, chunk, len(traces)),
        grid=(pairs // group,),
        out_shape=(
            jax.ShapeDtypeStruct((pairs * stations, lags), jnp.bfloat16),
            jax.ShapeDtypeStruct((pairs // group, 1, group), jnp.float32),
        ),
        in_specs=[pl.BlockSpec(memory_space=pltpu.SMEM)] + [vmem] * (len(traces) + 4),
        out_specs=(
            pl.BlockSpec((group * stations, lags), lambda i: (i, 0)),
            pl.BlockSpec((1, 1, group), lambda i: (i, 0, 0)),
        ),
        scratch_shapes=[
            pltpu.VMEM((events, stations, window), jnp.float32),
            pltpu.VMEM((events + 1, stations, LANES), jnp.float32),
            pltpu.VMEM((chunk * stations, window), jnp.bfloat16),
        ],
        compiler_params=pltpu.CompilerParams(vmem_limit_bytes=56 * 1024 * 1024),
        cost_estimate=pl.CostEstimate(flops=4_500_000_000, bytes_accessed=8_000_000, transcendentals=0),
    )(slots, *traces, presence, forward, inverse, weights)


def exchange(waveforms, sta_count, tables):
    events, stations, window = waveforms.shape
    share = stations // sta_count
    blocks = waveforms.reshape(events, sta_count, share, window)
    me = lax.axis_index("sta")
    half = sta_count // 2

    def for_station(i):
        return lax.dynamic_index_in_dim(blocks, i, axis=1, keepdims=False)

    def swap(piece, j):
        return lax.ppermute(piece, "sta", [(i, i ^ j) for i in range(sta_count)])

    later = [swap(for_station(me ^ j), j) for j in range(half, sta_count)]
    across = swap(jnp.stack([for_station(me ^ 2), for_station(me ^ 3)]), 2)
    beside = swap(jnp.concatenate([for_station(me ^ 1), across[1]], axis=0), 1)
    later[0], tables = lax.optimization_barrier((later[0], tables))
    tables = bring_call(tables)
    pieces = [for_station(me), beside[:events], across[0], beside[events:]] + later
    rows = half * events * share
    near = jnp.concatenate(pieces[:half][::-1], axis=0).reshape(rows, window)
    far = jnp.concatenate(pieces[half:][::-1], axis=0).reshape(rows, window)
    return near, far, tables


def exchange_whole(waveforms):
    window = waveforms.shape[2]
    arrived = lax.all_to_all(waveforms, "sta", split_axis=1, concat_axis=0, tiled=True)
    arrived = arrived.reshape(-1, window)
    half = arrived.shape[0] // 2
    count = lax.axis_size("evt")
    down = [(i, i - 1) for i in range(1, count)]
    up = [(i, i + 1) for i in range(count - 1)]
    next_low = lax.ppermute(arrived[:half], "evt", down)
    last_high = lax.ppermute(arrived[half:], "evt", up)
    return arrived, next_low, last_high


def triangle(count):
    return count * (count + 1) // 2


def own_list(block):
    band = block // 2
    return [(x, y) for x in range(block) for y in range(x + 1, min(x + band, block - 1) + 1)]


class Rows:
    def __init__(self, block):
        self.own = len(own_list(block))
        self.zero = 2 * self.own
        self.first = self.zero + 8
        self.second = self.first + triangle(block // 2)
        self.end = self.second + triangle(block // 2)
        self.lanes = -(-self.end // LANES) * LANES


def cross_spectra(first, second):
    half = first.shape[1] // 2
    ra, ia = first[:, :half], first[:, half:]
    rb, ib = second[:, :half], second[:, half:]
    return jnp.concatenate([ra * rb + ia * ib, ra * ib - ia * rb], axis=1)


def scaled_spectra(traces_ref, me, each, place, presence_ref, present, tables_ref, weights_ref, spec_ref):
    stations, window = spec_ref.shape[1:]
    events = traces_ref.shape[0] // stations
    pieces = events // each
    result = jnp.dot(traces_ref[...], tables_ref[:, :window], preferred_element_type=jnp.float32)
    rounded = result.astype(jnp.bfloat16).astype(jnp.float32)
    energy = jnp.sum(jnp.square(rounded) * weights_ref[...], axis=1, keepdims=True) + 1e-06
    gain = jnp.broadcast_to(lax.rsqrt(energy), (events * stations, LANES)).reshape(events, stations, LANES)
    rounded = rounded.reshape(events, stations, window)
    for j in range(pieces):
        shift = ((me ^ (pieces - 1 - j)) & (pieces - 1)) * each
        piece = slice(j * each, (j + 1) * each)
        scale = gain[piece] * presence_ref[pl.ds(present + shift, each)]
        scale = jnp.concatenate([scale] * (window // LANES), axis=2)
        spec_ref[pl.ds(place + shift, each)] = rounded[piece] * scale


def build(lhs_ref, low, pairs, first_of, second_of):
    for i in range(0, len(pairs), 2):
        both = [cross_spectra(first_of(x), second_of(y)) for x, y in pairs[i:i + 2]]
        rows = 2 * both[0].shape[0]
        lhs_ref[pl.ds((low + i) * rows // 2, rows), :] = jnp.concatenate(both, axis=0).astype(jnp.bfloat16)


def keep(table_ref, peaks, values, row):
    stations, lags = table_ref.shape[1:]
    lane = lax.broadcasted_iota(jnp.int32, (stations, LANES), 1)
    count = values.shape[0] // stations
    for i in range(count):
        top = jnp.max(values[i * stations:(i + 1) * stations], axis=1, keepdims=True)
        at, within = divmod(row + i, LANES)
        peaks[at] = jnp.where(lane == within, top, peaks[at])
    table_ref[pl.ds(row, count)] = values.reshape(count, stations, lags).astype(jnp.bfloat16)


def no_peaks(rows, stations):
    return [jnp.zeros((stations, LANES), jnp.float32) for _ in range(rows.lanes // LANES)]


def prepare_kernel(
    block, packed_ref, row_ref, count_ref, held_ref,
):
    place = lax.axis_index("evt")
    start = place * block
    lines = row_ref.shape[0]

    def stacked(line):
        return jnp.concatenate(
            [packed_ref[line:line + 1, i * LANES:(i + 1) * LANES] for i in range(lines)], axis=0
        )

    first, second, valid = stacked(0), stacked(1), stacked(2)
    rows = Rows(block)
    row = table_row(first - start, second - start, place, block, rows)
    row = jnp.where(valid > 0, row, rows.zero)
    row_ref[...] = jnp.clip(row, 0, rows.end - 1)

    presence = packed_ref[3:, :LANES]
    stations, events = presence.shape
    bits = jnp.zeros((1, events), jnp.int32)
    for s in range(stations):
        bits = bits + presence[s:s + 1] * (1 << s)
    bits = jnp.broadcast_to(bits, (lines, events))
    both = jnp.take_along_axis(bits, first, axis=1) & jnp.take_along_axis(bits, second, axis=1)
    count = jnp.zeros_like(both)
    for s in range(stations):
        count = count + (lax.shift_right_logical(both, s) & 1)
    count_ref[...] = (count * valid).astype(jnp.float32)

    lane = lax.broadcasted_iota(jnp.int32, presence.shape, 1)
    present = presence.astype(jnp.float32)
    for i in range(held_ref.shape[0]):
        mine = jnp.where(lane == start - block // 2 + i, present, 0.0)
        held_ref[i] = jnp.broadcast_to(jnp.sum(mine, axis=1, keepdims=True), (stations, LANES))


def bring_kernel(tables_ref, tables_out, sem):
    copy = pltpu.make_async_copy(tables_ref, tables_out, sem)
    copy.start()
    copy.wait()


def own_pairs(spec_ref, tables_ref, table_ref, peaks, lhs_ref):
    block, stations, window = spec_ref.shape
    half = window // 2
    pairs = own_list(block)
    chunk = 64
    for low in range(0, len(pairs), chunk):
        some = pairs[low:low + chunk]
        held = {x: spec_ref[x] for x, _ in some}
        build(lhs_ref, low, some, lambda x: held[x], lambda y: spec_ref[y])
        rows = pl.ds(low * stations, len(some) * stations)
        even = jnp.dot(lhs_ref[rows, :half], tables_ref[:half, window:], preferred_element_type=jnp.float32)
        odd = jnp.dot(lhs_ref[rows, half:], tables_ref[half:, window:], preferred_element_type=jnp.float32)
        keep(table_ref, peaks, even + odd, low)
        keep(table_ref, peaks, even - odd, len(pairs) + low)


def halo_pairs(high, own_ref, spec_ref, tables_ref, table_ref, peaks, lhs_ref, row):
    band, stations, window = spec_ref.shape

    def own(u):
        return own_ref[jnp.where(high, band + u, band - 1 - u)]

    def other(h):
        return spec_ref[jnp.where(high, h, band - 1 - h)]

    pairs = [(u, h) for u in range(band) for h in range(u + 1)]
    chunk = 68
    for low in range(0, len(pairs), chunk):
        some = pairs[low:low + chunk]
        held = {u: own(u) for u, _ in some}
        build(lhs_ref, low, some, lambda u: held[u], other)
        rows = pl.ds(low * stations, len(some) * stations)
        lagged = jnp.dot(lhs_ref[rows, :], tables_ref[:, window:], preferred_element_type=jnp.float32)
        keep(table_ref, peaks, lagged, row + low)


def own_kernel(
    each, near_ref, far_ref, presence_ref, tables_ref, weights_ref,
    spec_ref, table_ref, peak_ref, lhs_ref,
):
    block, stations, window = spec_ref.shape
    band = block // 2
    me = lax.axis_index("sta")
    mine = jnp.where(me * each < band, 0, band)
    for ref, place in ((near_ref, mine), (far_ref, band - mine)):
        scaled_spectra(
            ref, me, each, place, presence_ref, band + place, tables_ref, weights_ref, spec_ref
        )
    rows = Rows(block)
    peaks = no_peaks(rows, stations)
    own_pairs(spec_ref, tables_ref, table_ref, peaks, lhs_ref)
    table_ref[rows.zero] = jnp.zeros(table_ref.shape[1:], table_ref.dtype)
    peak_ref[...] = jnp.concatenate(peaks, axis=1)


def middle_kernel(
    each, halo_ref, own_ref, presence_ref, tables_ref, weights_ref, own_peak_ref,
    held_table_ref, table_ref, peak_ref, other_ref, lhs_ref,
):
    del held_table_ref
    block, stations, window = own_ref.shape
    band = block // 2
    me = lax.axis_index("sta")
    high = lax.axis_index("evt") % 2 == 0
    edge = jnp.where(high, 3 * band, 0)
    scaled_spectra(halo_ref, me, each, 0, presence_ref, edge, tables_ref, weights_ref, other_ref)
    rows = Rows(block)
    peaks = no_peaks(rows, stations)
    halo_pairs(high, own_ref, other_ref, tables_ref, table_ref, peaks, lhs_ref, rows.first)
    peak_ref[...] = own_peak_ref[...] + jnp.concatenate(peaks, axis=1)


def last_kernel(
    each, halo_ref, own_ref, presence_ref, tables_ref, weights_ref, peak_ref, row_ref, count_ref,
    held_table_ref, table_ref, sums_ref, other_ref, lhs_ref,
):
    del held_table_ref
    block, stations, window = own_ref.shape
    band = block // 2
    me = lax.axis_index("sta")
    high = lax.axis_index("evt") % 2 == 1
    edge = jnp.where(high, 3 * band, 0)
    scaled_spectra(halo_ref, me, each, 0, presence_ref, edge, tables_ref, weights_ref, other_ref)
    rows = Rows(block)
    peaks = no_peaks(rows, stations)
    halo_pairs(high, own_ref, other_ref, tables_ref, table_ref, peaks, lhs_ref, rows.second)
    row = row_ref[...]
    lanes = row & (LANES - 1)
    total = jnp.zeros(row.shape, jnp.float32)
    for at, late in enumerate(peaks):
        line = jnp.sum(peak_ref[:, at * LANES:(at + 1) * LANES] + late, axis=0, keepdims=True)
        picked = jnp.take_along_axis(jnp.broadcast_to(line, row.shape), lanes, axis=1)
        total = jnp.where(lax.shift_right_logical(row, 7) == at, picked, total)
    sums_ref[0] = total
    sums_ref[1] = count_ref[...]


def pick_kernel(start, group, row_ref, table_ref, *refs):
    out_ref, picked_ref, sems = refs[-3:]
    copies = []
    for low in range(0, picked_ref.shape[0], group):
        for i in range(low, low + group):
            picked_ref[i] = table_ref[row_ref[start + i]]
        copies.append(pltpu.make_async_copy(
            picked_ref.at[pl.ds(low, group)], out_ref.at[pl.ds(start + low, group)], sems.at[low // group]
        ))
        copies[-1].start()
    for copy in copies:
        copy.wait()


VMEM = pl.BlockSpec(memory_space=pltpu.VMEM)
SMEM = pl.BlockSpec(memory_space=pltpu.SMEM)
PARAMS = pltpu.CompilerParams(vmem_limit_bytes=20 * 1024 * 1024)


def cost(rows, lags, window, traces, moved):
    return pl.CostEstimate(
        flops=2 * window * (rows * lags + traces * window), bytes_accessed=moved, transcendentals=0
    )


def prepare_call(pair_events, pair_valid, presence, block):
    pairs = pair_events.shape[0]
    events, stations = presence.shape
    packed = jnp.concatenate(
        [pair_events.T, pair_valid[None], jnp.pad(presence.T, ((0, 0), (0, pairs - events)))], axis=0
    )
    line = (pairs // LANES, LANES)
    return pl.pallas_call(
        functools.partial(prepare_kernel, block),
        out_shape=(
            jax.ShapeDtypeStruct(line, jnp.int32),
            jax.ShapeDtypeStruct(line, jnp.float32),
            jax.ShapeDtypeStruct((2 * block, stations, LANES), jnp.float32),
        ),
        in_specs=[VMEM],
        out_specs=(VMEM,) * 3,
        compiler_params=PARAMS,
        cost_estimate=pl.CostEstimate(flops=1_000_000, bytes_accessed=1_000_000, transcendentals=0),
    )(packed)


def bring_call(tables):
    return pl.pallas_call(
        bring_kernel,
        out_shape=jax.ShapeDtypeStruct(tables.shape, tables.dtype),
        in_specs=[pl.BlockSpec(memory_space=pl.ANY)],
        out_specs=VMEM,
        scratch_shapes=[pltpu.SemaphoreType.DMA],
        compiler_params=PARAMS,
        cost_estimate=pl.CostEstimate(flops=0, bytes_accessed=5_000_000, transcendentals=0),
    )(tables)


def own_call(near, far, presence, tables, each, block):
    table_of, weights = tables
    window = table_of.shape[0]
    lags = table_of.shape[1] - window
    stations = presence.shape[1]
    rows = Rows(block)
    return pl.pallas_call(
        functools.partial(own_kernel, each),
        out_shape=(
            jax.ShapeDtypeStruct((block, stations, window), jnp.float32),
            jax.ShapeDtypeStruct((rows.end, stations, lags), jnp.bfloat16),
            jax.ShapeDtypeStruct((stations, rows.lanes), jnp.float32),
        ),
        in_specs=[VMEM] * 5,
        out_specs=(VMEM,) * 3,
        scratch_shapes=[pltpu.VMEM((rows.own * stations, window), jnp.bfloat16)],
        compiler_params=PARAMS,
        cost_estimate=cost(rows.own * stations, lags, window, near.shape[0] * 2, 8_000_000),
    )(near, far, presence, table_of, weights)


def middle_call(halo, own, presence, tables, peaks, table, each):
    table_of, weights = tables
    window = table_of.shape[0]
    lags = table_of.shape[1] - window
    block, stations = own.shape[:2]
    pairs = triangle(block // 2)
    return pl.pallas_call(
        functools.partial(middle_kernel, each),
        out_shape=(
            jax.ShapeDtypeStruct(table.shape, table.dtype),
            jax.ShapeDtypeStruct(peaks.shape, peaks.dtype),
        ),
        in_specs=[VMEM] * 7,
        out_specs=(VMEM,) * 2,
        scratch_shapes=[
            pltpu.VMEM((block // 2, stations, window), jnp.float32),
            pltpu.VMEM((pairs * stations, window), jnp.bfloat16),
        ],
        input_output_aliases={6: 0},
        compiler_params=PARAMS,
        cost_estimate=cost(pairs * stations, lags, window, halo.shape[0], 4_000_000),
    )(halo, own, presence, table_of, weights, peaks, table)


def last_call(halo, own, presence, tables, peaks, row, count, table, each):
    table_of, weights = tables
    window = table_of.shape[0]
    lags = table_of.shape[1] - window
    block, stations = own.shape[:2]
    pairs = triangle(block // 2)
    return pl.pallas_call(
        functools.partial(last_kernel, each),
        out_shape=(
            jax.ShapeDtypeStruct(table.shape, table.dtype),
            jax.ShapeDtypeStruct((2,) + row.shape, jnp.float32),
        ),
        in_specs=[VMEM] * 9,
        out_specs=(VMEM,) * 2,
        scratch_shapes=[
            pltpu.VMEM((block // 2, stations, window), jnp.float32),
            pltpu.VMEM((pairs * stations, window), jnp.bfloat16),
        ],
        input_output_aliases={8: 0},
        compiler_params=PARAMS,
        cost_estimate=cost(pairs * stations, lags, window, halo.shape[0], 4_000_000),
    )(halo, own, presence, table_of, weights, peaks, row, count, table)


def pick_call(row, table, held, start, count):
    group = 64
    anywhere = pl.BlockSpec(memory_space=pl.ANY)
    return pl.pallas_call(
        functools.partial(pick_kernel, start, group),
        out_shape=jax.ShapeDtypeStruct(row.shape + table.shape[1:], table.dtype),
        in_specs=[SMEM, VMEM] + [anywhere] * len(held),
        out_specs=anywhere,
        scratch_shapes=[
            pltpu.VMEM((count,) + table.shape[1:], table.dtype),
            pltpu.SemaphoreType.DMA((count // group,)),
        ],
        input_output_aliases={2: 0} if held else {},
        compiler_params=PARAMS,
        cost_estimate=pl.CostEstimate(flops=0, bytes_accessed=count * 20_000, transcendentals=0),
    )(row, table, *held)


def table_row(first, second, place, block, rows):
    band = block // 2
    low, apart = jnp.minimum(first, second), jnp.abs(first - second)
    past = jnp.maximum(low - band, 0)
    index = jnp.minimum(low, band) * band + past * (band - 1) - (past * (past - 1) >> 1) + apart - 1
    inside = jnp.where(second > first, index, rows.own + index)
    high = second >= block
    u = jnp.where(high, first - band, band - 1 - first)
    h = jnp.where(high, second - block, -1 - second)
    outside = jnp.where(jnp.where(high, 1, 0) == place % 2, rows.second, rows.first) + (u * (u + 1) >> 1) + h
    return jnp.where(high | (second < 0), outside, inside)


def banded(waveforms, pair_events, pair_valid, presence, block):
    each = waveforms.shape[0]
    forward, inverse, weights = spectral_tables(waveforms.shape[2], LAGS)
    tables = (jnp.asarray(np.concatenate([forward, inverse], axis=1)), jnp.asarray(weights))
    near, far, brought = exchange(waveforms, lax.axis_size("sta"), tables[0])
    ready = prepare_call(pair_events, pair_valid, presence, block)
    far, ready, brought = lax.optimization_barrier((far, ready, brought))
    tables = (brought, tables[1])
    me, place = lax.axis_index("sta"), lax.axis_index("evt")
    count = lax.axis_size("evt")
    inward = (place % 2 == 0) == (me * each < block // 2)

    def swapped(half, odd):
        links = [(i, i + 1) for i in range(odd, count - 1, 2)]
        return lax.ppermute(half, "evt", links + [(j, i) for i, j in links])

    first_halo = swapped(jnp.where(inward, far, near), 0)
    second_halo = swapped(jnp.where(inward, near, far), 1)
    row, count, held = ready
    own, table, peaks = own_call(near, far, held, tables, each, block)
    table, peaks = middle_call(first_halo, own, held, tables, peaks, table, each)
    table, sums = last_call(second_halo, own, held, tables, peaks, row, count, table, each)

    row = row.reshape(-1)
    sta_count = lax.axis_size("sta")

    def from_station(j):
        return lax.ppermute(sums, "sta", [(i, i ^ j) for i in range(sta_count)])

    split = row.shape[0] * 6 // 8
    arrived = from_station(4)
    correlation = pick_call(row, table, (), 0, split)
    sums, correlation = lax.optimization_barrier((sums + arrived, correlation))
    beside, across, aslant = from_station(1), from_station(2), from_station(3)
    correlation = pick_call(row, table, (correlation,), split, row.shape[0] - split)
    return correlation, (sums + beside) + (across + aslant)


def by_slot(waveforms, pair_events, pair_valid, presence, block):
    share = presence.shape[1]
    start = lax.axis_index("evt") * block
    traces = exchange_whole(waveforms)
    place = pair_events - start
    slot = jnp.where((place >= 0) & (place < block), 0, block) + place % block
    gained = jnp.where(pair_valid > 0, slot[:, 0], 2 * block)
    slots = jnp.stack([slot[:, 0], slot[:, 1], gained]).astype(jnp.int32)
    held = jnp.arange(2 * block, dtype=jnp.int32)
    held = jnp.where(held < block, held, jnp.where(held < block + block // 2, held, held - 2 * block))
    held = jnp.clip(start + held, 0, presence.shape[0] - 1)
    slot_presence = jnp.broadcast_to(
        jnp.take(presence.astype(jnp.float32), held, axis=0)[:, :, None], (2 * block, share, LANES)
    )
    few = presence.astype(jnp.bfloat16)
    event = jnp.arange(presence.shape[0], dtype=jnp.int32)
    first, second = (
        jnp.dot((pair_events[:, i:i + 1] == event).astype(jnp.bfloat16), few, preferred_element_type=jnp.float32)
        for i in (0, 1)
    )
    counts = jnp.sum(first * second, axis=1) * pair_valid.astype(jnp.float32)
    tables = tuple(jnp.asarray(x) for x in spectral_tables(waveforms.shape[2], LAGS))
    correlation, peaks = pair_call(slots, traces, slot_presence, tables)
    sums = lax.psum(jnp.stack([peaks.reshape(-1), counts]), "sta")
    return correlation.reshape(-1, share, correlation.shape[1]), sums


def body(waveforms, pair_events, pair_valid, presence):
    sta_count = lax.axis_size("sta")
    local_events, stations, window = waveforms.shape
    block = sta_count * local_events
    args = (waveforms, pair_events, pair_valid, presence, block)
    dense = sta_count == 8 and presence.shape[0] == LANES and block * block <= pair_events.shape[0]
    correlation, sums = (banded if dense else by_slot)(*args)
    pair_peak = sums[0] / jnp.maximum(sums[1], 1.0)
    return correlation, pair_peak.reshape(-1)


def solution(mesh):
    return jax.shard_map(
        body,
        mesh=mesh,
        in_specs=(P(("evt", "sta"), None, None), P("evt", None), P("evt"), P(None, "sta")),
        out_specs=(P("evt", "sta", None), P("evt")),
        check_vma=False,
    )
```
